32 devices in a mesh: grp: 8 (over y, x, core), chan: 4 (over z).
Axes of the slice: x: 2, y: 2, z: 4, core: 2. Of those that a mesh axis runs over, the one named last changes fastest.
Arguments:
- spectra: bfloat16 [512, 2, 2, 8192], P(('grp', 'chan')), may hold values from -45 to 45
- pair_blocks: int32 [8, 4, 18, 2], P('grp', 'chan'), may hold values from 0 to 31
- owners: int32 [8, 4, 18, 1], P('grp', 'chan'), may hold values from 0 to 7; in each aligned block of 18 rows (0 to 17, 18 to 35, ..., all dimensions but the last counted through in order) at most 3 rows name the same one
Outputs:
- stacks: float32 [8, 4, 24, 4, 1024], P('grp', 'chan')
The draws below stay inside these ranges and needn't reach their ends.
Inputs may be any that keep to these rules, and one draw needn't show every extreme that they name: `owners`: at most 3 of one device's 18 pair blocks name the same owner.
All inputs are finite; a program needn't handle non-finite values.
Results may differ from the reference program's by a relative error of at most 0.011.
Values may be sent and summed in bfloat16 or wider, within the bound.
No kernel may reach another device: no remote copies, remote signals or barrier semaphores. Data moves between devices by JAX's collectives and lax.ppermute only.
A program may use at most 128 MiB of HBM per device.

```python
import math
import jax
import jax.numpy as jnp
import numpy as np
from jax import lax

F = 8192
LAGS = 1024
BLK = 2
NB_SRC = 18
MOST = 3
WINDOWS = 2
CHANNELS = 512
GCH = 64
GBLK = 32
N_GRP = 8
N_CHAN = 4


def draw_spectra(key, part):
    keys = jax.random.split(key, 3)
    shape = (CHANNELS, WINDOWS, 2, F)
    base = jnp.clip(jax.random.normal(keys[0], shape, jnp.float32), -4.0, 4.0)
    rows = 10.0 ** jax.random.uniform(keys[1], (CHANNELS, WINDOWS, 1, 1), jnp.float32, -0.5, 0.5)
    spread = jnp.exp(jax.random.uniform(keys[2], (CHANNELS, WINDOWS, 1, F), jnp.float32, -1.0, 1.0))
    return (base * rows * spread).astype(jnp.bfloat16)


def set_ends(array, rng, least, largest):
    index_at = [jax.random.randint(jax.random.fold_in(rng, axis), (), 0, length) for axis, length in enumerate(array.shape)]
    widest = array.shape.index(max(array.shape))
    next_to = index_at[:widest] + [(index_at[widest] + 1) % array.shape[widest]] + index_at[widest + 1:]
    return array.at[tuple(index_at)].set(least).at[tuple(next_to)].set(largest)


def routed_block(key, own, number, rows, number_of, top, bound, slope):
    ranking = jax.random.permutation(key, number_of)
    crowded, usual = load_shares(number_of, rows * top, bound, slope, True), load_shares(number_of, rows * top, bound, slope, False)
    places = jnp.arange(number_of)

    def named(tallies, turn):
        used = int((tallies > 0).sum())
        fixed = max(1, used // 4)
        moved = fixed + (places - fixed + turn * (used - fixed)) % max(1, number_of - fixed)
        return jnp.zeros((number_of,), jnp.int32).at[ranking[jnp.where(places < fixed, places, moved)]].set(jnp.asarray(tallies, jnp.int32))

    tallies = jnp.where(number % 4 == 0, named(crowded, number // 4), named(usual, number - number // 4 - 1))
    mixed = jax.random.permutation(jax.random.fold_in(own, 3), number_of)
    giver, receiver = mixed[0:number_of // 2 * 2:2], mixed[1:number_of // 2 * 2:2]
    room = jnp.minimum(tallies[giver] - 1, bound - tallies[receiver]) // 2
    room = jnp.where((giver == ranking[0]) | (receiver == ranking[0]) | (tallies[receiver] == 0), 0, jnp.maximum(room, 0))
    moved = jax.random.randint(jax.random.fold_in(own, 4), (number_of // 2,), 0, 1 << 20) % (room + 1)
    tallies = tallies.at[giver].add(-moved).at[receiver].add(moved)
    labels = jnp.searchsorted(jnp.cumsum(tallies), jnp.arange(rows * top), side="right").astype(jnp.int32)
    table = labels.reshape(top, rows).T
    table = table[jax.random.permutation(jax.random.fold_in(own, 1), rows)]
    turn = jax.random.randint(jax.random.fold_in(own, 2), (rows, 1), 0, top)
    return jnp.take_along_axis(table, (jnp.arange(top)[None, :] + turn) % top, axis=1)


def load_shares(number_of, total, reach, lean, full):
    portions = [(1 << 20) // math.isqrt(standing ** lean) + 1 for standing in range(1, number_of + 1)]
    largest = reach if full else min(reach, max(-(-total // number_of), total * portions[0] // sum(portions)))
    least = 1 if total - largest >= number_of - 1 else 0
    holding, rest = [largest] + [least] * (number_of - 1), total - largest - least * (number_of - 1)
    while rest > 0:
        free = [i for i in range(1, number_of) if holding[i] < largest] or [i for i in range(1, number_of) if holding[i] < reach]
        pool, budget = sum([portions[i] for i in free]), rest
        for i in free:
            addition = min(reach - holding[i], max(1, budget * portions[i] // pool), rest)
            holding[i] = holding[i] + addition
            rest = rest - addition
    return np.array(holding)


def setup_inputs(seed: int = 0) -> dict:
    arg_keys = jax.random.split(jax.random.key(seed), 4)
    spectra = draw_spectra(jax.random.fold_in(arg_keys[3], 71), 0)
    pair_blocks = set_ends(jax.random.randint(arg_keys[1], (N_GRP, N_CHAN, NB_SRC, 2), 0, GBLK), jax.random.fold_in(arg_keys[1], 1), 0, GBLK - 1).astype(jnp.int32)
    owners_keys = jax.random.split(jax.random.fold_in(arg_keys[2], 1), N_GRP * N_CHAN * NB_SRC // NB_SRC)
    owners_turns = jax.random.permutation(jax.random.fold_in(arg_keys[2], 3), N_GRP * N_CHAN * NB_SRC // NB_SRC)
    owners = jax.vmap(lambda own, number: routed_block(jax.random.fold_in(arg_keys[2], 2), own, number, NB_SRC, N_GRP, 1, MOST, 2))(owners_keys, owners_turns).reshape((N_GRP, N_CHAN, NB_SRC, 1))
    return dict(spectra=spectra, pair_blocks=pair_blocks, owners=owners)


def lag_table(start, count):
    bins = start + jnp.arange(count, dtype=jnp.int32)
    lag_index = jnp.arange(LAGS, dtype=jnp.int32) - LAGS // 2
    phase = bins[:, None] * lag_index[None, :] % (2 * F)
    angle = phase.astype(jnp.float32) * (jnp.pi / F)
    weight = jnp.where(bins == 0, 1.0, 2.0).astype(jnp.float32) / jnp.sqrt(jnp.float32(F))
    cos_part = (jnp.cos(angle) * weight[:, None]).astype(jnp.bfloat16)
    sin_part = (-jnp.sin(angle) * weight[:, None]).astype(jnp.bfloat16)
    return (cos_part, sin_part)

def whiten(spectra):
    values = spectra.astype(jnp.float32)
    power = values[:, :, 0] ** 2 + values[:, :, 1] ** 2
    level = lax.optimization_barrier(jnp.mean(power, axis=-1, keepdims=True)) + 1e-05
    scale = lax.rsqrt(power + 0.1 * level)
    return (values * scale[:, :, None, :]).astype(jnp.bfloat16)

def cross_pairs(left, right):
    real_left = left[..., :, None, :, 0, :]
    imag_left = left[..., :, None, :, 1, :]
    real_right = right[..., None, :, :, 0, :]
    imag_right = right[..., None, :, :, 1, :]
    real_part = real_left * real_right + imag_left * imag_right
    imag_part = imag_left * real_right - real_left * imag_right
    both = jnp.stack([real_part, imag_part], axis=-2)
    return both.astype(jnp.bfloat16)

def order_ranks(owner_list):
    same = owner_list[..., :, None] == owner_list[..., None, :]
    count = owner_list.shape[-1]
    earlier = jnp.arange(count)[None, :] < jnp.arange(count)[:, None]
    return lax.optimization_barrier(jnp.sum(jnp.logical_and(same, earlier), axis=-1)).astype(jnp.int32)

def reference(spectra, pair_blocks, owners):
    white = whiten(spectra)
    cos_table, sin_table = lag_table(jnp.int32(0), F)
    groups = jnp.arange(N_GRP, dtype=jnp.int32)

    def one_group(group):
        panel = lax.dynamic_slice_in_dim(white, group * GCH, GCH, 0)
        blocks = pair_blocks[group]
        offsets = jnp.arange(BLK, dtype=jnp.int32)
        left_idx = (blocks[:, :, 0][:, :, None] * BLK + offsets).astype(jnp.int32)
        right_idx = (blocks[:, :, 1][:, :, None] * BLK + offsets).astype(jnp.int32)
        left = panel[left_idx].astype(jnp.float32)
        right = panel[right_idx].astype(jnp.float32)
        cross = cross_pairs(left, right)
        stacked = (lax.optimization_barrier(jnp.sum(cross.astype(jnp.float32), axis=-3)) / WINDOWS).astype(jnp.bfloat16)
        rows = stacked.reshape(-1, 2, F)
        corr = jnp.dot(rows[:, 0], cos_table, preferred_element_type=jnp.float32)
        corr = corr + jnp.dot(rows[:, 1], sin_table, preferred_element_type=jnp.float32)
        return corr.reshape(N_CHAN, NB_SRC, BLK * BLK, LAGS)
    values = lax.map(one_group, groups)
    owner_list = owners[..., 0].astype(jnp.int32)
    ranks = order_ranks(owner_list)
    slot_ids = (groups[:, None, None] * MOST + ranks).astype(jnp.int32)
    chan_ids = jnp.broadcast_to(jnp.arange(N_CHAN, dtype=jnp.int32)[None, :, None], owner_list.shape)
    stacks = jnp.zeros((N_GRP, N_CHAN, N_GRP * MOST, BLK * BLK, LAGS), jnp.float32)
    return stacks.at[owner_list, chan_ids, slot_ids].set(values)
```

```python
import functools

import jax
import jax.numpy as jnp
from jax import lax
from jax.experimental import pallas as pl
from jax.experimental.pallas import tpu as pltpu
from jax.sharding import PartitionSpec as P

F = 8192
LAGS = 1024
BLK = 2
NB_SRC = 18
MOST = 3
WINDOWS = 2
LANES = 128
PAIRS = BLK * BLK
VMEM_LIMIT = 48 * 1024 * 1024


def whiten_kernel(parts, spec_ref, out_ref):
    rows = spec_ref.shape[0]
    part_rows = F // LANES // parts

    def one(i, _):
        re = spec_ref[i, 0].astype(jnp.float32)
        im = spec_ref[i, 1].astype(jnp.float32)
        power = re * re + im * im
        level = jnp.sum(power, keepdims=True) * (1.0 / F) + 1e-05
        scale = lax.rsqrt(power + 0.1 * level)
        re = re * scale
        im = im * scale
        for z in range(parts):
            span = slice(z * part_rows, (z + 1) * part_rows)
            both = jnp.concatenate([re[span], im[span]], axis=0)
            out_ref[z, i] = both.astype(jnp.bfloat16)
        return 0

    lax.fori_loop(0, rows, one, 0, unroll=2)


def whiten(spectra, parts):
    rows = spectra.shape[0] * WINDOWS
    step = 8
    grid = spectra.reshape(rows, 2, F // LANES, LANES)
    depth = 2 * F // LANES // parts
    return pl.pallas_call(
        functools.partial(whiten_kernel, parts),
        grid=(rows // step,),
        in_specs=[pl.BlockSpec((step, 2, F // LANES, LANES), lambda i: (i, 0, 0, 0))],
        out_specs=pl.BlockSpec((parts, step, depth, LANES), lambda i: (0, i, 0, 0)),
        out_shape=jax.ShapeDtypeStruct((parts, rows, depth, LANES), jnp.bfloat16),
        name="whiten",
    )(grid)


def table_kernel(first_ref, hi_cos_ref, hi_sin_ref, lo_cos_ref, lo_sin_ref, out_ref):
    s = pl.program_id(0)
    hi_cos = hi_cos_ref[pl.ds(s, 1), :]
    hi_sin = hi_sin_ref[pl.ds(s, 1), :]
    lo_cos = lo_cos_ref[...]
    lo_sin = lo_sin_ref[...]
    zero_bin = jnp.logical_and(first_ref[0] == 0, s == 0)
    row = lax.broadcasted_iota(jnp.int32, lo_cos.shape, 0)
    weight = jnp.where(jnp.logical_and(row == 0, zero_bin), 0.5, 1.0)
    out_ref[0:LANES] = ((hi_cos * lo_cos - hi_sin * lo_sin) * weight).astype(jnp.bfloat16)
    out_ref[LANES:] = -((hi_sin * lo_cos + hi_cos * lo_sin) * weight).astype(jnp.bfloat16)


def tables(place, chunks):
    lag = jnp.arange(LAGS, dtype=jnp.int32) - LAGS // 2

    def angles(bins):
        phase = bins[:, None] * lag[None, :] % (2 * F)
        return phase.astype(jnp.float32) * (jnp.pi / F)

    high = angles((place * chunks + jnp.arange(chunks, dtype=jnp.int32)) * LANES)
    low = angles(jnp.arange(LANES, dtype=jnp.int32))
    unit = 2.0 / jnp.sqrt(jnp.float32(F))
    whole = lambda shape: pl.BlockSpec(shape, lambda s, first: (0, 0))
    return pl.pallas_call(
        table_kernel,
        grid_spec=pltpu.PrefetchScalarGridSpec(
            num_scalar_prefetch=1,
            grid=(chunks,),
            in_specs=[
                whole((chunks, LAGS)),
                whole((chunks, LAGS)),
                whole((LANES, LAGS)),
                whole((LANES, LAGS)),
            ],
            out_specs=pl.BlockSpec((2 * LANES, LAGS), lambda s, first: (s, 0)),
        ),
        out_shape=jax.ShapeDtypeStruct((chunks * 2 * LANES, LAGS), jnp.bfloat16),
        cost_estimate=pl.CostEstimate(
            flops=chunks * LANES * LAGS * 8, bytes_accessed=chunks * LANES * LAGS * 4, transcendentals=0
        ),
        name="tables",
    )(place[None], jnp.cos(high) * unit, jnp.sin(high) * unit, jnp.cos(low), jnp.sin(low))


def corr_kernel(chunks, per_step, pick_ref, panel_ref, table_ref, out_ref, cross, total):
    step = pl.program_id(0)
    rows = total.shape[0]

    @pl.when(step == 0)
    def build():
        def one(t, _):
            left = pick_ref[0, t] * (BLK * WINDOWS)
            right = pick_ref[1, t] * (BLK * WINDOWS)
            weight = pick_ref[2, t].astype(jnp.float32) * (1.0 / WINDOWS)
            real = [None] * PAIRS
            imag = [None] * PAIRS
            for w in range(WINDOWS):
                lefts = [panel_ref[left + p * WINDOWS + w].astype(jnp.float32) for p in range(BLK)]
                rights = [panel_ref[right + q * WINDOWS + w].astype(jnp.float32) for q in range(BLK)]
                for p in range(BLK):
                    for q in range(BLK):
                        ra, ia = lefts[p][:chunks], lefts[p][chunks:]
                        rb, ib = rights[q][:chunks], rights[q][chunks:]
                        re = ra * rb + ia * ib
                        im = ia * rb - ra * ib
                        n = p * BLK + q
                        real[n] = re if w == 0 else real[n] + re
                        imag[n] = im if w == 0 else imag[n] + im
            for n in range(PAIRS):
                cross[pl.ds(t * PAIRS + n, chunks, stride=rows), :] = real[n] * weight
                cross[pl.ds(chunks * rows + t * PAIRS + n, chunks, stride=rows), :] = imag[n] * weight
            return 0

        lax.fori_loop(0, rows // PAIRS, one, 0, unroll=2)

    pieces = []
    for i in range(per_step):
        at = pl.multiple_of((step * per_step + i) * rows, 8)
        pieces.append(cross[pl.ds(at, rows), :].astype(jnp.bfloat16))
        pieces.append(cross[pl.ds(chunks * rows + at, rows), :].astype(jnp.bfloat16))
    part = jnp.dot(
        jnp.concatenate(pieces, axis=1), table_ref[...], preferred_element_type=jnp.float32
    )

    @pl.when(step == 0)
    def start():
        total[...] = part

    @pl.when(step > 0)
    def add():
        total[...] += part

    @pl.when(step == pl.num_programs(0) - 1)
    def finish():
        out_ref[...] = total[...].astype(jnp.bfloat16)


def correlate(panel, pick, table, chunks):
    slots = pick.shape[1]
    rows = slots * PAIRS
    per_step = 4
    return pl.pallas_call(
        functools.partial(corr_kernel, chunks, per_step),
        grid_spec=pltpu.PrefetchScalarGridSpec(
            num_scalar_prefetch=1,
            grid=(chunks // per_step,),
            in_specs=[
                pl.BlockSpec(panel.shape, lambda i, pick: (0, 0, 0)),
                pl.BlockSpec((per_step * 2 * LANES, LAGS), lambda i, pick: (i, 0)),
            ],
            out_specs=pl.BlockSpec((rows, LAGS), lambda i, pick: (0, 0)),
            scratch_shapes=[
                pltpu.VMEM((2 * chunks * rows, LANES), jnp.float32),
                pltpu.VMEM((rows, LAGS), jnp.float32),
            ],
        ),
        out_shape=jax.ShapeDtypeStruct((rows, LAGS), jnp.bfloat16),
        compiler_params=pltpu.CompilerParams(vmem_limit_bytes=VMEM_LIMIT),
        cost_estimate=pl.CostEstimate(
            flops=rows * chunks * 4 * LANES * LAGS,
            bytes_accessed=chunks * LANES * LAGS * 4,
            transcendentals=0,
        ),
        name="correlate",
    )(pick, panel, table)


def local(spectra, pair_blocks, owners):
    groups = lax.axis_size("grp")
    parts = lax.axis_size("chan")
    place = lax.axis_index("chan")
    chunks = F // LANES // parts

    lists = jnp.concatenate([pair_blocks[0, 0], owners[0, 0]], axis=1)
    lists = lax.all_gather(lists, "chan", axis=0)

    white = whiten(spectra, parts)
    panel = lax.all_to_all(white, "chan", split_axis=0, concat_axis=0, tiled=True)
    panel = panel.reshape(parts * white.shape[1], 2 * chunks, LANES)

    owner = lists[:, :, 2]
    same = owner[:, :, None] == owner[:, None, :]
    earlier = jnp.arange(NB_SRC)[None, :] < jnp.arange(NB_SRC)[:, None]
    rank = jnp.sum(jnp.logical_and(same, earlier), axis=2)
    slot = (owner * parts + jnp.arange(parts)[:, None]) * MOST + rank
    slots = groups * parts * MOST
    holds = slot.reshape(-1)[None, :] == jnp.arange(slots)[:, None]
    values = jnp.stack([lists[:, :, 0].reshape(-1), lists[:, :, 1].reshape(-1), jnp.ones((parts * NB_SRC,), jnp.int32)])
    pick = jnp.sum(jnp.where(holds[None], values[:, None, :], 0), axis=2).astype(jnp.int32)

    table = tables(place, chunks)
    corr = correlate(panel, pick, table, chunks)
    corr = corr.reshape(groups * parts, MOST, PAIRS, LAGS)
    got = lax.all_to_all(corr, ("grp", "chan"), split_axis=0, concat_axis=0, tiled=True)
    got = got.reshape(groups, parts, MOST, PAIRS, LAGS).astype(jnp.float32)
    return jnp.sum(got, axis=1).reshape(1, 1, groups * MOST, PAIRS, LAGS)


def solution(mesh):
    return jax.shard_map(
        local,
        mesh=mesh,
        in_specs=(
            P(("grp", "chan"), None, None, None),
            P("grp", "chan", None, None),
            P("grp", "chan", None, None),
        ),
        out_specs=P("grp", "chan", None, None, None),
        check_vma=False,
    )
```

```python
import functools

import jax
import jax.numpy as jnp
from jax import lax
from jax.experimental import pallas as pl
from jax.experimental.pallas import tpu as pltpu
from jax.sharding import PartitionSpec as P

F = 8192
LAGS = 1024
BLK = 2
NB_SRC = 18
MOST = 3
WINDOWS = 2
LANES = 128
PAIRS = BLK * BLK
VMEM_LIMIT = 48 * 1024 * 1024


def whiten_kernel(parts, spec_ref, out_ref):
    blocks = F // LANES
    each = blocks // parts

    def values(k):
        span = slice(k * LANES, (k + 1) * LANES)
        re = spec_ref[0, :, span].astype(jnp.float32)
        im = spec_ref[1, :, span].astype(jnp.float32)
        return re, im, re * re + im * im

    sums = [None] * 4
    for k in range(blocks):
        power = values(k)[2]
        sums[k % 4] = power if k < 4 else sums[k % 4] + power
    total = jnp.sum((sums[0] + sums[1]) + (sums[2] + sums[3]), axis=1, keepdims=True)
    level = 0.1 * (total * (1.0 / F) + 1e-05)
    for k in range(blocks):
        re, im, power = values(k)
        scale = lax.rsqrt(power + level)
        at = k % each * 2 * LANES
        out_ref[k // each, :, at : at + LANES] = (re * scale).astype(jnp.bfloat16)
        out_ref[k // each, :, at + LANES : at + 2 * LANES] = (im * scale).astype(jnp.bfloat16)


def whiten(spectra, parts):
    rows = spectra.shape[0] * WINDOWS
    step = 16
    planes = jnp.transpose(spectra.reshape(rows, 2, F), (1, 0, 2))
    width = 2 * F // parts
    return pl.pallas_call(
        functools.partial(whiten_kernel, parts),
        grid=(rows // step,),
        in_specs=[pl.BlockSpec((2, step, F), lambda i: (0, i, 0))],
        out_specs=pl.BlockSpec((parts, step, width), lambda i: (0, i, 0)),
        out_shape=jax.ShapeDtypeStruct((parts, rows, width), jnp.bfloat16),
        name="whiten",
    )(planes)


def table_kernel(first_ref, hi_cos_ref, hi_sin_ref, lo_cos_ref, lo_sin_ref, out_ref):
    s = pl.program_id(0)
    hi_cos = hi_cos_ref[pl.ds(s, 1), :]
    hi_sin = hi_sin_ref[pl.ds(s, 1), :]
    lo_cos = lo_cos_ref[...]
    lo_sin = lo_sin_ref[...]
    zero_bin = jnp.logical_and(first_ref[0] == 0, s == 0)
    row = lax.broadcasted_iota(jnp.int32, lo_cos.shape, 0)
    weight = jnp.where(jnp.logical_and(row == 0, zero_bin), 0.5, 1.0)
    out_ref[0:LANES] = ((hi_cos * lo_cos - hi_sin * lo_sin) * weight).astype(jnp.bfloat16)
    out_ref[LANES:] = -((hi_sin * lo_cos + hi_cos * lo_sin) * weight).astype(jnp.bfloat16)


def tables(place, chunks):
    lag = jnp.arange(LAGS, dtype=jnp.int32) - LAGS // 2

    def angles(bins):
        phase = bins[:, None] * lag[None, :] % (2 * F)
        return phase.astype(jnp.float32) * (jnp.pi / F)

    high = angles((place * chunks + jnp.arange(chunks, dtype=jnp.int32)) * LANES)
    low = angles(jnp.arange(LANES, dtype=jnp.int32))
    unit = 2.0 / jnp.sqrt(jnp.float32(F))
    whole = lambda shape: pl.BlockSpec(shape, lambda s, first: (0, 0))
    return pl.pallas_call(
        table_kernel,
        grid_spec=pltpu.PrefetchScalarGridSpec(
            num_scalar_prefetch=1,
            grid=(chunks,),
            in_specs=[
                whole((chunks, LAGS)),
                whole((chunks, LAGS)),
                whole((LANES, LAGS)),
                whole((LANES, LAGS)),
            ],
            out_specs=pl.BlockSpec((2 * LANES, LAGS), lambda s, first: (s, 0)),
        ),
        out_shape=jax.ShapeDtypeStruct((chunks * 2 * LANES, LAGS), jnp.bfloat16),
        cost_estimate=pl.CostEstimate(
            flops=chunks * LANES * LAGS * 8, bytes_accessed=chunks * LANES * LAGS * 4, transcendentals=0
        ),
        name="tables",
    )(place[None], jnp.cos(high) * unit, jnp.sin(high) * unit, jnp.cos(low), jnp.sin(low))


def corr_kernel(per_step, rows_ref, place_ref, panel_ref, table_ref, out_ref, total):
    step = pl.program_id(0)
    count = total.shape[0] // PAIRS
    chosen = jnp.dot(rows_ref[...], panel_ref[...], preferred_element_type=jnp.float32)

    def row(side, channel, window, start):
        first = ((side * BLK + channel) * WINDOWS + window) * count
        return chosen[first : first + count, start : start + LANES]

    columns = []
    for i in range(per_step):
        at = i * 2 * LANES
        real = []
        imag = []
        for p in range(BLK):
            for q in range(BLK):
                re = 0.0
                im = 0.0
                for w in range(WINDOWS):
                    ra, ia = row(0, p, w, at), row(0, p, w, at + LANES)
                    rb, ib = row(1, q, w, at), row(1, q, w, at + LANES)
                    re = re + (ra * rb + ia * ib)
                    im = im + (ia * rb - ra * ib)
                real.append(re * (1.0 / WINDOWS))
                imag.append(im * (1.0 / WINDOWS))
        columns.append(jnp.concatenate(real, axis=0).astype(jnp.bfloat16))
        columns.append(jnp.concatenate(imag, axis=0).astype(jnp.bfloat16))
    part = jnp.dot(
        jnp.concatenate(columns, axis=1), table_ref[...], preferred_element_type=jnp.float32
    )

    @pl.when(step == 0)
    def start():
        total[...] = part

    @pl.when(step > 0)
    def add():
        total[...] += part

    @pl.when(step == pl.num_programs(0) - 1)
    def finish():
        out_ref[...] = jnp.dot(
            place_ref[...], total[...].astype(jnp.bfloat16), preferred_element_type=jnp.float32
        ).astype(jnp.bfloat16)


def correlate(panel, rows, place, table):
    per_step = 4
    span = per_step * 2 * LANES
    return pl.pallas_call(
        functools.partial(corr_kernel, per_step),
        grid=(panel.shape[1] // span,),
        in_specs=[
            pl.BlockSpec(rows.shape, lambda i: (0, 0)),
            pl.BlockSpec(place.shape, lambda i: (0, 0)),
            pl.BlockSpec((panel.shape[0], span), lambda i: (0, i)),
            pl.BlockSpec((span, LAGS), lambda i: (i, 0)),
        ],
        out_specs=pl.BlockSpec((place.shape[0], LAGS), lambda i: (0, 0)),
        scratch_shapes=[pltpu.VMEM((place.shape[1], LAGS), jnp.float32)],
        out_shape=jax.ShapeDtypeStruct((place.shape[0], LAGS), jnp.bfloat16),
        compiler_params=pltpu.CompilerParams(vmem_limit_bytes=VMEM_LIMIT),
        cost_estimate=pl.CostEstimate(
            flops=2 * place.shape[1] * panel.shape[1] * LAGS,
            bytes_accessed=panel.shape[1] * LAGS * 2,
            transcendentals=0,
        ),
        name="correlate",
    )(rows, place, panel, table)


def choosers(lists, groups, parts, place, height):
    blocks = lists[:, :, :2].reshape(-1, 2)
    owner = lists[:, :, 2]
    offsets = jnp.arange(BLK * WINDOWS, dtype=jnp.int32)
    wanted = blocks.T[:, None, :] * (BLK * WINDOWS) + offsets[None, :, None]
    rows = wanted.reshape(-1, 1) == jnp.arange(height, dtype=jnp.int32)[None, :]
    same = owner[:, :, None] == owner[:, None, :]
    earlier = jnp.arange(NB_SRC)[None, :] < jnp.arange(NB_SRC)[:, None]
    rank = jnp.sum(jnp.logical_and(same, earlier), axis=2)
    source = (place - jnp.arange(parts, dtype=jnp.int32)) % parts
    slot = ((owner * parts + source[:, None]) * MOST + rank).reshape(-1)
    target = slot[None, :] * PAIRS + jnp.arange(PAIRS, dtype=jnp.int32)[:, None]
    slots = groups * parts * MOST * PAIRS
    chosen = jnp.arange(slots, dtype=jnp.int32)[:, None] == target.reshape(1, -1)
    return rows.astype(jnp.bfloat16), chosen.astype(jnp.bfloat16)


def local(spectra, pair_blocks, owners):
    groups = lax.axis_size("grp")
    parts = lax.axis_size("chan")
    place = lax.axis_index("chan")
    chunks = F // LANES // parts

    own = jnp.concatenate([pair_blocks[0, 0], owners[0, 0]], axis=1)
    lists = [own]
    for shift in range(1, parts):
        lists.append(lax.ppermute(own, "chan", [(i, (i + shift) % parts) for i in range(parts)]))

    white = whiten(spectra, parts)
    panel = lax.all_to_all(white, "chan", split_axis=0, concat_axis=0, tiled=True)
    panel = panel.reshape(parts * white.shape[1], white.shape[2])

    rows, chosen = choosers(jnp.stack(lists), groups, parts, place, panel.shape[0])
    table = tables(place, chunks)
    corr = correlate(panel, rows, chosen, table)
    corr = corr.reshape(groups * parts, MOST, PAIRS, LAGS)
    got = lax.all_to_all(corr, ("grp", "chan"), split_axis=0, concat_axis=0, tiled=True)
    got = got.reshape(groups, parts, MOST, PAIRS, LAGS).astype(jnp.float32)
    return jnp.sum(got, axis=1).reshape(1, 1, groups * MOST, PAIRS, LAGS)


def solution(mesh):
    return jax.shard_map(
        local,
        mesh=mesh,
        in_specs=(
            P(("grp", "chan"), None, None, None),
            P("grp", "chan", None, None),
            P("grp", "chan", None, None),
        ),
        out_specs=P("grp", "chan", None, None, None),
        check_vma=False,
    )
```

```python
import functools

import jax
import jax.numpy as jnp
from jax import lax
from jax.experimental import pallas as pl
from jax.experimental.pallas import tpu as pltpu
from jax.sharding import PartitionSpec as P

F = 8192
LAGS = 1024
BLK = 2
NB_SRC = 18
MOST = 3
WINDOWS = 2
LANES = 128
PAIRS = BLK * BLK
VMEM_LIMIT = 48 * 1024 * 1024


def whiten_kernel(parts, spec_ref, notes_ref, out_ref):
    blocks = F // LANES
    each = blocks // parts

    def values(k):
        span = slice(k * LANES, (k + 1) * LANES)
        re = spec_ref[0, :, span].astype(jnp.float32)
        im = spec_ref[1, :, span].astype(jnp.float32)
        return re, im, re * re + im * im

    for z in range(parts):
        out_ref[z, :, each * 2 * LANES :] = notes_ref[...]
    sums = [None] * 4
    for k in range(blocks):
        power = values(k)[2]
        sums[k % 4] = power if k < 4 else sums[k % 4] + power
    total = jnp.sum((sums[0] + sums[1]) + (sums[2] + sums[3]), axis=1, keepdims=True)
    level = 0.1 * (total * (1.0 / F) + 1e-05)
    for k in range(blocks):
        re, im, power = values(k)
        scale = lax.rsqrt(power + level)
        at = k % each * 2 * LANES
        out_ref[k // each, :, at : at + LANES] = (re * scale).astype(jnp.bfloat16)
        out_ref[k // each, :, at + LANES : at + 2 * LANES] = (im * scale).astype(jnp.bfloat16)


def whiten(spectra, notes, parts):
    rows = spectra.shape[0] * WINDOWS
    step = 16
    planes = jnp.transpose(spectra.reshape(rows, 2, F), (1, 0, 2))
    width = 2 * F // parts + LANES
    return pl.pallas_call(
        functools.partial(whiten_kernel, parts),
        grid=(rows // step,),
        in_specs=[
            pl.BlockSpec((2, step, F), lambda i: (0, i, 0)),
            pl.BlockSpec((step, LANES), lambda i: (i, 0)),
        ],
        out_specs=pl.BlockSpec((parts, step, width), lambda i: (0, i, 0)),
        out_shape=jax.ShapeDtypeStruct((parts, rows, width), jnp.bfloat16),
        name="whiten",
    )(planes, notes)


def table_kernel(first_ref, hi_cos_ref, hi_sin_ref, lo_cos_ref, lo_sin_ref, out_ref):
    s = pl.program_id(0)
    hi_cos = hi_cos_ref[pl.ds(s, 1), :]
    hi_sin = hi_sin_ref[pl.ds(s, 1), :]
    lo_cos = lo_cos_ref[...]
    lo_sin = lo_sin_ref[...]
    zero_bin = jnp.logical_and(first_ref[0] == 0, s == 0)
    row = lax.broadcasted_iota(jnp.int32, lo_cos.shape, 0)
    weight = jnp.where(jnp.logical_and(row == 0, zero_bin), 0.5, 1.0)
    out_ref[0:LANES] = ((hi_cos * lo_cos - hi_sin * lo_sin) * weight).astype(jnp.bfloat16)
    out_ref[LANES:] = -((hi_sin * lo_cos + hi_cos * lo_sin) * weight).astype(jnp.bfloat16)


def tables(place, chunks):
    lag = jnp.arange(LAGS, dtype=jnp.int32) - LAGS // 2

    def angles(bins):
        phase = bins[:, None] * lag[None, :] % (2 * F)
        return phase.astype(jnp.float32) * (jnp.pi / F)

    high = angles((place * chunks + jnp.arange(chunks, dtype=jnp.int32)) * LANES)
    low = angles(jnp.arange(LANES, dtype=jnp.int32))
    unit = 2.0 / jnp.sqrt(jnp.float32(F))
    whole = lambda shape: pl.BlockSpec(shape, lambda s, first: (0, 0))
    return pl.pallas_call(
        table_kernel,
        grid_spec=pltpu.PrefetchScalarGridSpec(
            num_scalar_prefetch=1,
            grid=(chunks,),
            in_specs=[
                whole((chunks, LAGS)),
                whole((chunks, LAGS)),
                whole((LANES, LAGS)),
                whole((LANES, LAGS)),
            ],
            out_specs=pl.BlockSpec((2 * LANES, LAGS), lambda s, first: (s, 0)),
        ),
        out_shape=jax.ShapeDtypeStruct((chunks * 2 * LANES, LAGS), jnp.bfloat16),
        cost_estimate=pl.CostEstimate(
            flops=chunks * LANES * LAGS * 8, bytes_accessed=chunks * LANES * LAGS * 4, transcendentals=0
        ),
        name="tables",
    )(place[None], jnp.cos(high) * unit, jnp.sin(high) * unit, jnp.cos(low), jnp.sin(low))


def choosers(parts, notes_ref, rows_ref, place_ref):
    count = parts * NB_SRC
    height = notes_ref.shape[0]

    def iota(shape, axis):
        return lax.broadcasted_iota(jnp.int32, shape, axis).astype(jnp.float32)

    line = iota((count, height), 0)
    at = line
    for z in range(1, parts):
        at = at + jnp.where(line >= z * NB_SRC, float(height // parts - NB_SRC), 0.0)
    listed = (at == iota((count, height), 1)).astype(jnp.float32).astype(jnp.bfloat16)
    notes = jnp.dot(listed, notes_ref[...], preferred_element_type=jnp.float32)
    left, right, owner, source = [notes[:, i : i + 1] for i in range(4)]
    across = iota((count, height), 1)
    picks = []
    for block in (left, right):
        for offset in range(BLK * WINDOWS):
            hit = across == block * (BLK * WINDOWS) + offset
            picks.append(hit.astype(jnp.float32))
    rows_ref[...] = jnp.concatenate(picks, axis=0).astype(jnp.bfloat16)

    owned = (iota((count, LANES), 1) == owner).astype(jnp.float32)
    other = iota((count, count), 1)
    before = jnp.logical_and(other < iota((count, count), 0), other >= source * NB_SRC)
    before = before.astype(jnp.float32).astype(jnp.bfloat16)
    seen = jnp.dot(before, owned.astype(jnp.bfloat16), preferred_element_type=jnp.float32)
    rank = jnp.sum(owned * seen, axis=1, keepdims=True)
    target = ((owner * parts + source) * MOST + rank) * PAIRS
    across = iota((count, place_ref.shape[1]), 1)
    places = [(across == target + n).astype(jnp.float32) for n in range(PAIRS)]
    place_ref[...] = jnp.concatenate(places, axis=0).astype(jnp.bfloat16)


def corr_kernel(per_step, parts, notes_ref, panel_ref, table_ref, out_ref, total, rows_ref, place_ref):
    step = pl.program_id(0)
    count = total.shape[0] // PAIRS

    @pl.when(step == 0)
    def prepare():
        choosers(parts, notes_ref, rows_ref, place_ref)

    chosen = jnp.dot(rows_ref[...], panel_ref[...], preferred_element_type=jnp.float32)

    def row(side, channel, window, start):
        first = ((side * BLK + channel) * WINDOWS + window) * count
        return chosen[first : first + count, start : start + LANES]

    columns = []
    for i in range(per_step):
        at = i * 2 * LANES
        real = []
        imag = []
        for p in range(BLK):
            for q in range(BLK):
                re = 0.0
                im = 0.0
                for w in range(WINDOWS):
                    ra, ia = row(0, p, w, at), row(0, p, w, at + LANES)
                    rb, ib = row(1, q, w, at), row(1, q, w, at + LANES)
                    re = re + (ra * rb + ia * ib)
                    im = im + (ia * rb - ra * ib)
                real.append(re * (1.0 / WINDOWS))
                imag.append(im * (1.0 / WINDOWS))
        columns.append(jnp.concatenate(real, axis=0).astype(jnp.bfloat16))
        columns.append(jnp.concatenate(imag, axis=0).astype(jnp.bfloat16))
    part = jnp.dot(
        jnp.concatenate(columns, axis=1), table_ref[...], preferred_element_type=jnp.float32
    )

    @pl.when(step == 0)
    def start():
        total[...] = part

    @pl.when(step > 0)
    def add():
        total[...] += part

    @pl.when(step == pl.num_programs(0) - 1)
    def finish():
        out_ref[...] = lax.dot_general(
            place_ref[...],
            total[...].astype(jnp.bfloat16),
            (((0,), (0,)), ((), ())),
            preferred_element_type=jnp.float32,
        ).astype(jnp.bfloat16)


def correlate(panel, table, groups, parts):
    per_step = 4
    span = per_step * 2 * LANES
    height = panel.shape[0]
    steps = panel.shape[1] // span
    pairs = parts * NB_SRC * PAIRS
    slots = groups * parts * MOST * PAIRS
    return pl.pallas_call(
        functools.partial(corr_kernel, per_step, parts),
        grid=(steps,),
        in_specs=[
            pl.BlockSpec((height, LANES), lambda i: (0, steps * span // LANES)),
            pl.BlockSpec((height, span), lambda i: (0, i)),
            pl.BlockSpec((span, LAGS), lambda i: (i, 0)),
        ],
        out_specs=pl.BlockSpec((slots, LAGS), lambda i: (0, 0)),
        scratch_shapes=[
            pltpu.VMEM((pairs, LAGS), jnp.float32),
            pltpu.VMEM((2 * pairs, height), jnp.bfloat16),
            pltpu.VMEM((pairs, slots), jnp.bfloat16),
        ],
        out_shape=jax.ShapeDtypeStruct((slots, LAGS), jnp.bfloat16),
        compiler_params=pltpu.CompilerParams(vmem_limit_bytes=VMEM_LIMIT),
        cost_estimate=pl.CostEstimate(
            flops=2 * pairs * steps * span * LAGS,
            bytes_accessed=steps * span * LAGS * 2,
            transcendentals=0,
        ),
        name="correlate",
    )(panel, panel, table)


def local(spectra, pair_blocks, owners):
    groups = lax.axis_size("grp")
    parts = lax.axis_size("chan")
    place = lax.axis_index("chan")
    chunks = F // LANES // parts
    rows = spectra.shape[0] * WINDOWS

    lane = lax.broadcasted_iota(jnp.int32, (NB_SRC, LANES), 1)
    blocks = pair_blocks[0, 0]
    notes = jnp.where(lane == 0, blocks[:, :1], jnp.where(lane == 1, blocks[:, 1:], place))
    notes = jnp.where(lane == 2, owners[0, 0], notes).astype(jnp.bfloat16)
    notes = jnp.pad(notes, ((0, rows - NB_SRC), (0, 0)))
    white = whiten(spectra, notes, parts)
    panel = lax.all_to_all(white, "chan", split_axis=0, concat_axis=0, tiled=True)
    panel = panel.reshape(parts * rows, white.shape[2])

    table = tables(place, chunks)
    corr = correlate(panel, table, groups, parts)
    corr = corr.reshape(groups * parts, MOST, PAIRS, LAGS)
    got = lax.all_to_all(corr, ("grp", "chan"), split_axis=0, concat_axis=0, tiled=True)
    got = got.reshape(groups, parts, MOST, PAIRS, LAGS).astype(jnp.float32)
    return jnp.sum(got, axis=1).reshape(1, 1, groups * MOST, PAIRS, LAGS)


def solution(mesh):
    return jax.shard_map(
        local,
        mesh=mesh,
        in_specs=(
            P(("grp", "chan"), None, None, None),
            P("grp", "chan", None, None),
            P("grp", "chan", None, None),
        ),
        out_specs=P("grp", "chan", None, None, None),
        check_vma=False,
    )
```

```python
import functools

import jax
import jax.numpy as jnp
from jax import lax
from jax.experimental import pallas as pl
from jax.experimental.pallas import tpu as pltpu
from jax.sharding import PartitionSpec as P

F = 8192
LAGS = 1024
BLK = 2
NB_SRC = 18
MOST = 3
WINDOWS = 2
LANES = 128
PAIRS = BLK * BLK
VMEM_LIMIT = 48 * 1024 * 1024


def whiten_kernel(parts, place_ref, spec_ref, notes_ref, *out_refs):
    blocks = F // LANES
    each = blocks // parts
    place = place_ref[0]

    def values(start):
        span = pl.ds(start, LANES)
        re = spec_ref[0, :, span].astype(jnp.float32)
        im = spec_ref[1, :, span].astype(jnp.float32)
        return re, im, re * re + im * im

    for out_ref in out_refs:
        out_ref[:, each * 2 * LANES :] = notes_ref[...]
    sums = [None] * 4
    for k in range(blocks):
        power = values(k * LANES)[2]
        sums[k % 4] = power if k < 4 else sums[k % 4] + power
    total = jnp.sum((sums[0] + sums[1]) + (sums[2] + sums[3]), axis=1, keepdims=True)
    level = 0.1 * (total * (1.0 / F) + 1e-05)
    for d, out_ref in enumerate(out_refs):
        first = jnp.bitwise_xor(place, d) * each
        for k in range(each):
            re, im, power = values(pl.multiple_of((first + k) * LANES, LANES))
            scale = lax.rsqrt(power + level)
            at = k * 2 * LANES
            out_ref[:, at : at + LANES] = (re * scale).astype(jnp.bfloat16)
            out_ref[:, at + LANES : at + 2 * LANES] = (im * scale).astype(jnp.bfloat16)


def whiten(spectra, notes, place, parts):
    rows = spectra.shape[0] * WINDOWS
    step = 16
    planes = jnp.transpose(spectra.reshape(rows, 2, F), (1, 0, 2))
    width = 2 * F // parts + LANES
    return pl.pallas_call(
        functools.partial(whiten_kernel, parts),
        grid_spec=pltpu.PrefetchScalarGridSpec(
            num_scalar_prefetch=1,
            grid=(rows // step,),
            in_specs=[
                pl.BlockSpec((2, step, F), lambda i, place: (0, i, 0)),
                pl.BlockSpec((step, LANES), lambda i, place: (i, 0)),
            ],
            out_specs=[pl.BlockSpec((step, width), lambda i, place: (i, 0))] * parts,
        ),
        out_shape=[jax.ShapeDtypeStruct((rows, width), jnp.bfloat16)] * parts,
        name="whiten",
    )(place[None], planes, notes)


def table_kernel(first_ref, hi_cos_ref, hi_sin_ref, lo_cos_ref, lo_sin_ref, out_ref):
    s = pl.program_id(0)
    hi_cos = hi_cos_ref[pl.ds(s, 1), :]
    hi_sin = hi_sin_ref[pl.ds(s, 1), :]
    lo_cos = lo_cos_ref[...]
    lo_sin = lo_sin_ref[...]
    zero_bin = jnp.logical_and(first_ref[0] == 0, s == 0)
    row = lax.broadcasted_iota(jnp.int32, lo_cos.shape, 0)
    weight = jnp.where(jnp.logical_and(row == 0, zero_bin), 0.5, 1.0)
    out_ref[0:LANES] = ((hi_cos * lo_cos - hi_sin * lo_sin) * weight).astype(jnp.bfloat16)
    out_ref[LANES:] = -((hi_sin * lo_cos + hi_cos * lo_sin) * weight).astype(jnp.bfloat16)


def tables(place, chunks):
    lag = jnp.arange(LAGS, dtype=jnp.int32) - LAGS // 2

    def angles(bins):
        phase = bins[:, None] * lag[None, :] % (2 * F)
        return phase.astype(jnp.float32) * (jnp.pi / F)

    high = angles((place * chunks + jnp.arange(chunks, dtype=jnp.int32)) * LANES)
    low = angles(jnp.arange(LANES, dtype=jnp.int32))
    unit = 2.0 / jnp.sqrt(jnp.float32(F))
    whole = lambda shape: pl.BlockSpec(shape, lambda s, first: (0, 0))
    return pl.pallas_call(
        table_kernel,
        grid_spec=pltpu.PrefetchScalarGridSpec(
            num_scalar_prefetch=1,
            grid=(chunks,),
            in_specs=[
                whole((chunks, LAGS)),
                whole((chunks, LAGS)),
                whole((LANES, LAGS)),
                whole((LANES, LAGS)),
            ],
            out_specs=pl.BlockSpec((2 * LANES, LAGS), lambda s, first: (s, 0)),
        ),
        out_shape=jax.ShapeDtypeStruct((chunks * 2 * LANES, LAGS), jnp.bfloat16),
        cost_estimate=pl.CostEstimate(
            flops=chunks * LANES * LAGS * 8, bytes_accessed=chunks * LANES * LAGS * 4, transcendentals=0
        ),
        name="tables",
    )(place[None], jnp.cos(high) * unit, jnp.sin(high) * unit, jnp.cos(low), jnp.sin(low))


def choosers(parts, place, packed, rows_ref, place_ref):
    count = parts * NB_SRC
    height = packed.shape[0]
    blocks = height // parts // (BLK * WINDOWS)

    def iota(shape, axis):
        return lax.broadcasted_iota(jnp.int32, shape, axis)

    def ones(hit):
        return hit.astype(jnp.float32).astype(jnp.bfloat16)

    line = iota((count, height), 0)
    at = line
    for z in range(1, parts):
        at = at + jnp.where(line >= z * NB_SRC, height // parts - NB_SRC, 0)
    listed = ones(at == iota((count, height), 1))
    notes = jnp.dot(listed, packed, preferred_element_type=jnp.float32).astype(jnp.int32)
    left, right, owner, source = [notes[:, i : i + 1] for i in range(4)]
    across = iota((count, height), 1)
    flip = place * blocks
    picks = []
    for block in (left, right):
        for offset in range(BLK * WINDOWS):
            picks.append((across == jnp.bitwise_xor(block, flip) * (BLK * WINDOWS) + offset).astype(jnp.float32))
    rows_ref[...] = jnp.concatenate(picks, axis=0).astype(jnp.bfloat16)

    owned = (iota((count, LANES), 1) == owner).astype(jnp.float32)
    other = iota((count, count), 1)
    before = ones(jnp.logical_and(other < iota((count, count), 0), other >= jnp.bitwise_xor(source, place) * NB_SRC))
    seen = jnp.dot(before, owned.astype(jnp.bfloat16), preferred_element_type=jnp.float32)
    rank = jnp.sum(owned * seen, axis=1, keepdims=True).astype(jnp.int32)
    target = ((owner * parts + source) * MOST + rank) * PAIRS
    across = iota((count, place_ref.shape[1]), 1)
    places = [(across == target + n).astype(jnp.float32) for n in range(PAIRS)]
    place_ref[...] = jnp.concatenate(places, axis=0).astype(jnp.bfloat16)


def corr_kernel(per_step, parts, place, *refs):
    note_refs, panel_refs = refs[:parts], refs[parts : 2 * parts]
    table_ref, out_ref, total, rows_ref, place_ref = refs[2 * parts :]
    step = pl.program_id(0)
    count = total.shape[0] // PAIRS

    @pl.when(step == 0)
    def prepare():
        choosers(parts, place[0], jnp.concatenate([ref[...] for ref in note_refs]), rows_ref, place_ref)

    panel = jnp.concatenate([ref[...] for ref in panel_refs])
    chosen = jnp.dot(rows_ref[...], panel, preferred_element_type=jnp.float32)

    def row(side, channel, window, start):
        first = ((side * BLK + channel) * WINDOWS + window) * count
        return chosen[first : first + count, start : start + LANES]

    columns = []
    for i in range(per_step):
        at = i * 2 * LANES
        real = []
        imag = []
        for p in range(BLK):
            for q in range(BLK):
                re = 0.0
                im = 0.0
                for w in range(WINDOWS):
                    ra, ia = row(0, p, w, at), row(0, p, w, at + LANES)
                    rb, ib = row(1, q, w, at), row(1, q, w, at + LANES)
                    re = re + (ra * rb + ia * ib)
                    im = im + (ia * rb - ra * ib)
                real.append(re * (1.0 / WINDOWS))
                imag.append(im * (1.0 / WINDOWS))
        columns.append(jnp.concatenate(real, axis=0).astype(jnp.bfloat16))
        columns.append(jnp.concatenate(imag, axis=0).astype(jnp.bfloat16))
    part = jnp.dot(
        jnp.concatenate(columns, axis=1), table_ref[...], preferred_element_type=jnp.float32
    )

    @pl.when(step == 0)
    def start():
        total[...] = part

    @pl.when(step > 0)
    def add():
        total[...] += part

    @pl.when(step == pl.num_programs(0) - 1)
    def finish():
        out_ref[...] = lax.dot_general(
            place_ref[...],
            total[...].astype(jnp.bfloat16),
            (((0,), (0,)), ((), ())),
            preferred_element_type=jnp.float32,
        ).astype(jnp.bfloat16)


def correlate(panels, table, place, groups):
    per_step = 4
    parts = len(panels)
    span = per_step * 2 * LANES
    deep = panels[0].shape[0]
    steps = panels[0].shape[1] // span
    pairs = parts * NB_SRC * PAIRS
    slots = groups * parts * MOST * PAIRS
    return pl.pallas_call(
        functools.partial(corr_kernel, per_step, parts),
        grid_spec=pltpu.PrefetchScalarGridSpec(
            num_scalar_prefetch=1,
            grid=(steps,),
            in_specs=[pl.BlockSpec((deep, LANES), lambda i, place: (0, steps * span // LANES))] * parts
            + [pl.BlockSpec((deep, span), lambda i, place: (0, i))] * parts
            + [pl.BlockSpec((span, LAGS), lambda i, place: (i, 0))],
            out_specs=pl.BlockSpec((slots, LAGS), lambda i, place: (0, 0)),
            scratch_shapes=[
                pltpu.VMEM((pairs, LAGS), jnp.float32),
                pltpu.VMEM((2 * pairs, deep * parts), jnp.bfloat16),
                pltpu.VMEM((pairs, slots), jnp.bfloat16),
            ],
        ),
        out_shape=jax.ShapeDtypeStruct((slots, LAGS), jnp.bfloat16),
        compiler_params=pltpu.CompilerParams(vmem_limit_bytes=VMEM_LIMIT),
        cost_estimate=pl.CostEstimate(
            flops=2 * pairs * steps * span * LAGS,
            bytes_accessed=steps * span * LAGS * 2,
            transcendentals=0,
        ),
        name="correlate",
    )(place[None], *panels, *panels, table)


def local(spectra, pair_blocks, owners):
    groups = lax.axis_size("grp")
    parts = lax.axis_size("chan")
    place = lax.axis_index("chan")
    chunks = F // LANES // parts
    rows = spectra.shape[0] * WINDOWS

    lane = lax.broadcasted_iota(jnp.int32, (NB_SRC, LANES), 1)
    blocks = pair_blocks[0, 0]
    notes = jnp.where(lane == 0, blocks[:, :1], jnp.where(lane == 1, blocks[:, 1:], place))
    notes = jnp.where(lane == 2, owners[0, 0], notes).astype(jnp.bfloat16)
    notes = jnp.pad(notes, ((0, rows - NB_SRC), (0, 0)))
    panels = list(whiten(spectra, notes, place, parts))
    for d in reversed(range(1, parts)):
        panels[d] = lax.ppermute(panels[d], "chan", [(i, i ^ d) for i in range(parts)])

    table = tables(place, chunks)
    corr = correlate(panels, table, place, groups)
    corr = corr.reshape(groups * parts, MOST, PAIRS, LAGS)
    got = lax.all_to_all(corr, ("grp", "chan"), split_axis=0, concat_axis=0, tiled=True)
    got = got.reshape(groups, parts, MOST, PAIRS, LAGS).astype(jnp.float32)
    return jnp.sum(got, axis=1).reshape(1, 1, groups * MOST, PAIRS, LAGS)


def solution(mesh):
    return jax.shard_map(
        local,
        mesh=mesh,
        in_specs=(
            P(("grp", "chan"), None, None, None),
            P("grp", "chan", None, None),
            P("grp", "chan", None, None),
        ),
        out_specs=P("grp", "chan", None, None, None),
        check_vma=False,
    )
```

```python
import functools

import jax
import jax.numpy as jnp
from jax import lax
from jax.experimental import pallas as pl
from jax.experimental.pallas import tpu as pltpu
from jax.sharding import PartitionSpec as P

F = 8192
LAGS = 1024
BLK = 2
NB_SRC = 18
MOST = 3
WINDOWS = 2
LANES = 128
PAIRS = BLK * BLK
VMEM_LIMIT = 48 * 1024 * 1024
HALVES = 2
JOINT = 1


def whiten_kernel(parts, second, place_ref, spec_ref, *refs):
    blocks = F // LANES
    each = blocks // parts
    place = place_ref[0]
    out_refs = list(refs[-parts:])

    def values(start):
        span = pl.ds(start, LANES)
        re = spec_ref[0, :, span].astype(jnp.float32)
        im = spec_ref[1, :, span].astype(jnp.float32)
        return re, im, re * re + im * im

    if second:
        deep = spec_ref.shape[1]
        joint = out_refs[JOINT]
        joint[:deep] = refs[0][...]
        joint[deep:, each * 2 * LANES :] = jnp.zeros((deep, LANES), jnp.bfloat16)
        out_refs[JOINT] = joint.at[deep:]
    else:
        pairs_ref, owners_ref = refs[:2]
        shape = (spec_ref.shape[1], LANES)
        line = lax.broadcasted_iota(jnp.int32, shape, 0)
        spare = jnp.zeros((1, LANES - NB_SRC), jnp.int32)
        wide = lambda row: jnp.broadcast_to(jnp.concatenate([row, spare], axis=1), shape)
        notes = jnp.where(line == 0, wide(pairs_ref[0:1]), jnp.where(line == 1, wide(pairs_ref[1:2]), place))
        notes = jnp.where(line == 2, wide(owners_ref[...]), notes)
        notes = notes.astype(jnp.float32).astype(jnp.bfloat16)
        for out_ref in out_refs:
            out_ref[:, each * 2 * LANES :] = notes
    sums = [None] * 4
    for k in range(blocks):
        power = values(k * LANES)[2]
        sums[k % 4] = power if k < 4 else sums[k % 4] + power
    total = jnp.sum((sums[0] + sums[1]) + (sums[2] + sums[3]), axis=1, keepdims=True)
    level = 0.1 * (total * (1.0 / F) + 1e-05)
    for d, out_ref in enumerate(out_refs):
        first = jnp.bitwise_xor(place, d) * each
        for k in range(each):
            re, im, power = values(pl.multiple_of((first + k) * LANES, LANES))
            scale = lax.rsqrt(power + level)
            at = k * 2 * LANES
            out_ref[:, at : at + LANES] = (re * scale).astype(jnp.bfloat16)
            out_ref[:, at + LANES : at + 2 * LANES] = (im * scale).astype(jnp.bfloat16)


def whiten(spectra, others, place, parts, second):
    rows = spectra.shape[0] * WINDOWS
    planes = jnp.transpose(spectra.reshape(rows, 2, F), (1, 0, 2))
    width = 2 * F // parts
    shapes = [(rows, width if second else width + LANES)] * parts
    if second:
        shapes[JOINT] = (HALVES * rows, width + LANES)
    whole = lambda array: pl.BlockSpec(array.shape, lambda i, place: (0,) * array.ndim)
    return list(pl.pallas_call(
        functools.partial(whiten_kernel, parts, second),
        grid_spec=pltpu.PrefetchScalarGridSpec(
            num_scalar_prefetch=1,
            grid=(1,),
            in_specs=[whole(array) for array in [planes, *others]],
            out_specs=[pl.BlockSpec(shape, lambda i, place: (0, 0)) for shape in shapes],
        ),
        out_shape=[jax.ShapeDtypeStruct(shape, jnp.bfloat16) for shape in shapes],
        name="whiten",
    )(place[None], planes, *others))


def table_kernel(first_ref, hi_cos_ref, hi_sin_ref, lo_cos_ref, lo_sin_ref, out_ref):
    s = pl.program_id(0)
    hi_cos = hi_cos_ref[pl.ds(s, 1), :]
    hi_sin = hi_sin_ref[pl.ds(s, 1), :]
    lo_cos = lo_cos_ref[...]
    lo_sin = lo_sin_ref[...]
    zero_bin = jnp.logical_and(first_ref[0] == 0, s == 0)
    row = lax.broadcasted_iota(jnp.int32, lo_cos.shape, 0)
    weight = jnp.where(jnp.logical_and(row == 0, zero_bin), 0.5, 1.0)
    out_ref[0:LANES] = ((hi_cos * lo_cos - hi_sin * lo_sin) * weight).astype(jnp.bfloat16)
    out_ref[LANES:] = -((hi_sin * lo_cos + hi_cos * lo_sin) * weight).astype(jnp.bfloat16)


def tables(place, chunks):
    lag = jnp.arange(LAGS, dtype=jnp.int32) - LAGS // 2

    def angles(bins):
        phase = bins[:, None] * lag[None, :] % (2 * F)
        return phase.astype(jnp.float32) * (jnp.pi / F)

    high = angles((place * chunks + jnp.arange(chunks, dtype=jnp.int32)) * LANES)
    low = angles(jnp.arange(LANES, dtype=jnp.int32))
    unit = 2.0 / jnp.sqrt(jnp.float32(F))
    whole = lambda shape: pl.BlockSpec(shape, lambda s, first: (0, 0))
    return pl.pallas_call(
        table_kernel,
        grid_spec=pltpu.PrefetchScalarGridSpec(
            num_scalar_prefetch=1,
            grid=(chunks,),
            in_specs=[
                whole((chunks, LAGS)),
                whole((chunks, LAGS)),
                whole((LANES, LAGS)),
                whole((LANES, LAGS)),
            ],
            out_specs=pl.BlockSpec((2 * LANES, LAGS), lambda s, first: (s, 0)),
        ),
        out_shape=jax.ShapeDtypeStruct((chunks * 2 * LANES, LAGS), jnp.bfloat16),
        cost_estimate=pl.CostEstimate(
            flops=chunks * LANES * LAGS * 8, bytes_accessed=chunks * LANES * LAGS * 4, transcendentals=0
        ),
        name="tables",
    )(place[None], jnp.cos(high) * unit, jnp.sin(high) * unit, jnp.cos(low), jnp.sin(low))


def choosers(parts, place, packed, rows_ref, place_ref):
    count = parts * NB_SRC
    height = rows_ref.shape[1]
    blocks = packed.shape[0] // parts // (BLK * WINDOWS)

    def iota(shape, axis):
        return lax.broadcasted_iota(jnp.int32, shape, axis)

    def ones(hit):
        return hit.astype(jnp.float32).astype(jnp.bfloat16)

    line = iota((count, 1), 0)
    group = jnp.zeros_like(line)
    for z in range(1, parts):
        group = group + jnp.where(line >= z * NB_SRC, 1, 0)
    deep = packed.shape[0] // parts
    here = iota((count, LANES), 1) == line - group * NB_SRC

    def column(kind):
        row = ones(iota((count, packed.shape[0]), 1) == group * deep + kind)
        found = jnp.dot(row, packed, preferred_element_type=jnp.float32)
        return jnp.sum(jnp.where(here, found, 0.0), axis=1, keepdims=True).astype(jnp.int32)

    left, right, owner, source = [column(kind) for kind in range(4)]
    across = iota((count, height), 1)
    picks = []
    for block in (left, right):
        place_of = jnp.bitwise_xor(lax.shift_right_logical(block, (HALVES * blocks).bit_length() - 1), place)
        half = jnp.bitwise_and(lax.shift_right_logical(block, blocks.bit_length() - 1), HALVES - 1)
        inner = jnp.bitwise_and(block, blocks - 1)
        first = (half * parts + place_of) * deep + inner * (BLK * WINDOWS)
        for offset in range(BLK * WINDOWS):
            picks.append((across == first + offset).astype(jnp.float32))
    rows_ref[...] = jnp.concatenate(picks, axis=0).astype(jnp.bfloat16)

    owned = (iota((count, LANES), 1) == owner).astype(jnp.float32)
    other = iota((count, count), 1)
    before = ones(jnp.logical_and(other < iota((count, count), 0), other >= jnp.bitwise_xor(source, place) * NB_SRC))
    seen = jnp.dot(before, owned.astype(jnp.bfloat16), preferred_element_type=jnp.float32)
    rank = jnp.sum(owned * seen, axis=1, keepdims=True).astype(jnp.int32)
    target = ((owner * parts + source) * MOST + rank) * PAIRS
    across = iota((count, place_ref.shape[1]), 1)
    places = [(across == target + n).astype(jnp.float32) for n in range(PAIRS)]
    place_ref[...] = jnp.concatenate(places, axis=0).astype(jnp.bfloat16)


def corr_kernel(per_step, parts, place, *refs):
    note_refs, panel_refs = refs[:parts], list(refs[parts : 3 * parts - 1])
    table_ref, out_ref, total, rows_ref, place_ref = refs[3 * parts - 1 :]
    deep = panel_refs[0].shape[0]
    panel_refs.insert(parts + JOINT, panel_refs[JOINT].at[deep:])
    panel_refs[JOINT] = panel_refs[JOINT].at[:deep]
    step = pl.program_id(0)
    count = total.shape[0] // PAIRS

    @pl.when(step == 0)
    def prepare():
        choosers(parts, place[0], jnp.concatenate([ref[:deep] for ref in note_refs]), rows_ref, place_ref)

    panel = jnp.concatenate([ref[...] for ref in panel_refs])
    chosen = jnp.dot(rows_ref[...], panel, preferred_element_type=jnp.float32)

    def row(side, channel, window, start):
        first = ((side * BLK + channel) * WINDOWS + window) * count
        return chosen[first : first + count, start : start + LANES]

    columns = []
    for i in range(per_step):
        at = i * 2 * LANES
        real = []
        imag = []
        for p in range(BLK):
            for q in range(BLK):
                re = 0.0
                im = 0.0
                for w in range(WINDOWS):
                    ra, ia = row(0, p, w, at), row(0, p, w, at + LANES)
                    rb, ib = row(1, q, w, at), row(1, q, w, at + LANES)
                    re = re + (ra * rb + ia * ib)
                    im = im + (ia * rb - ra * ib)
                real.append(re * (1.0 / WINDOWS))
                imag.append(im * (1.0 / WINDOWS))
        columns.append(jnp.concatenate(real, axis=0).astype(jnp.bfloat16))
        columns.append(jnp.concatenate(imag, axis=0).astype(jnp.bfloat16))
    part = jnp.dot(
        jnp.concatenate(columns, axis=1), table_ref[...], preferred_element_type=jnp.float32
    )

    @pl.when(step == 0)
    def start():
        total[...] = part

    @pl.when(step > 0)
    def add():
        total[...] += part

    @pl.when(step == pl.num_programs(0) - 1)
    def finish():
        out_ref[...] = lax.dot_general(
            place_ref[...],
            total[...].astype(jnp.bfloat16),
            (((0,), (0,)), ((), ())),
            preferred_element_type=jnp.float32,
        ).astype(jnp.bfloat16)


def correlate(panels, table, place, groups, parts):
    per_step = 4
    span = per_step * 2 * LANES
    deep = panels[0].shape[0]
    steps = table.shape[0] // span
    pairs = parts * NB_SRC * PAIRS
    slots = groups * parts * MOST * PAIRS
    return pl.pallas_call(
        functools.partial(corr_kernel, per_step, parts),
        grid_spec=pltpu.PrefetchScalarGridSpec(
            num_scalar_prefetch=1,
            grid=(steps,),
            in_specs=[
                pl.BlockSpec((array.shape[0], LANES), lambda i, place: (0, steps * span // LANES))
                for array in panels[:parts]
            ]
            + [pl.BlockSpec((array.shape[0], span), lambda i, place: (0, i)) for array in panels]
            + [pl.BlockSpec((span, LAGS), lambda i, place: (i, 0))],
            out_specs=pl.BlockSpec((slots, LAGS), lambda i, place: (0, 0)),
            scratch_shapes=[
                pltpu.VMEM((pairs, LAGS), jnp.float32),
                pltpu.VMEM((2 * pairs, deep * parts * HALVES), jnp.bfloat16),
                pltpu.VMEM((pairs, slots), jnp.bfloat16),
            ],
        ),
        out_shape=jax.ShapeDtypeStruct((slots, LAGS), jnp.bfloat16),
        compiler_params=pltpu.CompilerParams(vmem_limit_bytes=VMEM_LIMIT),
        cost_estimate=pl.CostEstimate(
            flops=2 * pairs * steps * span * LAGS,
            bytes_accessed=steps * span * LAGS * 2,
            transcendentals=0,
        ),
        name="correlate",
    )(place[None], *panels[:parts], *panels, table)


def local(spectra, pair_blocks, owners):
    groups = lax.axis_size("grp")
    parts = lax.axis_size("chan")
    place = lax.axis_index("chan")
    chunks = F // LANES // parts
    lists = [pair_blocks[0, 0].T, owners[0, 0].T]
    each = spectra.shape[0] // HALVES
    def swap(array, d):
        return lax.ppermute(array, "chan", [(i, i ^ d) for i in range(parts)])

    first = whiten(spectra[:each], lists, place, parts, False)
    apart = [d for d in reversed(range(1, parts)) if d != JOINT]
    spectra, ready = lax.optimization_barrier((spectra, first[JOINT]))
    for d in apart:
        first[d] = swap(first[d], d)
    second = whiten(spectra[each:], [ready], place, parts, True)
    for d in apart:
        second[d] = swap(second[d], d)
    first[JOINT] = swap(second.pop(JOINT), JOINT)
    panels = first + second

    table = tables(place, chunks)
    corr = correlate(panels, table, place, groups, parts)
    corr = corr.reshape(groups * parts, MOST, PAIRS, LAGS)
    got = lax.all_to_all(corr, ("grp", "chan"), split_axis=0, concat_axis=0, tiled=True)
    got = got.reshape(groups, parts, MOST, PAIRS, LAGS).astype(jnp.float32)
    return jnp.sum(got, axis=1).reshape(1, 1, groups * MOST, PAIRS, LAGS)


def solution(mesh):
    return jax.shard_map(
        local,
        mesh=mesh,
        in_specs=(
            P(("grp", "chan"), None, None, None),
            P("grp", "chan", None, None),
            P("grp", "chan", None, None),
        ),
        out_specs=P("grp", "chan", None, None, None),
        check_vma=False,
    )
```

```python
import functools

import jax
import jax.numpy as jnp
from jax import lax
from jax.experimental import pallas as pl
from jax.experimental.pallas import tpu as pltpu
from jax.sharding import PartitionSpec as P

F = 8192
LAGS = 1024
BLK = 2
NB_SRC = 18
MOST = 3
WINDOWS = 2
LANES = 128
PAIRS = BLK * BLK
VMEM_LIMIT = 48 * 1024 * 1024
HALVES = 2
JOINT = 1


def whiten_kernel(parts, second, place_ref, spec_ref, *refs):
    blocks = F // LANES
    each = blocks // parts
    place = place_ref[0]
    out_refs = list(refs[-parts:])

    def values(start):
        span = pl.ds(start, LANES)
        re = spec_ref[0, :, span].astype(jnp.float32)
        im = spec_ref[1, :, span].astype(jnp.float32)
        return re, im, re * re + im * im

    if second:
        deep = spec_ref.shape[1]
        joint = out_refs[JOINT]
        joint[:deep] = refs[0][...]
        joint[deep:, each * 2 * LANES :] = jnp.zeros((deep, LANES), jnp.bfloat16)
        out_refs[JOINT] = joint.at[deep:]
    else:
        pairs_ref = refs[0]
        shape = (spec_ref.shape[1], LANES)
        line = lax.broadcasted_iota(jnp.int32, shape, 0)
        spare = jnp.zeros((1, LANES - NB_SRC), jnp.int32)
        wide = lambda row: jnp.broadcast_to(jnp.concatenate([row, spare], axis=1), shape)
        notes = jnp.where(line == 0, wide(pairs_ref[0:1]), wide(pairs_ref[1:2]))
        notes = notes.astype(jnp.float32).astype(jnp.bfloat16)
        for out_ref in out_refs:
            out_ref[:, each * 2 * LANES :] = notes
    sums = [None] * 4
    for k in range(blocks):
        power = values(k * LANES)[2]
        sums[k % 4] = power if k < 4 else sums[k % 4] + power
    total = jnp.sum((sums[0] + sums[1]) + (sums[2] + sums[3]), axis=1, keepdims=True)
    level = 0.1 * (total * (1.0 / F) + 1e-05)
    for d, out_ref in enumerate(out_refs):
        first = jnp.bitwise_xor(place, d) * each
        for k in range(each):
            re, im, power = values(pl.multiple_of((first + k) * LANES, LANES))
            scale = lax.rsqrt(power + level)
            at = k * 2 * LANES
            out_ref[:, at : at + LANES] = (re * scale).astype(jnp.bfloat16)
            out_ref[:, at + LANES : at + 2 * LANES] = (im * scale).astype(jnp.bfloat16)


def whiten(spectra, others, place, parts, second):
    rows = spectra.shape[0] * WINDOWS
    planes = jnp.transpose(spectra.reshape(rows, 2, F), (1, 0, 2))
    width = 2 * F // parts
    shapes = [(rows, width if second else width + LANES)] * parts
    if second:
        shapes[JOINT] = (HALVES * rows, width + LANES)
    whole = lambda array: pl.BlockSpec(array.shape, lambda i, place: (0,) * array.ndim)
    return list(pl.pallas_call(
        functools.partial(whiten_kernel, parts, second),
        grid_spec=pltpu.PrefetchScalarGridSpec(
            num_scalar_prefetch=1,
            grid=(1,),
            in_specs=[whole(array) for array in [planes, *others]],
            out_specs=[pl.BlockSpec(shape, lambda i, place: (0, 0)) for shape in shapes],
        ),
        out_shape=[jax.ShapeDtypeStruct(shape, jnp.bfloat16) for shape in shapes],
        name="whiten",
    )(place[None], planes, *others))


def table_kernel(first_ref, hi_cos_ref, hi_sin_ref, mid_cos_ref, mid_sin_ref, lo_cos_ref, lo_sin_ref, out_ref, cos, sin):
    s = pl.program_id(0)
    few = lo_cos_ref.shape[0]

    @pl.when(s == 0)
    def combine():
        lo_cos = lo_cos_ref[...]
        lo_sin = lo_sin_ref[...]
        for i in range(LANES // few):
            mid_cos = mid_cos_ref[i : i + 1]
            mid_sin = mid_sin_ref[i : i + 1]
            cos[i * few : (i + 1) * few] = mid_cos * lo_cos - mid_sin * lo_sin
            sin[i * few : (i + 1) * few] = mid_sin * lo_cos + mid_cos * lo_sin

    hi_cos = hi_cos_ref[pl.ds(s, 1), :]
    hi_sin = hi_sin_ref[pl.ds(s, 1), :]
    minus_cos = -hi_cos
    for i in range(0, LANES, 16):
        lo_cos = cos[i : i + 16]
        lo_sin = sin[i : i + 16]
        out_ref[i : i + 16] = (hi_cos * lo_cos - hi_sin * lo_sin).astype(jnp.bfloat16)
        out_ref[LANES + i : LANES + i + 16] = (minus_cos * lo_sin - hi_sin * lo_cos).astype(jnp.bfloat16)

    @pl.when(jnp.logical_and(first_ref[0] == 0, s == 0))
    def zero_bin():
        row = lax.broadcasted_iota(jnp.int32, (16, LAGS), 0)
        weight = jnp.where(row == 0, 0.5, 1.0)
        out_ref[0:16] = ((hi_cos * cos[0:16] - hi_sin * sin[0:16]) * weight).astype(jnp.bfloat16)


def tables(place, chunks):
    lag = jnp.arange(LAGS, dtype=jnp.int32) - LAGS // 2
    few = 8
    middle = LANES // few
    bins = jnp.concatenate([
        (place * chunks + jnp.arange(chunks, dtype=jnp.int32)) * LANES,
        jnp.arange(middle, dtype=jnp.int32) * few,
        jnp.arange(few, dtype=jnp.int32),
    ])
    phase = bins[:, None] * lag[None, :] % (2 * F)
    angle = phase.astype(jnp.float32) * (jnp.pi / F)
    cos = jnp.cos(angle)
    sin = jnp.sin(angle)
    unit = 2.0 / jnp.sqrt(jnp.float32(F))
    cuts = [slice(0, chunks), slice(chunks, chunks + middle), slice(chunks + middle, None)]
    operands = [cos[cuts[0]] * unit, sin[cuts[0]] * unit, cos[cuts[1]], sin[cuts[1]], cos[cuts[2]], sin[cuts[2]]]
    return pl.pallas_call(
        table_kernel,
        grid_spec=pltpu.PrefetchScalarGridSpec(
            num_scalar_prefetch=1,
            grid=(chunks,),
            in_specs=[pl.BlockSpec(array.shape, lambda s, first: (0, 0)) for array in operands],
            out_specs=pl.BlockSpec((2 * LANES, LAGS), lambda s, first: (s, 0)),
            scratch_shapes=[pltpu.VMEM((LANES, LAGS), jnp.float32)] * 2,
        ),
        out_shape=jax.ShapeDtypeStruct((chunks * 2 * LANES, LAGS), jnp.bfloat16),
        cost_estimate=pl.CostEstimate(
            flops=chunks * LANES * LAGS * 8, bytes_accessed=chunks * LANES * LAGS * 4, transcendentals=0
        ),
        name="tables",
    )(place[None], *operands)


def iota(shape, axis):
    return lax.broadcasted_iota(jnp.int32, shape, axis)


def ones(hit):
    return hit.astype(jnp.float32).astype(jnp.bfloat16)


def choose_rows(parts, lists, place, packed, rows_ref):
    height = rows_ref.shape[1]
    count = rows_ref.shape[0] // (2 * BLK * WINDOWS)
    deep = packed.shape[0] // lists
    blocks = deep // (BLK * WINDOWS)
    line = iota((count, 1), 0)
    group = jnp.zeros_like(line)
    for z in range(1, lists):
        group = group + jnp.where(line >= z * NB_SRC, 1, 0)
    here = iota((count, LANES), 1) == line - group * NB_SRC

    def column(kind):
        row = ones(iota((count, packed.shape[0]), 1) == group * deep + kind)
        found = jnp.dot(row, packed, preferred_element_type=jnp.float32)
        return jnp.sum(jnp.where(here, found, 0.0), axis=1, keepdims=True).astype(jnp.int32)

    across = iota((count, height), 1)
    picks = []
    for block in (column(0), column(1)):
        source = jnp.bitwise_xor(lax.shift_right_logical(block, (HALVES * blocks).bit_length() - 1), place)
        half = jnp.bitwise_and(lax.shift_right_logical(block, blocks.bit_length() - 1), HALVES - 1)
        inner = jnp.bitwise_and(block, blocks - 1)
        first = (half * parts + source) * deep + inner * (BLK * WINDOWS)
        for offset in range(BLK * WINDOWS):
            picks.append((across == first + offset).astype(jnp.float32))
    rows_ref[...] = jnp.concatenate(picks, axis=0).astype(jnp.bfloat16)


def corr_kernel(per_step, parts, lists, place, *refs):
    refs = list(refs)
    note_refs, panel_refs, refs = refs[:lists], refs[lists : lists + 2 * parts - 1], refs[lists + 2 * parts - 1 :]
    table_ref, out_refs, (total, rows_ref) = refs[0], refs[1:-2], refs[-2:]
    deep = panel_refs[0].shape[0]
    panel_refs.insert(parts + JOINT, panel_refs[JOINT].at[deep:])
    panel_refs[JOINT] = panel_refs[JOINT].at[:deep]
    step = pl.program_id(0)
    count = total.shape[0] // PAIRS

    @pl.when(step == 0)
    def prepare():
        packed = jnp.concatenate([ref[:deep] for ref in note_refs])
        choose_rows(parts, lists, place[0], packed, rows_ref)

    panel = jnp.concatenate([ref[...] for ref in panel_refs])
    chosen = jnp.dot(rows_ref[...], panel, preferred_element_type=jnp.float32)

    def row(side, channel, window, start):
        first = ((side * BLK + channel) * WINDOWS + window) * count
        return chosen[first : first + count, start : start + LANES]

    columns = []
    for i in range(per_step):
        at = i * 2 * LANES
        real = []
        imag = []
        for p in range(BLK):
            for q in range(BLK):
                re = 0.0
                im = 0.0
                for w in range(WINDOWS):
                    ra, ia = row(0, p, w, at), row(0, p, w, at + LANES)
                    rb, ib = row(1, q, w, at), row(1, q, w, at + LANES)
                    re = re + (ra * rb + ia * ib)
                    im = im + (ia * rb - ra * ib)
                real.append(re * (1.0 / WINDOWS))
                imag.append(im * (1.0 / WINDOWS))
        columns.append(jnp.concatenate(real, axis=0).astype(jnp.bfloat16))
        columns.append(jnp.concatenate(imag, axis=0).astype(jnp.bfloat16))
    part = jnp.dot(
        jnp.concatenate(columns, axis=1), table_ref[...], preferred_element_type=jnp.float32
    )

    @pl.when(step == 0)
    def start():
        total[...] = part

    @pl.when(step > 0)
    def add():
        total[...] += part

    @pl.when(step == pl.num_programs(0) - 1)
    def finish():
        each = NB_SRC * PAIRS
        for i, out_ref in enumerate(out_refs):
            target = iota((each, count), 0) + i * each
            order = [ones(target == iota((each, count), 1) * PAIRS + n) for n in range(PAIRS)]
            out_ref[...] = sum(
                jnp.dot(
                    order[n],
                    total[n * count : (n + 1) * count].astype(jnp.bfloat16),
                    preferred_element_type=jnp.float32,
                )
                for n in range(PAIRS)
            ).astype(jnp.bfloat16)


def correlate(panels, table, place, parts, wanted):
    per_step = 4
    span = per_step * 2 * LANES
    deep = panels[0].shape[0]
    steps = table.shape[0] // span
    lists = len(wanted)
    count = -(-lists * NB_SRC // 8) * 8
    each = NB_SRC * PAIRS
    return pl.pallas_call(
        functools.partial(corr_kernel, per_step, parts, lists),
        grid_spec=pltpu.PrefetchScalarGridSpec(
            num_scalar_prefetch=1,
            grid=(steps,),
            in_specs=[
                pl.BlockSpec((panels[d].shape[0], LANES), lambda i, place: (0, steps * span // LANES))
                for d in wanted
            ]
            + [pl.BlockSpec((array.shape[0], span), lambda i, place: (0, i)) for array in panels]
            + [pl.BlockSpec((span, LAGS), lambda i, place: (i, 0))],
            out_specs=[pl.BlockSpec((each, LAGS), lambda i, place: (0, 0))] * lists,
            scratch_shapes=[
                pltpu.VMEM((count * PAIRS, LAGS), jnp.float32),
                pltpu.VMEM((2 * BLK * WINDOWS * count, deep * parts * HALVES), jnp.bfloat16),
            ],
        ),
        out_shape=[jax.ShapeDtypeStruct((each, LAGS), jnp.bfloat16)] * lists,
        compiler_params=pltpu.CompilerParams(vmem_limit_bytes=VMEM_LIMIT),
        cost_estimate=pl.CostEstimate(
            flops=2 * count * PAIRS * steps * span * LAGS,
            bytes_accessed=steps * span * LAGS * 2,
            transcendentals=0,
        ),
        name="correlate",
    )(place[None], *[panels[d] for d in wanted], *panels, table)


def settle_kernel(owners_ref, *refs):
    part_refs, out_ref = refs[:-1], refs[-1]
    rows = out_ref.shape[0]
    slots = rows // PAIRS
    each = NB_SRC * PAIRS
    tall = 24
    spare = jnp.full((1, LANES - NB_SRC), rows, jnp.int32)
    owner = jnp.concatenate([owners_ref[...], spare], axis=1)
    wide = jnp.broadcast_to(owner, (tall, LANES)).astype(jnp.float32)
    line, lane = iota((tall, LANES), 0), iota((tall, LANES), 1)
    other = jnp.sum(jnp.where(line == lane, wide, 0.0), axis=1, keepdims=True)
    earlier = jnp.logical_and(other == wide, line < lane).astype(jnp.float32)
    rank = jnp.sum(earlier, axis=0, keepdims=True)
    slot = owner.astype(jnp.float32) * MOST + rank
    held = ones(iota((slots, LANES), 0).astype(jnp.float32) == slot)
    down = ones(lax.shift_right_logical(iota((rows, slots), 0), 2) == iota((rows, slots), 1))
    over = ones(lax.shift_right_logical(iota((LANES, each), 1), 2) == iota((LANES, each), 0))
    block = jnp.dot(down, held, preferred_element_type=jnp.float32).astype(jnp.bfloat16)
    block = jnp.dot(block, over, preferred_element_type=jnp.float32)
    same = jnp.bitwise_and(iota((rows, each), 0), PAIRS - 1) == jnp.bitwise_and(iota((rows, each), 1), PAIRS - 1)
    chosen = jnp.where(same, block, 0.0).astype(jnp.bfloat16)
    total = sum(ref[...].astype(jnp.float32) for ref in part_refs)
    out_ref[...] = jnp.dot(chosen, total.astype(jnp.bfloat16), preferred_element_type=jnp.float32).astype(jnp.bfloat16)


def settle(owners, partials, groups):
    rows = groups * MOST * PAIRS
    return pl.pallas_call(
        settle_kernel,
        out_shape=jax.ShapeDtypeStruct((rows, LAGS), jnp.bfloat16),
        name="settle",
    )(owners, *partials)


def local(spectra, pair_blocks, owners):
    groups = lax.axis_size("grp")
    parts = lax.axis_size("chan")
    place = lax.axis_index("chan")
    chunks = F // LANES // parts
    each = spectra.shape[0] // HALVES

    def swap(array, d):
        return lax.ppermute(array, "chan", [(i, i ^ d) for i in range(parts)])

    first = whiten(spectra[:each], [pair_blocks[0, 0].T], place, parts, False)
    apart = [d for d in reversed(range(1, parts)) if d != JOINT]
    spectra, ready = lax.optimization_barrier((spectra, first[JOINT]))
    for d in apart:
        first[d] = swap(first[d], d)
    second = whiten(spectra[each:], [ready], place, parts, True)
    for d in apart:
        second[d] = swap(second[d], d)
    first[JOINT] = swap(second.pop(JOINT), JOINT)
    panels = first + second

    table = tables(place, chunks)
    order = list(reversed(range(parts)))
    partials = []
    for wanted in (order[: parts // 2], order[parts // 2 :]):
        for d, rows in zip(wanted, correlate(panels, table, place, parts, wanted)):
            partials.append(swap(rows, d) if d else rows)
    corr = settle(owners[0, 0].T, partials, groups)
    corr = corr.reshape(groups, MOST, PAIRS, LAGS)
    got = lax.all_to_all(corr, "grp", split_axis=0, concat_axis=0, tiled=True)
    return got.astype(jnp.float32).reshape(1, 1, groups * MOST, PAIRS, LAGS)


def solution(mesh):
    return jax.shard_map(
        local,
        mesh=mesh,
        in_specs=(
            P(("grp", "chan"), None, None, None),
            P("grp", "chan", None, None),
            P("grp", "chan", None, None),
        ),
        out_specs=P("grp", "chan", None, None, None),
        check_vma=False,
    )
```

```python
import functools

import jax
import jax.numpy as jnp
import numpy as np
from jax import lax
from jax.experimental import pallas as pl
from jax.experimental.pallas import tpu as pltpu
from jax.sharding import PartitionSpec as P

F = 8192
LAGS = 1024
BLK = 2
NB_SRC = 18
MOST = 3
WINDOWS = 2
LANES = 128
PAIRS = BLK * BLK
VMEM_LIMIT = 24 * 1024 * 1024
HALF = LAGS // 2
ROOM = 4
HALVES = 2
JOINT = 1


def whiten_kernel(parts, second, place_ref, spec_ref, *refs):
    blocks = F // LANES
    each = blocks // parts
    place = place_ref[0]
    out_refs = list(refs[-parts:])

    def values(start):
        span = pl.ds(start, LANES)
        re = spec_ref[0, :, span].astype(jnp.float32)
        im = spec_ref[1, :, span].astype(jnp.float32)
        return re, im, re * re + im * im

    if second:
        deep = spec_ref.shape[1]
        joint = out_refs[JOINT]
        joint[:deep] = refs[0][...]
        joint[deep:, each * 2 * LANES :] = jnp.zeros((deep, LANES), jnp.bfloat16)
        out_refs[JOINT] = joint.at[deep:]
    else:
        pairs_ref = refs[0]
        shape = (spec_ref.shape[1], LANES)
        line = lax.broadcasted_iota(jnp.int32, shape, 0)
        spare = jnp.zeros((1, LANES - NB_SRC), jnp.int32)
        wide = lambda row: jnp.broadcast_to(jnp.concatenate([row, spare], axis=1), shape)
        notes = jnp.where(line == 0, wide(pairs_ref[0:1]), wide(pairs_ref[1:2]))
        notes = notes.astype(jnp.float32).astype(jnp.bfloat16)
        for out_ref in out_refs:
            out_ref[:, each * 2 * LANES :] = notes
    sums = [None] * 4
    for k in range(blocks):
        power = values(k * LANES)[2]
        sums[k % 4] = power if k < 4 else sums[k % 4] + power
    total = jnp.sum((sums[0] + sums[1]) + (sums[2] + sums[3]), axis=1, keepdims=True)
    level = 0.1 * (total * (1.0 / F) + 1e-05)
    for d, out_ref in enumerate(out_refs):
        first = jnp.bitwise_xor(place, d) * each
        for k in range(each):
            re, im, power = values(pl.multiple_of((first + k) * LANES, LANES))
            scale = lax.rsqrt(power + level)
            at = k * 2 * LANES
            out_ref[:, at : at + LANES] = (re * scale).astype(jnp.bfloat16)
            out_ref[:, at + LANES : at + 2 * LANES] = (im * scale).astype(jnp.bfloat16)


def whiten(spectra, others, place, parts, second):
    rows = spectra.shape[0] * WINDOWS
    planes = jnp.transpose(spectra.reshape(rows, 2, F), (1, 0, 2))
    width = 2 * F // parts
    shapes = [(rows, width if second else width + LANES)] * parts
    if second:
        shapes[JOINT] = (HALVES * rows, width + LANES)
    whole = lambda array: pl.BlockSpec(array.shape, lambda i, place: (0,) * array.ndim)
    return list(pl.pallas_call(
        functools.partial(whiten_kernel, parts, second),
        grid_spec=pltpu.PrefetchScalarGridSpec(
            num_scalar_prefetch=1,
            grid=(1,),
            in_specs=[whole(array) for array in [planes, *others]],
            out_specs=[pl.BlockSpec(shape, lambda i, place: (0, 0)) for shape in shapes],
        ),
        out_shape=[jax.ShapeDtypeStruct(shape, jnp.bfloat16) for shape in shapes],
        compiler_params=pltpu.CompilerParams(vmem_limit_bytes=VMEM_LIMIT),
        name="whiten",
    )(place[None], planes, *others))


def table_kernel(first_ref, hi_cos_ref, hi_sin_ref, mid_cos_ref, mid_sin_ref, lo_cos_ref, lo_sin_ref, out_ref, cos, sin):
    s = pl.program_id(0)
    few = lo_cos_ref.shape[0]

    @pl.when(s == 0)
    def combine():
        lo_cos = lo_cos_ref[...]
        lo_sin = lo_sin_ref[...]
        for i in range(LANES // few):
            mid_cos = mid_cos_ref[i : i + 1]
            mid_sin = mid_sin_ref[i : i + 1]
            cos[i * few : (i + 1) * few] = mid_cos * lo_cos - mid_sin * lo_sin
            sin[i * few : (i + 1) * few] = mid_sin * lo_cos + mid_cos * lo_sin

    hi_cos = hi_cos_ref[pl.ds(s, 1), :]
    hi_sin = hi_sin_ref[pl.ds(s, 1), :]
    minus_cos = -hi_cos
    for i in range(0, LANES, 16):
        lo_cos = cos[i : i + 16]
        lo_sin = sin[i : i + 16]
        out_ref[i : i + 16, :HALF] = (hi_cos * lo_cos - hi_sin * lo_sin).astype(jnp.bfloat16)
        out_ref[i : i + 16, HALF:] = (minus_cos * lo_sin - hi_sin * lo_cos).astype(jnp.bfloat16)

    @pl.when(jnp.logical_and(first_ref[0] == 0, s == 0))
    def zero_bin():
        row = lax.broadcasted_iota(jnp.int32, (16, HALF), 0)
        weight = jnp.where(row == 0, 0.5, 1.0)
        out_ref[0:16, :HALF] = ((hi_cos * cos[0:16] - hi_sin * sin[0:16]) * weight).astype(jnp.bfloat16)


def tables(place, chunks):
    lag = jnp.arange(HALF, dtype=jnp.int32)
    few = 8
    middle = LANES // few
    bins = jnp.concatenate([
        (place * chunks + jnp.arange(chunks, dtype=jnp.int32)) * LANES,
        jnp.arange(middle, dtype=jnp.int32) * few,
        jnp.arange(few, dtype=jnp.int32),
    ])
    phase = bins[:, None] * lag[None, :] % (2 * F)
    angle = phase.astype(jnp.float32) * (jnp.pi / F)
    cos = jnp.cos(angle)
    sin = jnp.sin(angle)
    unit = 2.0 / jnp.sqrt(jnp.float32(F))
    cuts = [slice(0, chunks), slice(chunks, chunks + middle), slice(chunks + middle, None)]
    operands = [cos[cuts[0]] * unit, sin[cuts[0]] * unit, cos[cuts[1]], sin[cuts[1]], cos[cuts[2]], sin[cuts[2]]]
    return pl.pallas_call(
        table_kernel,
        grid_spec=pltpu.PrefetchScalarGridSpec(
            num_scalar_prefetch=1,
            grid=(chunks,),
            in_specs=[pl.BlockSpec(array.shape, lambda s, first: (0, 0)) for array in operands],
            out_specs=pl.BlockSpec((LANES, LAGS), lambda s, first: (s, 0)),
            scratch_shapes=[pltpu.VMEM((LANES, HALF), jnp.float32)] * 2,
        ),
        out_shape=jax.ShapeDtypeStruct((chunks * LANES, LAGS), jnp.bfloat16),
        cost_estimate=pl.CostEstimate(
            flops=chunks * LANES * LAGS * 4, bytes_accessed=chunks * LANES * LAGS * 2, transcendentals=0
        ),
        compiler_params=pltpu.CompilerParams(vmem_limit_bytes=VMEM_LIMIT),
        name="tables",
    )(place[None], *operands)


def iota(shape, axis):
    return lax.broadcasted_iota(jnp.int32, shape, axis)


def ones(hit):
    return hit.astype(jnp.float32).astype(jnp.bfloat16)


def choose_rows(parts, lists, place, packed, rows_ref):
    height = rows_ref.shape[1]
    count = rows_ref.shape[0] // (2 * BLK * WINDOWS)
    deep = packed.shape[0] // lists
    blocks = deep // (BLK * WINDOWS)
    line = iota((count, 1), 0)
    group = jnp.zeros_like(line)
    for z in range(1, lists):
        group = group + jnp.where(line >= z * NB_SRC, 1, 0)
    here = iota((count, LANES), 1) == line - group * NB_SRC

    def column(kind):
        row = ones(iota((count, packed.shape[0]), 1) == group * deep + kind)
        found = jnp.dot(row, packed, preferred_element_type=jnp.float32)
        return jnp.sum(jnp.where(here, found, 0.0), axis=1, keepdims=True).astype(jnp.int32)

    across = iota((count, height), 1)
    picks = []
    for block in (column(0), column(1)):
        source = jnp.bitwise_xor(lax.shift_right_logical(block, (HALVES * blocks).bit_length() - 1), place)
        half = jnp.bitwise_and(lax.shift_right_logical(block, blocks.bit_length() - 1), HALVES - 1)
        inner = jnp.bitwise_and(block, blocks - 1)
        first = (half * parts + source) * deep + inner * (BLK * WINDOWS)
        for offset in range(BLK * WINDOWS):
            picks.append((across == first + offset).astype(jnp.float32))
    rows_ref[...] = jnp.concatenate(picks, axis=0).astype(jnp.bfloat16)


def corr_kernel(per_step, parts, lists, place, *refs):
    refs = list(refs)
    note_refs, panel_refs, refs = refs[:lists], refs[lists : lists + 2 * parts - 1], refs[lists + 2 * parts - 1 :]
    (table_ref, ends_ref), out_refs, (total, edge, rows_ref) = refs[:2], refs[2:-3], refs[-3:]
    deep = panel_refs[0].shape[0]
    panel_refs.insert(parts + JOINT, panel_refs[JOINT].at[deep:])
    panel_refs[JOINT] = panel_refs[JOINT].at[:deep]
    step = pl.program_id(0)
    count = total.shape[0] // PAIRS

    @pl.when(step == 0)
    def prepare():
        packed = jnp.concatenate([ref[:deep] for ref in note_refs])
        choose_rows(parts, lists, place[0], packed, rows_ref)

    panel = jnp.concatenate([ref[...] for ref in panel_refs])
    chosen = jnp.dot(rows_ref[...], panel, preferred_element_type=jnp.float32)

    def row(side, channel, window, start):
        first = ((side * BLK + channel) * WINDOWS + window) * count
        return chosen[first : first + count, start : start + LANES]

    reals = []
    imags = []
    lane = iota((1, LANES), 1)
    first_bin = jnp.logical_and(jnp.logical_and(place[0] == 0, step == 0), lane == 0)
    edge_part = 0.0
    for i in range(per_step):
        at = i * 2 * LANES
        real = []
        imag = []
        for p in range(BLK):
            for q in range(BLK):
                re = 0.0
                im = 0.0
                for w in range(WINDOWS):
                    ra, ia = row(0, p, w, at), row(0, p, w, at + LANES)
                    rb, ib = row(1, q, w, at), row(1, q, w, at + LANES)
                    re = re + (ra * rb + ia * ib)
                    im = im + (ia * rb - ra * ib)
                real.append(re * (1.0 / WINDOWS))
                imag.append(im * (1.0 / WINDOWS))
        real = jnp.concatenate(real, axis=0)
        imag = jnp.concatenate(imag, axis=0)
        ends = ends_ref[0:1]
        if i == 0:
            ends = jnp.where(first_bin, 0.5 * ends, ends)
        edge_part = edge_part + (real * ends + imag * ends_ref[1:2])
        reals.append(real.astype(jnp.bfloat16))
        imags.append(imag.astype(jnp.bfloat16))

    def transform(pieces, columns):
        rows = jnp.concatenate(pieces, axis=1)
        return jnp.dot(rows, table_ref[:, columns], preferred_element_type=jnp.float32)

    even = transform(reals, slice(0, HALF))
    odd = transform(imags, slice(HALF, LAGS))

    @pl.when(step == 0)
    def start():
        total[:, :HALF] = even
        total[:, HALF:] = odd
        edge[...] = edge_part

    @pl.when(step > 0)
    def add():
        total[:, :HALF] += even
        total[:, HALF:] += odd
        edge[...] += edge_part

    @pl.when(step == pl.num_programs(0) - 1)
    def finish():
        even = total[:, :HALF]
        odd = total[:, HALF:]
        later = (even + odd).astype(jnp.bfloat16)
        mirror = ones(iota((HALF, HALF), 0) + iota((HALF, HALF), 1) == HALF)
        sooner = jnp.dot((even - odd).astype(jnp.bfloat16), mirror, preferred_element_type=jnp.float32)
        least = jnp.sum(edge[...], axis=1, keepdims=True)
        sooner = jnp.where(iota(sooner.shape, 1) == 0, least, sooner).astype(jnp.bfloat16)
        each = NB_SRC * PAIRS
        shape = (each * len(out_refs), PAIRS * count)
        column = iota(shape, 1)
        number = column * PAIRS
        for n in range(1, PAIRS):
            number = number - jnp.where(column >= n * count, count * PAIRS - 1, 0)
        order = ones(iota(shape, 0) == number)
        both = jnp.concatenate([sooner, later], axis=1)
        rows = jnp.dot(order, both, preferred_element_type=jnp.float32)
        for i, out_ref in enumerate(out_refs):
            out_ref[...] = rows[i * each : (i + 1) * each].astype(jnp.bfloat16)


def correlate(panels, table, place, parts, wanted):
    per_step = 4
    span = per_step * 2 * LANES
    deep = panels[0].shape[0]
    steps = 2 * table.shape[0] // span
    lists = len(wanted)
    count = -(-lists * NB_SRC // 8) * 8
    each = NB_SRC * PAIRS
    turn = np.arange(LANES) * (np.pi / 16)
    ends = np.stack([np.cos(turn), np.sin(turn)]) * (2.0 / np.sqrt(F))
    return pl.pallas_call(
        functools.partial(corr_kernel, per_step, parts, lists),
        grid_spec=pltpu.PrefetchScalarGridSpec(
            num_scalar_prefetch=1,
            grid=(steps,),
            in_specs=[
                pl.BlockSpec((panels[d].shape[0], LANES), lambda i, place: (0, steps * span // LANES))
                for d in wanted
            ]
            + [pl.BlockSpec((array.shape[0], span), lambda i, place: (0, i)) for array in panels]
            + [
                pl.BlockSpec((span // 2, LAGS), lambda i, place: (i, 0)),
                pl.BlockSpec((2, LANES), lambda i, place: (0, 0)),
            ],
            out_specs=[pl.BlockSpec((each, LAGS), lambda i, place: (0, 0))] * lists,
            scratch_shapes=[
                pltpu.VMEM((count * PAIRS, LAGS), jnp.float32),
                pltpu.VMEM((count * PAIRS, LANES), jnp.float32),
                pltpu.VMEM((2 * BLK * WINDOWS * count, deep * parts * HALVES), jnp.bfloat16),
            ],
        ),
        out_shape=[jax.ShapeDtypeStruct((each, LAGS), jnp.bfloat16)] * lists,
        compiler_params=pltpu.CompilerParams(vmem_limit_bytes=VMEM_LIMIT),
        cost_estimate=pl.CostEstimate(
            flops=count * PAIRS * steps * span * LAGS,
            bytes_accessed=steps * span * LAGS,
            transcendentals=0,
        ),
        name="correlate",
    )(place[None], *[panels[d] for d in wanted], *panels, table, jnp.asarray(ends, jnp.float32))


def settle_kernel(owners_ref, *refs):
    part_refs, out_ref = refs[:-1], refs[-1]
    rows = out_ref.shape[0]
    slots = rows // PAIRS
    each = NB_SRC * PAIRS
    tall = 24
    spare = jnp.full((1, LANES - NB_SRC), rows, jnp.int32)
    owner = jnp.concatenate([owners_ref[...], spare], axis=1)
    wide = jnp.broadcast_to(owner, (tall, LANES)).astype(jnp.float32)
    line, lane = iota((tall, LANES), 0), iota((tall, LANES), 1)
    other = jnp.sum(jnp.where(line == lane, wide, 0.0), axis=1, keepdims=True)
    earlier = jnp.logical_and(other == wide, line < lane).astype(jnp.float32)
    rank = jnp.sum(earlier, axis=0, keepdims=True)
    slot = owner.astype(jnp.float32) * ROOM + rank
    held = ones(iota((slots, LANES), 0).astype(jnp.float32) == slot)
    down = ones(lax.shift_right_logical(iota((rows, slots), 0), 2) == iota((rows, slots), 1))
    over = ones(lax.shift_right_logical(iota((LANES, each), 1), 2) == iota((LANES, each), 0))
    block = jnp.dot(down, held, preferred_element_type=jnp.float32).astype(jnp.bfloat16)
    block = jnp.dot(block, over, preferred_element_type=jnp.float32)
    same = jnp.bitwise_and(iota((rows, each), 0), PAIRS - 1) == jnp.bitwise_and(iota((rows, each), 1), PAIRS - 1)
    chosen = jnp.where(same, block, 0.0).astype(jnp.bfloat16)
    total = sum(ref[...].astype(jnp.float32) for ref in part_refs)
    out_ref[...] = jnp.dot(chosen, total.astype(jnp.bfloat16), preferred_element_type=jnp.float32).astype(jnp.bfloat16)


def settle(owners, partials, groups):
    rows = groups * ROOM * PAIRS
    return pl.pallas_call(
        settle_kernel,
        out_shape=jax.ShapeDtypeStruct((rows, LAGS), jnp.bfloat16),
        compiler_params=pltpu.CompilerParams(vmem_limit_bytes=VMEM_LIMIT),
        name="settle",
    )(owners, *partials)


def local(spectra, pair_blocks, owners):
    groups = lax.axis_size("grp")
    parts = lax.axis_size("chan")
    place = lax.axis_index("chan")
    chunks = F // LANES // parts
    each = spectra.shape[0] // HALVES

    def swap(array, d):
        return lax.ppermute(array, "chan", [(i, i ^ d) for i in range(parts)])

    first = whiten(spectra[:each], [pair_blocks[0, 0].T], place, parts, False)
    apart = [d for d in reversed(range(1, parts)) if d != JOINT]
    spectra, ready = lax.optimization_barrier((spectra, first[JOINT]))
    for d in apart:
        first[d] = swap(first[d], d)
    second = whiten(spectra[each:], [ready], place, parts, True)
    for d in apart:
        second[d] = swap(second[d], d)
    first[JOINT] = swap(second.pop(JOINT), JOINT)
    panels = first + second

    table = tables(place, chunks)
    order = list(reversed(range(parts)))
    partials = []
    for wanted in (order[: parts // 2], order[parts // 2 :]):
        for d, rows in zip(wanted, correlate(panels, table, place, parts, wanted)):
            partials.append(swap(rows, d) if d else rows)
    corr = settle(owners[0, 0].T, partials, groups)
    corr = corr.reshape(groups, ROOM * PAIRS, LAGS)
    got = lax.all_to_all(corr, "grp", split_axis=0, concat_axis=0, tiled=True)
    got = got[:, : MOST * PAIRS].reshape(groups * MOST, PAIRS, LAGS)
    return got.astype(jnp.float32).reshape(1, 1, groups * MOST, PAIRS, LAGS)


def solution(mesh):
    return jax.shard_map(
        local,
        mesh=mesh,
        in_specs=(
            P(("grp", "chan"), None, None, None),
            P("grp", "chan", None, None),
            P("grp", "chan", None, None),
        ),
        out_specs=P("grp", "chan", None, None, None),
        check_vma=False,
    )
```

```python
import functools

import jax
import jax.numpy as jnp
import numpy as np
from jax import lax
from jax.experimental import pallas as pl
from jax.experimental.pallas import tpu as pltpu
from jax.sharding import PartitionSpec as P

F = 8192
LAGS = 1024
BLK = 2
NB_SRC = 18
MOST = 3
WINDOWS = 2
LANES = 128
PAIRS = BLK * BLK
VMEM_LIMIT = 24 * 1024 * 1024
HALF = LAGS // 2
ROOM = 4
HALVES = 2
JOINT = 1


def whiten_kernel(parts, second, place_ref, spec_ref, *refs):
    blocks = F // LANES
    each = blocks // parts
    place = place_ref[0]
    out_refs = list(refs[-parts:])

    def values(start):
        span = pl.ds(start, LANES)
        re = spec_ref[0, :, span].astype(jnp.float32)
        im = spec_ref[1, :, span].astype(jnp.float32)
        return re, im, re * re + im * im

    if second:
        deep = spec_ref.shape[1]
        joint = out_refs[JOINT]
        joint[:deep, : each * 2 * LANES] = refs[0][...]
        joint[:deep, each * 2 * LANES :] = jnp.zeros((deep, LANES), jnp.bfloat16)
        out_refs[JOINT] = joint.at[deep:]
        pairs_ref = refs[1]
        shape = (spec_ref.shape[1], LANES)
        line = lax.broadcasted_iota(jnp.int32, shape, 0)
        spare = jnp.zeros((1, LANES - NB_SRC), jnp.int32)
        wide = lambda row: jnp.broadcast_to(jnp.concatenate([row, spare], axis=1), shape)
        notes = jnp.where(line == 0, wide(pairs_ref[0:1]), wide(pairs_ref[1:2]))
        notes = notes.astype(jnp.float32).astype(jnp.bfloat16)
        for out_ref in out_refs:
            out_ref[:, each * 2 * LANES :] = notes
    sums = [None] * 4
    for k in range(blocks):
        power = values(k * LANES)[2]
        sums[k % 4] = power if k < 4 else sums[k % 4] + power
    total = jnp.sum((sums[0] + sums[1]) + (sums[2] + sums[3]), axis=1, keepdims=True)
    level = 0.1 * (total * (1.0 / F) + 1e-05)
    for d, out_ref in enumerate(out_refs):
        first = jnp.bitwise_xor(place, d) * each
        for k in range(each):
            re, im, power = values(pl.multiple_of((first + k) * LANES, LANES))
            scale = lax.rsqrt(power + level)
            at = k * 2 * LANES
            out_ref[:, at : at + LANES] = (re * scale).astype(jnp.bfloat16)
            out_ref[:, at + LANES : at + 2 * LANES] = (im * scale).astype(jnp.bfloat16)


def whiten(spectra, others, place, parts, second):
    rows = spectra.shape[0] * WINDOWS
    planes = jnp.transpose(spectra.reshape(rows, 2, F), (1, 0, 2))
    width = 2 * F // parts
    shapes = [(rows, width + LANES if second else width)] * parts
    if second:
        shapes[JOINT] = (HALVES * rows, width + LANES)
    whole = lambda array: pl.BlockSpec(array.shape, lambda i, place: (0,) * array.ndim)
    return list(pl.pallas_call(
        functools.partial(whiten_kernel, parts, second),
        grid_spec=pltpu.PrefetchScalarGridSpec(
            num_scalar_prefetch=1,
            grid=(1,),
            in_specs=[whole(array) for array in [planes, *others]],
            out_specs=[pl.BlockSpec(shape, lambda i, place: (0, 0)) for shape in shapes],
        ),
        out_shape=[jax.ShapeDtypeStruct(shape, jnp.bfloat16) for shape in shapes],
        compiler_params=pltpu.CompilerParams(vmem_limit_bytes=VMEM_LIMIT),
        name="whiten",
    )(place[None], planes, *others))


def table_kernel(first_ref, hi_cos_ref, hi_sin_ref, mid_cos_ref, mid_sin_ref, lo_cos_ref, lo_sin_ref, out_ref, cos, sin):
    s = pl.program_id(0)
    few = lo_cos_ref.shape[0]

    @pl.when(s == 0)
    def combine():
        lo_cos = lo_cos_ref[...]
        lo_sin = lo_sin_ref[...]
        for i in range(LANES // few):
            mid_cos = mid_cos_ref[i : i + 1]
            mid_sin = mid_sin_ref[i : i + 1]
            cos[i * few : (i + 1) * few] = mid_cos * lo_cos - mid_sin * lo_sin
            sin[i * few : (i + 1) * few] = mid_sin * lo_cos + mid_cos * lo_sin

    hi_cos = hi_cos_ref[pl.ds(s, 1), :]
    hi_sin = hi_sin_ref[pl.ds(s, 1), :]
    minus_cos = -hi_cos
    for i in range(0, LANES, 16):
        lo_cos = cos[i : i + 16]
        lo_sin = sin[i : i + 16]
        out_ref[i : i + 16, :HALF] = (hi_cos * lo_cos - hi_sin * lo_sin).astype(jnp.bfloat16)
        out_ref[i : i + 16, HALF:] = (minus_cos * lo_sin - hi_sin * lo_cos).astype(jnp.bfloat16)

    @pl.when(jnp.logical_and(first_ref[0] == 0, s == 0))
    def zero_bin():
        row = lax.broadcasted_iota(jnp.int32, (16, HALF), 0)
        weight = jnp.where(row == 0, 0.5, 1.0)
        out_ref[0:16, :HALF] = ((hi_cos * cos[0:16] - hi_sin * sin[0:16]) * weight).astype(jnp.bfloat16)


def tables(place, chunks):
    lag = jnp.arange(HALF, dtype=jnp.int32)
    few = 8
    middle = LANES // few
    bins = jnp.concatenate([
        (place * chunks + jnp.arange(chunks, dtype=jnp.int32)) * LANES,
        jnp.arange(middle, dtype=jnp.int32) * few,
        jnp.arange(few, dtype=jnp.int32),
    ])
    phase = bins[:, None] * lag[None, :] % (2 * F)
    angle = phase.astype(jnp.float32) * (jnp.pi / F)
    cos = jnp.cos(angle)
    sin = jnp.sin(angle)
    unit = 2.0 / jnp.sqrt(jnp.float32(F))
    cuts = [slice(0, chunks), slice(chunks, chunks + middle), slice(chunks + middle, None)]
    operands = [cos[cuts[0]] * unit, sin[cuts[0]] * unit, cos[cuts[1]], sin[cuts[1]], cos[cuts[2]], sin[cuts[2]]]
    return pl.pallas_call(
        table_kernel,
        grid_spec=pltpu.PrefetchScalarGridSpec(
            num_scalar_prefetch=1,
            grid=(chunks,),
            in_specs=[pl.BlockSpec(array.shape, lambda s, first: (0, 0)) for array in operands],
            out_specs=pl.BlockSpec((LANES, LAGS), lambda s, first: (s, 0)),
            scratch_shapes=[pltpu.VMEM((LANES, HALF), jnp.float32)] * 2,
        ),
        out_shape=jax.ShapeDtypeStruct((chunks * LANES, LAGS), jnp.bfloat16),
        cost_estimate=pl.CostEstimate(
            flops=chunks * LANES * LAGS * 4, bytes_accessed=chunks * LANES * LAGS * 2, transcendentals=0
        ),
        compiler_params=pltpu.CompilerParams(vmem_limit_bytes=VMEM_LIMIT),
        name="tables",
    )(place[None], *operands)


def iota(shape, axis):
    return lax.broadcasted_iota(jnp.int32, shape, axis)


def ones(hit):
    return hit.astype(jnp.float32).astype(jnp.bfloat16)


def choose_rows(parts, lists, place, packed, rows_ref):
    height = rows_ref.shape[1]
    count = rows_ref.shape[0] // (2 * BLK * WINDOWS)
    deep = packed.shape[0] // lists
    blocks = deep // (BLK * WINDOWS)
    line = iota((count, 1), 0)
    group = jnp.zeros_like(line)
    for z in range(1, lists):
        group = group + jnp.where(line >= z * NB_SRC, 1, 0)
    here = iota((count, LANES), 1) == line - group * NB_SRC

    def column(kind):
        row = ones(iota((count, packed.shape[0]), 1) == group * deep + kind)
        found = jnp.dot(row, packed, preferred_element_type=jnp.float32)
        return jnp.sum(jnp.where(here, found, 0.0), axis=1, keepdims=True).astype(jnp.int32)

    across = iota((count, height), 1)
    picks = []
    for block in (column(0), column(1)):
        source = jnp.bitwise_xor(lax.shift_right_logical(block, (HALVES * blocks).bit_length() - 1), place)
        half = jnp.bitwise_and(lax.shift_right_logical(block, blocks.bit_length() - 1), HALVES - 1)
        inner = jnp.bitwise_and(block, blocks - 1)
        first = (half * parts + source) * deep + inner * (BLK * WINDOWS)
        for offset in range(BLK * WINDOWS):
            picks.append((across == first + offset).astype(jnp.float32))
    rows_ref[...] = jnp.concatenate(picks, axis=0).astype(jnp.bfloat16)


def corr_kernel(per_step, parts, lists, place, *refs):
    refs = list(refs)
    note_refs, panel_refs, refs = refs[:lists], refs[lists : lists + 2 * parts - 1], refs[lists + 2 * parts - 1 :]
    (table_ref, ends_ref), out_refs, (total, edge, rows_ref) = refs[:2], refs[2:-3], refs[-3:]
    deep = panel_refs[0].shape[0]
    panel_refs.insert(parts + JOINT, panel_refs[JOINT].at[deep:])
    panel_refs[JOINT] = panel_refs[JOINT].at[:deep]
    step = pl.program_id(0)
    count = total.shape[0] // PAIRS

    @pl.when(step == 0)
    def prepare():
        packed = jnp.concatenate([ref[ref.shape[0] - deep :] for ref in note_refs])
        choose_rows(parts, lists, place[0], packed, rows_ref)

    panel = jnp.concatenate([ref[...] for ref in panel_refs])
    chosen = jnp.dot(rows_ref[...], panel, preferred_element_type=jnp.float32)

    def row(side, channel, window, start):
        first = ((side * BLK + channel) * WINDOWS + window) * count
        return chosen[first : first + count, start : start + LANES]

    reals = []
    imags = []
    lane = iota((1, LANES), 1)
    first_bin = jnp.logical_and(jnp.logical_and(place[0] == 0, step == 0), lane == 0)
    edge_part = 0.0
    for i in range(per_step):
        at = i * 2 * LANES
        real = []
        imag = []
        for p in range(BLK):
            for q in range(BLK):
                re = 0.0
                im = 0.0
                for w in range(WINDOWS):
                    ra, ia = row(0, p, w, at), row(0, p, w, at + LANES)
                    rb, ib = row(1, q, w, at), row(1, q, w, at + LANES)
                    re = re + (ra * rb + ia * ib)
                    im = im + (ia * rb - ra * ib)
                real.append(re * (1.0 / WINDOWS))
                imag.append(im * (1.0 / WINDOWS))
        real = jnp.concatenate(real, axis=0)
        imag = jnp.concatenate(imag, axis=0)
        ends = ends_ref[0:1]
        if i == 0:
            ends = jnp.where(first_bin, 0.5 * ends, ends)
        edge_part = edge_part + (real * ends + imag * ends_ref[1:2])
        reals.append(real.astype(jnp.bfloat16))
        imags.append(imag.astype(jnp.bfloat16))

    def transform(pieces, columns):
        rows = jnp.concatenate(pieces, axis=1)
        return jnp.dot(rows, table_ref[:, columns], preferred_element_type=jnp.float32)

    even = transform(reals, slice(0, HALF))
    odd = transform(imags, slice(HALF, LAGS))

    @pl.when(step == 0)
    def start():
        total[:, :HALF] = even
        total[:, HALF:] = odd
        edge[...] = edge_part

    @pl.when(step > 0)
    def add():
        total[:, :HALF] += even
        total[:, HALF:] += odd
        edge[...] += edge_part

    @pl.when(step == pl.num_programs(0) - 1)
    def finish():
        even = total[:, :HALF]
        odd = total[:, HALF:]
        later = (even + odd).astype(jnp.bfloat16)
        mirror = ones(iota((HALF, HALF), 0) + iota((HALF, HALF), 1) == HALF)
        sooner = jnp.dot((even - odd).astype(jnp.bfloat16), mirror, preferred_element_type=jnp.float32)
        least = jnp.sum(edge[...], axis=1, keepdims=True)
        sooner = jnp.where(iota(sooner.shape, 1) == 0, least, sooner).astype(jnp.bfloat16)
        each = NB_SRC * PAIRS
        shape = (each * len(out_refs), PAIRS * count)
        column = iota(shape, 1)
        number = column * PAIRS
        for n in range(1, PAIRS):
            number = number - jnp.where(column >= n * count, count * PAIRS - 1, 0)
        order = ones(iota(shape, 0) == number)
        both = jnp.concatenate([sooner, later], axis=1)
        rows = jnp.dot(order, both, preferred_element_type=jnp.float32)
        for i, out_ref in enumerate(out_refs):
            out_ref[...] = rows[i * each : (i + 1) * each].astype(jnp.bfloat16)


def correlate(panels, table, place, parts, wanted):
    per_step = 4
    span = per_step * 2 * LANES
    deep = panels[0].shape[0]
    steps = 2 * table.shape[0] // span
    lists = len(wanted)
    count = -(-lists * NB_SRC // 8) * 8
    each = NB_SRC * PAIRS
    noted = panels[parts:]
    noted.insert(JOINT, panels[JOINT])
    turn = np.arange(LANES) * (np.pi / 16)
    ends = np.stack([np.cos(turn), np.sin(turn)]) * (2.0 / np.sqrt(F))
    return pl.pallas_call(
        functools.partial(corr_kernel, per_step, parts, lists),
        grid_spec=pltpu.PrefetchScalarGridSpec(
            num_scalar_prefetch=1,
            grid=(steps,),
            in_specs=[
                pl.BlockSpec((noted[d].shape[0], LANES), lambda i, place: (0, steps * span // LANES))
                for d in wanted
            ]
            + [pl.BlockSpec((array.shape[0], span), lambda i, place: (0, i)) for array in panels]
            + [
                pl.BlockSpec((span // 2, LAGS), lambda i, place: (i, 0)),
                pl.BlockSpec((2, LANES), lambda i, place: (0, 0)),
            ],
            out_specs=[pl.BlockSpec((each, LAGS), lambda i, place: (0, 0))] * lists,
            scratch_shapes=[
                pltpu.VMEM((count * PAIRS, LAGS), jnp.float32),
                pltpu.VMEM((count * PAIRS, LANES), jnp.float32),
                pltpu.VMEM((2 * BLK * WINDOWS * count, deep * parts * HALVES), jnp.bfloat16),
            ],
        ),
        out_shape=[jax.ShapeDtypeStruct((each, LAGS), jnp.bfloat16)] * lists,
        compiler_params=pltpu.CompilerParams(vmem_limit_bytes=VMEM_LIMIT),
        cost_estimate=pl.CostEstimate(
            flops=count * PAIRS * steps * span * LAGS,
            bytes_accessed=steps * span * LAGS,
            transcendentals=0,
        ),
        name="correlate",
    )(place[None], *[noted[d] for d in wanted], *panels, table, jnp.asarray(ends, jnp.float32))


def settle_kernel(groups, mine_ref, owners_ref, *refs):
    part_refs, out_refs = refs[:-groups], refs[-groups:]
    rows = groups * ROOM * PAIRS
    slots = rows // PAIRS
    each = NB_SRC * PAIRS
    tall = 24
    spare = jnp.full((1, LANES - NB_SRC), rows, jnp.int32)
    owner = jnp.concatenate([owners_ref[...], spare], axis=1)
    wide = jnp.broadcast_to(owner, (tall, LANES)).astype(jnp.float32)
    line, lane = iota((tall, LANES), 0), iota((tall, LANES), 1)
    other = jnp.sum(jnp.where(line == lane, wide, 0.0), axis=1, keepdims=True)
    earlier = jnp.logical_and(other == wide, line < lane).astype(jnp.float32)
    rank = jnp.sum(earlier, axis=0, keepdims=True)
    slot = jnp.bitwise_xor(owner, mine_ref[0]).astype(jnp.float32) * ROOM + rank
    held = ones(iota((slots, LANES), 0).astype(jnp.float32) == slot)
    down = ones(lax.shift_right_logical(iota((rows, slots), 0), 2) == iota((rows, slots), 1))
    over = ones(lax.shift_right_logical(iota((LANES, each), 1), 2) == iota((LANES, each), 0))
    block = jnp.dot(down, held, preferred_element_type=jnp.float32).astype(jnp.bfloat16)
    block = jnp.dot(block, over, preferred_element_type=jnp.float32)
    same = jnp.bitwise_and(iota((rows, each), 0), PAIRS - 1) == jnp.bitwise_and(iota((rows, each), 1), PAIRS - 1)
    chosen = jnp.where(same, block, 0.0).astype(jnp.bfloat16)
    total = sum(ref[...].astype(jnp.float32) for ref in part_refs)
    placed = jnp.dot(chosen, total.astype(jnp.bfloat16), preferred_element_type=jnp.float32)
    deep = ROOM * PAIRS
    for m, out_ref in enumerate(out_refs):
        out_ref[...] = placed[m * deep : (m + 1) * deep].astype(jnp.bfloat16)


def settle(owners, partials, mine, groups):
    whole = lambda array: pl.BlockSpec(array.shape, lambda i, mine: (0, 0))
    outs = [jax.ShapeDtypeStruct((ROOM * PAIRS, LAGS), jnp.bfloat16)] * groups
    return list(pl.pallas_call(
        functools.partial(settle_kernel, groups),
        grid_spec=pltpu.PrefetchScalarGridSpec(
            num_scalar_prefetch=1,
            grid=(1,),
            in_specs=[whole(array) for array in [owners, *partials]],
            out_specs=[whole(array) for array in outs],
        ),
        out_shape=outs,
        compiler_params=pltpu.CompilerParams(vmem_limit_bytes=VMEM_LIMIT),
        name="settle",
    )(mine[None], owners, *partials))


def widen_kernel(mine_ref, *refs):
    part_refs, out_ref = refs[:-1], refs[-1]
    for m, part_ref in enumerate(part_refs):
        values = part_ref[...].astype(jnp.float32)
        first = jnp.bitwise_xor(mine_ref[0], m) * MOST
        for r in range(MOST):
            out_ref[first + r] = values[r * PAIRS : (r + 1) * PAIRS]


def widen(pieces, mine):
    shape = (len(pieces) * MOST, PAIRS, LAGS)
    return pl.pallas_call(
        widen_kernel,
        grid_spec=pltpu.PrefetchScalarGridSpec(
            num_scalar_prefetch=1,
            grid=(1,),
            in_specs=[pl.BlockSpec(array.shape, lambda i, mine: (0, 0)) for array in pieces],
            out_specs=pl.BlockSpec(shape, lambda i, mine: (0, 0, 0)),
        ),
        out_shape=jax.ShapeDtypeStruct(shape, jnp.float32),
        compiler_params=pltpu.CompilerParams(vmem_limit_bytes=VMEM_LIMIT),
        name="widen",
    )(mine[None], *pieces)


def local(spectra, pair_blocks, owners):
    groups = lax.axis_size("grp")
    parts = lax.axis_size("chan")
    place = lax.axis_index("chan")
    chunks = F // LANES // parts
    each = spectra.shape[0] // HALVES

    def swap(array, d):
        return lax.ppermute(array, "chan", [(i, i ^ d) for i in range(parts)])

    first = whiten(spectra[:each], [], place, parts, False)
    apart = [d for d in reversed(range(1, parts)) if d != JOINT]
    spectra, ready = lax.optimization_barrier((spectra, first[JOINT]))
    for d in apart:
        first[d] = swap(first[d], d)
    second = whiten(spectra[each:], [ready, pair_blocks[0, 0].T], place, parts, True)
    for d in apart:
        second[d] = swap(second[d], d)
    first[JOINT] = swap(second.pop(JOINT), JOINT)
    panels = first + second

    table = tables(place, chunks)
    order = list(reversed(range(parts)))
    partials = []
    for wanted in (order[: parts // 2], order[parts // 2 :]):
        for d, rows in zip(wanted, correlate(panels, table, place, parts, wanted)):
            partials.append(swap(rows, d) if d else rows)
    mine = lax.axis_index("grp")
    pieces = settle(owners[0, 0].T, partials, mine, groups)
    for m in reversed(range(1, groups)):
        pieces[m] = lax.ppermute(pieces[m], "grp", [(i, i ^ m) for i in range(groups)])
    return widen(pieces, mine)[None, None]


def solution(mesh):
    return jax.shard_map(
        local,
        mesh=mesh,
        in_specs=(
            P(("grp", "chan"), None, None, None),
            P("grp", "chan", None, None),
            P("grp", "chan", None, None),
        ),
        out_specs=P("grp", "chan", None, None, None),
        check_vma=False,
    )
```

```python
import functools

import jax
import jax.numpy as jnp
import numpy as np
from jax import lax
from jax.experimental import pallas as pl
from jax.experimental.pallas import tpu as pltpu
from jax.sharding import PartitionSpec as P

F = 8192
LAGS = 1024
BLK = 2
NB_SRC = 18
MOST = 3
WINDOWS = 2
LANES = 128
PAIRS = BLK * BLK
VMEM_LIMIT = 24 * 1024 * 1024
HALF = LAGS // 2
ROOM = 4
WAVES = 2


def whiten_kernel(parts, place_ref, spec_ref, pairs_ref, *out_refs):
    blocks = F // LANES
    each = blocks // parts
    share = each // WAVES
    place = place_ref[0]

    def values(start):
        span = pl.ds(start, LANES)
        re = spec_ref[0, :, span].astype(jnp.float32)
        im = spec_ref[1, :, span].astype(jnp.float32)
        return re, im, re * re + im * im

    shape = (spec_ref.shape[1], LANES)
    line = lax.broadcasted_iota(jnp.int32, shape, 0)
    spare = jnp.zeros((1, LANES - NB_SRC), jnp.int32)
    wide = lambda row: jnp.broadcast_to(jnp.concatenate([row, spare], axis=1), shape)
    notes = jnp.where(line == 0, wide(pairs_ref[0:1]), wide(pairs_ref[1:2]))
    notes = notes.astype(jnp.float32).astype(jnp.bfloat16)
    for out_ref in out_refs[:parts]:
        out_ref[:, share * 2 * LANES :] = notes
    sums = [None] * 4
    for k in range(blocks):
        power = values(k * LANES)[2]
        sums[k % 4] = power if k < 4 else sums[k % 4] + power
    total = jnp.sum((sums[0] + sums[1]) + (sums[2] + sums[3]), axis=1, keepdims=True)
    level = 0.1 * (total * (1.0 / F) + 1e-05)
    for index, out_ref in enumerate(out_refs):
        first = jnp.bitwise_xor(place, index % parts) * each + index // parts * share
        for k in range(share):
            re, im, power = values(pl.multiple_of((first + k) * LANES, LANES))
            scale = lax.rsqrt(power + level)
            at = k * 2 * LANES
            out_ref[:, at : at + LANES] = (re * scale).astype(jnp.bfloat16)
            out_ref[:, at + LANES : at + 2 * LANES] = (im * scale).astype(jnp.bfloat16)


def whiten(spectra, pairs, place, parts):
    rows = spectra.shape[0] * WINDOWS
    planes = jnp.transpose(spectra.reshape(rows, 2, F), (1, 0, 2))
    width = 2 * F // parts // WAVES
    shapes = [(rows, width + LANES)] * parts + [(rows, width)] * parts * (WAVES - 1)
    whole = lambda array: pl.BlockSpec(array.shape, lambda i, place: (0,) * array.ndim)
    outs = pl.pallas_call(
        functools.partial(whiten_kernel, parts),
        grid_spec=pltpu.PrefetchScalarGridSpec(
            num_scalar_prefetch=1,
            grid=(1,),
            in_specs=[whole(array) for array in [planes, pairs]],
            out_specs=[pl.BlockSpec(shape, lambda i, place: (0, 0)) for shape in shapes],
        ),
        out_shape=[jax.ShapeDtypeStruct(shape, jnp.bfloat16) for shape in shapes],
        compiler_params=pltpu.CompilerParams(vmem_limit_bytes=VMEM_LIMIT),
        name="whiten",
    )(place[None], planes, pairs)
    return list(outs[:parts]), list(outs[parts:])


def table_kernel(first_ref, hi_cos_ref, hi_sin_ref, mid_cos_ref, mid_sin_ref, lo_cos_ref, lo_sin_ref, out_ref, cos, sin):
    s = pl.program_id(0)
    few = lo_cos_ref.shape[0]

    @pl.when(s == 0)
    def combine():
        lo_cos = lo_cos_ref[...]
        lo_sin = lo_sin_ref[...]
        for i in range(LANES // few):
            mid_cos = mid_cos_ref[i : i + 1]
            mid_sin = mid_sin_ref[i : i + 1]
            cos[i * few : (i + 1) * few] = mid_cos * lo_cos - mid_sin * lo_sin
            sin[i * few : (i + 1) * few] = mid_sin * lo_cos + mid_cos * lo_sin

    hi_cos = hi_cos_ref[pl.ds(s, 1), :]
    hi_sin = hi_sin_ref[pl.ds(s, 1), :]
    minus_cos = -hi_cos
    for i in range(0, LANES, 16):
        lo_cos = cos[i : i + 16]
        lo_sin = sin[i : i + 16]
        out_ref[i : i + 16, :HALF] = (hi_cos * lo_cos - hi_sin * lo_sin).astype(jnp.bfloat16)
        out_ref[i : i + 16, HALF:] = (minus_cos * lo_sin - hi_sin * lo_cos).astype(jnp.bfloat16)

    @pl.when(jnp.logical_and(first_ref[0] == 0, s == 0))
    def zero_bin():
        row = lax.broadcasted_iota(jnp.int32, (16, HALF), 0)
        weight = jnp.where(row == 0, 0.5, 1.0)
        out_ref[0:16, :HALF] = ((hi_cos * cos[0:16] - hi_sin * sin[0:16]) * weight).astype(jnp.bfloat16)


def tables(place, chunks):
    lag = jnp.arange(HALF, dtype=jnp.int32)
    few = 8
    middle = LANES // few
    bins = jnp.concatenate([
        (place * chunks + jnp.arange(chunks, dtype=jnp.int32)) * LANES,
        jnp.arange(middle, dtype=jnp.int32) * few,
        jnp.arange(few, dtype=jnp.int32),
    ])
    phase = bins[:, None] * lag[None, :] % (2 * F)
    angle = phase.astype(jnp.float32) * (jnp.pi / F)
    cos = jnp.cos(angle)
    sin = jnp.sin(angle)
    unit = 2.0 / jnp.sqrt(jnp.float32(F))
    cuts = [slice(0, chunks), slice(chunks, chunks + middle), slice(chunks + middle, None)]
    operands = [cos[cuts[0]] * unit, sin[cuts[0]] * unit, cos[cuts[1]], sin[cuts[1]], cos[cuts[2]], sin[cuts[2]]]
    return pl.pallas_call(
        table_kernel,
        grid_spec=pltpu.PrefetchScalarGridSpec(
            num_scalar_prefetch=1,
            grid=(chunks,),
            in_specs=[pl.BlockSpec(array.shape, lambda s, first: (0, 0)) for array in operands],
            out_specs=pl.BlockSpec((LANES, LAGS), lambda s, first: (s, 0)),
            scratch_shapes=[pltpu.VMEM((LANES, HALF), jnp.float32)] * 2,
        ),
        out_shape=jax.ShapeDtypeStruct((chunks * LANES, LAGS), jnp.bfloat16),
        cost_estimate=pl.CostEstimate(
            flops=chunks * LANES * LAGS * 4, bytes_accessed=chunks * LANES * LAGS * 2, transcendentals=0
        ),
        compiler_params=pltpu.CompilerParams(vmem_limit_bytes=VMEM_LIMIT),
        name="tables",
    )(place[None], *operands)


def iota(shape, axis):
    return lax.broadcasted_iota(jnp.int32, shape, axis)


def ones(hit):
    return hit.astype(jnp.float32).astype(jnp.bfloat16)


def choose_rows(lists, place, packed, rows_ref):
    height = rows_ref.shape[1]
    count = rows_ref.shape[0] // (2 * BLK * WINDOWS)
    deep = packed.shape[0] // lists
    blocks = deep // (BLK * WINDOWS)
    line = iota((count, 1), 0)
    group = jnp.zeros_like(line)
    for z in range(1, lists):
        group = group + jnp.where(line >= z * NB_SRC, 1, 0)
    here = iota((count, LANES), 1) == line - group * NB_SRC

    def column(kind):
        row = ones(iota((count, packed.shape[0]), 1) == group * deep + kind)
        found = jnp.dot(row, packed, preferred_element_type=jnp.float32)
        return jnp.sum(jnp.where(here, found, 0.0), axis=1, keepdims=True).astype(jnp.int32)

    across = iota((count, height), 1)
    picks = []
    for block in (column(0), column(1)):
        first = jnp.bitwise_xor(block, place * blocks) * (BLK * WINDOWS)
        for offset in range(BLK * WINDOWS):
            picks.append((across == first + offset).astype(jnp.float32))
    rows_ref[...] = jnp.concatenate(picks, axis=0).astype(jnp.bfloat16)


def corr_kernel(per_step, parts, lists, wave, place, *refs):
    panel_refs, (table_ref, ends_ref), refs = refs[:parts], refs[parts : parts + 2], refs[parts + 2 :]
    step = pl.program_id(0)
    if wave:
        (total_in, edge_in, rows_ref), out_refs, (total, edge) = refs[:3], refs[3:-2], refs[-2:]
    else:
        note_refs, (total, edge, rows_ref) = refs[:lists], refs[lists:]

        @pl.when(step == 0)
        def prepare():
            choose_rows(lists, place[0], jnp.concatenate([ref[...] for ref in note_refs]), rows_ref)

    count = total.shape[0] // PAIRS
    panel = jnp.concatenate([ref[...] for ref in panel_refs])
    chosen = jnp.dot(rows_ref[...], panel, preferred_element_type=jnp.float32)

    def row(side, channel, window, start):
        first = ((side * BLK + channel) * WINDOWS + window) * count
        return chosen[first : first + count, start : start + LANES]

    reals = []
    imags = []
    lane = iota((1, LANES), 1)
    first_bin = jnp.logical_and(jnp.logical_and(place[0] == 0, step == 0), lane == 0)
    edge_part = 0.0
    for i in range(per_step):
        at = i * 2 * LANES
        real = []
        imag = []
        for p in range(BLK):
            for q in range(BLK):
                re = 0.0
                im = 0.0
                for w in range(WINDOWS):
                    ra, ia = row(0, p, w, at), row(0, p, w, at + LANES)
                    rb, ib = row(1, q, w, at), row(1, q, w, at + LANES)
                    re = re + (ra * rb + ia * ib)
                    im = im + (ia * rb - ra * ib)
                real.append(re * (1.0 / WINDOWS))
                imag.append(im * (1.0 / WINDOWS))
        real = jnp.concatenate(real, axis=0)
        imag = jnp.concatenate(imag, axis=0)
        ends = ends_ref[0:1]
        if i == 0 and wave == 0:
            ends = jnp.where(first_bin, 0.5 * ends, ends)
        edge_part = edge_part + (real * ends + imag * ends_ref[1:2])
        reals.append(real.astype(jnp.bfloat16))
        imags.append(imag.astype(jnp.bfloat16))

    def transform(pieces, columns):
        rows = jnp.concatenate(pieces, axis=1)
        return jnp.dot(rows, table_ref[:, columns], preferred_element_type=jnp.float32)

    even = transform(reals, slice(0, HALF))
    odd = transform(imags, slice(HALF, LAGS))

    @pl.when(step == 0)
    def start():
        total[:, :HALF] = total_in[:, :HALF] + even if wave else even
        total[:, HALF:] = total_in[:, HALF:] + odd if wave else odd
        edge[...] = edge_in[...] + edge_part if wave else edge_part

    @pl.when(step > 0)
    def add():
        total[:, :HALF] += even
        total[:, HALF:] += odd
        edge[...] += edge_part

    if wave < WAVES - 1:
        return

    @pl.when(step == pl.num_programs(0) - 1)
    def finish():
        even = total[:, :HALF]
        odd = total[:, HALF:]
        later = (even + odd).astype(jnp.bfloat16)
        mirror = ones(iota((HALF, HALF), 0) + iota((HALF, HALF), 1) == HALF)
        sooner = jnp.dot((even - odd).astype(jnp.bfloat16), mirror, preferred_element_type=jnp.float32)
        least = jnp.sum(edge[...], axis=1, keepdims=True)
        sooner = jnp.where(iota(sooner.shape, 1) == 0, least, sooner).astype(jnp.bfloat16)
        each = NB_SRC * PAIRS
        shape = (each * len(out_refs), PAIRS * count)
        column = iota(shape, 1)
        number = column * PAIRS
        for n in range(1, PAIRS):
            number = number - jnp.where(column >= n * count, count * PAIRS - 1, 0)
        order = ones(iota(shape, 0) == number)
        both = jnp.concatenate([sooner, later], axis=1)
        rows = jnp.dot(order, both, preferred_element_type=jnp.float32)
        for i, out_ref in enumerate(out_refs):
            out_ref[...] = rows[i * each : (i + 1) * each].astype(jnp.bfloat16)


def correlate(panels, table, place, parts, wanted, wave, before):
    per_step = 4
    span = per_step * 2 * LANES
    rows = panels[0].shape[0]
    steps = 2 * table.shape[0] // span // WAVES
    lists = len(wanted)
    count = -(-lists * NB_SRC // 8) * 8
    each = NB_SRC * PAIRS
    turn = np.arange(LANES) * (np.pi / 16)
    ends = np.stack([np.cos(turn), np.sin(turn)]) * (2.0 / np.sqrt(F))
    sums = [
        jax.ShapeDtypeStruct((count * PAIRS, LAGS), jnp.float32),
        jax.ShapeDtypeStruct((count * PAIRS, LANES), jnp.float32),
    ]
    chosen = jax.ShapeDtypeStruct((2 * BLK * WINDOWS * count, rows * parts), jnp.bfloat16)
    whole = lambda array: pl.BlockSpec(array.shape, lambda i, place: (0, 0))
    if wave:
        extra = before
        extra_specs = [whole(array) for array in before]
        outs = [jax.ShapeDtypeStruct((each, LAGS), jnp.bfloat16)] * lists
        scratch = [pltpu.VMEM(array.shape, array.dtype) for array in sums]
    else:
        extra = [panels[d] for d in wanted]
        extra_specs = [pl.BlockSpec((rows, LANES), lambda i, place: (0, steps * span // LANES))] * lists
        outs = [*sums, chosen]
        scratch = []
    return pl.pallas_call(
        functools.partial(corr_kernel, per_step, parts, lists, wave),
        grid_spec=pltpu.PrefetchScalarGridSpec(
            num_scalar_prefetch=1,
            grid=(steps,),
            in_specs=[
                *[pl.BlockSpec((rows, span), lambda i, place: (0, i))] * parts,
                pl.BlockSpec((span // 2, LAGS), lambda i, place: (i + wave * steps, 0)),
                pl.BlockSpec((2, LANES), lambda i, place: (0, 0)),
                *extra_specs,
            ],
            out_specs=[whole(array) for array in outs],
            scratch_shapes=scratch,
        ),
        out_shape=outs,
        compiler_params=pltpu.CompilerParams(vmem_limit_bytes=VMEM_LIMIT),
        cost_estimate=pl.CostEstimate(
            flops=count * PAIRS * steps * span * LAGS,
            bytes_accessed=steps * span * LAGS,
            transcendentals=0,
        ),
        name="correlate",
    )(place[None], *panels, table, jnp.asarray(ends, jnp.float32), *extra)


def settle_kernel(groups, mine_ref, owners_ref, *refs):
    part_refs, out_refs = refs[:-groups], refs[-groups:]
    rows = groups * ROOM * PAIRS
    slots = rows // PAIRS
    each = NB_SRC * PAIRS
    tall = 24
    spare = jnp.full((1, LANES - NB_SRC), rows, jnp.int32)
    owner = jnp.concatenate([owners_ref[...], spare], axis=1)
    wide = jnp.broadcast_to(owner, (tall, LANES)).astype(jnp.float32)
    line, lane = iota((tall, LANES), 0), iota((tall, LANES), 1)
    other = jnp.sum(jnp.where(line == lane, wide, 0.0), axis=1, keepdims=True)
    earlier = jnp.logical_and(other == wide, line < lane).astype(jnp.float32)
    rank = jnp.sum(earlier, axis=0, keepdims=True)
    slot = jnp.bitwise_xor(owner, mine_ref[0]).astype(jnp.float32) * ROOM + rank
    held = ones(iota((slots, LANES), 0).astype(jnp.float32) == slot)
    down = ones(lax.shift_right_logical(iota((rows, slots), 0), 2) == iota((rows, slots), 1))
    over = ones(lax.shift_right_logical(iota((LANES, each), 1), 2) == iota((LANES, each), 0))
    block = jnp.dot(down, held, preferred_element_type=jnp.float32).astype(jnp.bfloat16)
    block = jnp.dot(block, over, preferred_element_type=jnp.float32)
    same = jnp.bitwise_and(iota((rows, each), 0), PAIRS - 1) == jnp.bitwise_and(iota((rows, each), 1), PAIRS - 1)
    chosen = jnp.where(same, block, 0.0).astype(jnp.bfloat16)
    total = sum(ref[...].astype(jnp.float32) for ref in part_refs)
    placed = jnp.dot(chosen, total.astype(jnp.bfloat16), preferred_element_type=jnp.float32)
    deep = ROOM * PAIRS
    for m, out_ref in enumerate(out_refs):
        out_ref[...] = placed[m * deep : (m + 1) * deep].astype(jnp.bfloat16)


def settle(owners, partials, mine, groups):
    whole = lambda array: pl.BlockSpec(array.shape, lambda i, mine: (0, 0))
    outs = [jax.ShapeDtypeStruct((ROOM * PAIRS, LAGS), jnp.bfloat16)] * groups
    return list(pl.pallas_call(
        functools.partial(settle_kernel, groups),
        grid_spec=pltpu.PrefetchScalarGridSpec(
            num_scalar_prefetch=1,
            grid=(1,),
            in_specs=[whole(array) for array in [owners, *partials]],
            out_specs=[whole(array) for array in outs],
        ),
        out_shape=outs,
        compiler_params=pltpu.CompilerParams(vmem_limit_bytes=VMEM_LIMIT),
        name="settle",
    )(mine[None], owners, *partials))


def widen_kernel(mine_ref, *refs):
    part_refs, out_ref = refs[:-1], refs[-1]
    for m, part_ref in enumerate(part_refs):
        values = part_ref[...].astype(jnp.float32)
        first = jnp.bitwise_xor(mine_ref[0], m) * MOST
        for r in range(MOST):
            out_ref[first + r] = values[r * PAIRS : (r + 1) * PAIRS]


def widen(pieces, mine):
    shape = (len(pieces) * MOST, PAIRS, LAGS)
    return pl.pallas_call(
        widen_kernel,
        grid_spec=pltpu.PrefetchScalarGridSpec(
            num_scalar_prefetch=1,
            grid=(1,),
            in_specs=[pl.BlockSpec(array.shape, lambda i, mine: (0, 0)) for array in pieces],
            out_specs=pl.BlockSpec(shape, lambda i, mine: (0, 0, 0)),
        ),
        out_shape=jax.ShapeDtypeStruct(shape, jnp.float32),
        compiler_params=pltpu.CompilerParams(vmem_limit_bytes=VMEM_LIMIT),
        name="widen",
    )(mine[None], *pieces)


def local(spectra, pair_blocks, owners):
    groups = lax.axis_size("grp")
    parts = lax.axis_size("chan")
    place = lax.axis_index("chan")
    chunks = F // LANES // parts

    def swap(array, d):
        return lax.ppermute(array, "chan", [(i, i ^ d) for i in range(parts)])

    def exchange(panels):
        moved = {d: swap(panels[d], d) for d in reversed(range(1, parts))}
        return panels[:1] + [moved[d] for d in range(1, parts)]

    first, second = whiten(spectra, pair_blocks[0, 0].T, place, parts)
    first = exchange(first)
    table = tables(place, chunks)
    table, second = lax.optimization_barrier((table, second))
    second = exchange(second)

    order = list(reversed(range(parts)))
    halves = (order[: parts // 2], order[parts // 2 :])
    sums = [correlate(first, table, place, parts, wanted, 0, None) for wanted in halves]
    second, sums = lax.optimization_barrier((second, sums))
    partials = []
    for wanted, before in zip(halves, sums):
        for d, rows in zip(wanted, correlate(second, table, place, parts, wanted, 1, before)):
            partials.append(swap(rows, d) if d else rows)
    mine = lax.axis_index("grp")
    pieces = settle(owners[0, 0].T, partials, mine, groups)
    for m in reversed(range(1, groups)):
        pieces[m] = lax.ppermute(pieces[m], "grp", [(i, i ^ m) for i in range(groups)])
    return widen(pieces, mine)[None, None]


def solution(mesh):
    return jax.shard_map(
        local,
        mesh=mesh,
        in_specs=(
            P(("grp", "chan"), None, None, None),
            P("grp", "chan", None, None),
            P("grp", "chan", None, None),
        ),
        out_specs=P("grp", "chan", None, None, None),
        check_vma=False,
    )
```

```python
import functools

import jax
import jax.numpy as jnp
import numpy as np
from jax import lax
from jax.experimental import pallas as pl
from jax.experimental.pallas import tpu as pltpu
from jax.sharding import PartitionSpec as P

F = 8192
LAGS = 1024
BLK = 2
NB_SRC = 18
MOST = 3
WINDOWS = 2
LANES = 128
PAIRS = BLK * BLK
VMEM_LIMIT = 24 * 1024 * 1024
HALF = LAGS // 2
ROOM = 4
WAVES = 2


def whiten_kernel(parts, place_ref, spec_ref, pairs_ref, *out_refs):
    blocks = F // LANES
    each = blocks // parts
    share = each // WAVES
    place = place_ref[0]

    def values(start):
        span = pl.ds(start, LANES)
        re = spec_ref[0, :, span].astype(jnp.float32)
        im = spec_ref[1, :, span].astype(jnp.float32)
        return re, im, re * re + im * im

    shape = (spec_ref.shape[1], LANES)
    line = lax.broadcasted_iota(jnp.int32, shape, 0)
    spare = jnp.zeros((1, LANES - NB_SRC), jnp.int32)
    wide = lambda row: jnp.broadcast_to(jnp.concatenate([row, spare], axis=1), shape)
    notes = jnp.where(line == 0, wide(pairs_ref[0:1]), wide(pairs_ref[1:2]))
    notes = notes.astype(jnp.float32).astype(jnp.bfloat16)
    for out_ref in out_refs[:parts]:
        out_ref[:, share * 2 * LANES :] = notes
    sums = [None] * 4
    for k in range(blocks):
        power = values(k * LANES)[2]
        sums[k % 4] = power if k < 4 else sums[k % 4] + power
    total = jnp.sum((sums[0] + sums[1]) + (sums[2] + sums[3]), axis=1, keepdims=True)
    level = 0.1 * (total * (1.0 / F) + 1e-05)
    for index, out_ref in enumerate(out_refs):
        first = jnp.bitwise_xor(place, index % parts) * each + index // parts * share
        for k in range(share):
            re, im, power = values(pl.multiple_of((first + k) * LANES, LANES))
            scale = lax.rsqrt(power + level)
            at = k * 2 * LANES
            out_ref[:, at : at + LANES] = (re * scale).astype(jnp.bfloat16)
            out_ref[:, at + LANES : at + 2 * LANES] = (im * scale).astype(jnp.bfloat16)


def whiten(spectra, pairs, place, parts):
    rows = spectra.shape[0] * WINDOWS
    planes = jnp.transpose(spectra.reshape(rows, 2, F), (1, 0, 2))
    width = 2 * F // parts // WAVES
    shapes = [(rows, width + LANES)] * parts + [(rows, width)] * parts * (WAVES - 1)
    whole = lambda array: pl.BlockSpec(array.shape, lambda i, place: (0,) * array.ndim)
    outs = pl.pallas_call(
        functools.partial(whiten_kernel, parts),
        grid_spec=pltpu.PrefetchScalarGridSpec(
            num_scalar_prefetch=1,
            grid=(1,),
            in_specs=[whole(array) for array in [planes, pairs]],
            out_specs=[pl.BlockSpec(shape, lambda i, place: (0, 0)) for shape in shapes],
        ),
        out_shape=[jax.ShapeDtypeStruct(shape, jnp.bfloat16) for shape in shapes],
        compiler_params=pltpu.CompilerParams(vmem_limit_bytes=VMEM_LIMIT),
        name="whiten",
    )(place[None], planes, pairs)
    return list(outs[:parts]), list(outs[parts:])


def table_kernel(first_ref, hi_cos_ref, hi_sin_ref, mid_cos_ref, mid_sin_ref, lo_cos_ref, lo_sin_ref, out_ref, cos, sin):
    s = pl.program_id(0)
    few = lo_cos_ref.shape[0]

    @pl.when(s == 0)
    def combine():
        lo_cos = lo_cos_ref[...]
        lo_sin = lo_sin_ref[...]
        for i in range(LANES // few):
            mid_cos = mid_cos_ref[i : i + 1]
            mid_sin = mid_sin_ref[i : i + 1]
            cos[i * few : (i + 1) * few] = mid_cos * lo_cos - mid_sin * lo_sin
            sin[i * few : (i + 1) * few] = mid_sin * lo_cos + mid_cos * lo_sin

    hi_cos = hi_cos_ref[pl.ds(s, 1), :]
    hi_sin = hi_sin_ref[pl.ds(s, 1), :]
    minus_cos = -hi_cos
    for i in range(0, LANES, 16):
        lo_cos = cos[i : i + 16]
        lo_sin = sin[i : i + 16]
        out_ref[i : i + 16, :HALF] = (hi_cos * lo_cos - hi_sin * lo_sin).astype(jnp.bfloat16)
        out_ref[i : i + 16, HALF:] = (minus_cos * lo_sin - hi_sin * lo_cos).astype(jnp.bfloat16)

    @pl.when(jnp.logical_and(first_ref[0] == 0, s == 0))
    def zero_bin():
        row = lax.broadcasted_iota(jnp.int32, (16, HALF), 0)
        weight = jnp.where(row == 0, 0.5, 1.0)
        out_ref[0:16, :HALF] = ((hi_cos * cos[0:16] - hi_sin * sin[0:16]) * weight).astype(jnp.bfloat16)


def tables(place, chunks):
    lag = jnp.arange(HALF, dtype=jnp.int32)
    few = 8
    middle = LANES // few
    bins = jnp.concatenate([
        (place * chunks + jnp.arange(chunks, dtype=jnp.int32)) * LANES,
        jnp.arange(middle, dtype=jnp.int32) * few,
        jnp.arange(few, dtype=jnp.int32),
    ])
    phase = bins[:, None] * lag[None, :] % (2 * F)
    angle = phase.astype(jnp.float32) * (jnp.pi / F)
    cos = jnp.cos(angle)
    sin = jnp.sin(angle)
    unit = 2.0 / jnp.sqrt(jnp.float32(F))
    cuts = [slice(0, chunks), slice(chunks, chunks + middle), slice(chunks + middle, None)]
    operands = [cos[cuts[0]] * unit, sin[cuts[0]] * unit, cos[cuts[1]], sin[cuts[1]], cos[cuts[2]], sin[cuts[2]]]
    return pl.pallas_call(
        table_kernel,
        grid_spec=pltpu.PrefetchScalarGridSpec(
            num_scalar_prefetch=1,
            grid=(chunks,),
            in_specs=[pl.BlockSpec(array.shape, lambda s, first: (0, 0)) for array in operands],
            out_specs=pl.BlockSpec((LANES, LAGS), lambda s, first: (s, 0)),
            scratch_shapes=[pltpu.VMEM((LANES, HALF), jnp.float32)] * 2,
        ),
        out_shape=jax.ShapeDtypeStruct((chunks * LANES, LAGS), jnp.bfloat16),
        cost_estimate=pl.CostEstimate(
            flops=chunks * LANES * LAGS * 4, bytes_accessed=chunks * LANES * LAGS * 2, transcendentals=0
        ),
        compiler_params=pltpu.CompilerParams(vmem_limit_bytes=VMEM_LIMIT),
        name="tables",
    )(place[None], *operands)


def iota(shape, axis):
    return lax.broadcasted_iota(jnp.int32, shape, axis)


def ones(hit):
    return hit.astype(jnp.float32).astype(jnp.bfloat16)


def choose_rows(lists, place, packed, rows_ref):
    height = rows_ref.shape[1]
    count = rows_ref.shape[0] // (2 * BLK * WINDOWS)
    deep = packed.shape[0] // lists
    blocks = deep // (BLK * WINDOWS)
    line = iota((count, 1), 0)
    group = jnp.zeros_like(line)
    for z in range(1, lists):
        group = group + jnp.where(line >= z * NB_SRC, 1, 0)
    here = iota((count, LANES), 1) == line - group * NB_SRC

    def column(kind):
        row = ones(iota((count, packed.shape[0]), 1) == group * deep + kind)
        found = jnp.dot(row, packed, preferred_element_type=jnp.float32)
        return jnp.sum(jnp.where(here, found, 0.0), axis=1, keepdims=True).astype(jnp.int32)

    across = iota((count, height), 1)
    picks = []
    for block in (column(0), column(1)):
        first = jnp.bitwise_xor(block, place * blocks) * (BLK * WINDOWS)
        for offset in range(BLK * WINDOWS):
            picks.append((across == first + offset).astype(jnp.float32))
    rows_ref[...] = jnp.concatenate(picks, axis=0).astype(jnp.bfloat16)


def corr_kernel(per_step, parts, lists, wave, place, *refs):
    panel_refs, (table_ref, ends_ref), refs = refs[:parts], refs[parts : parts + 2], refs[parts + 2 :]
    step = pl.program_id(0)
    if wave:
        (total_in, edge_in, rows_ref), out_refs, (total, edge) = refs[:3], refs[3:-2], refs[-2:]
    else:
        note_refs, (total, edge, rows_ref) = refs[:lists], refs[lists:]

        @pl.when(step == 0)
        def prepare():
            choose_rows(lists, place[0], jnp.concatenate([ref[...] for ref in note_refs]), rows_ref)

    count = total.shape[0] // PAIRS
    panel = jnp.concatenate([ref[...] for ref in panel_refs])
    chosen = jnp.dot(rows_ref[...], panel, preferred_element_type=jnp.float32)

    def row(side, channel, window, start):
        first = ((side * BLK + channel) * WINDOWS + window) * count
        return chosen[first : first + count, start : start + LANES]

    reals = []
    imags = []
    lane = iota((1, LANES), 1)
    first_bin = jnp.logical_and(jnp.logical_and(place[0] == 0, step == 0), lane == 0)
    edge_part = 0.0
    for i in range(per_step):
        at = i * 2 * LANES
        real = []
        imag = []
        for p in range(BLK):
            for q in range(BLK):
                re = 0.0
                im = 0.0
                for w in range(WINDOWS):
                    ra, ia = row(0, p, w, at), row(0, p, w, at + LANES)
                    rb, ib = row(1, q, w, at), row(1, q, w, at + LANES)
                    re = re + (ra * rb + ia * ib)
                    im = im + (ia * rb - ra * ib)
                real.append(re * (1.0 / WINDOWS))
                imag.append(im * (1.0 / WINDOWS))
        real = jnp.concatenate(real, axis=0)
        imag = jnp.concatenate(imag, axis=0)
        ends = ends_ref[0:1]
        if i == 0 and wave == 0:
            ends = jnp.where(first_bin, 0.5 * ends, ends)
        edge_part = edge_part + (real * ends + imag * ends_ref[1:2])
        reals.append(real.astype(jnp.bfloat16))
        imags.append(imag.astype(jnp.bfloat16))

    def transform(pieces, columns):
        rows = jnp.concatenate(pieces, axis=1)
        return jnp.dot(rows, table_ref[:, columns], preferred_element_type=jnp.float32)

    even = transform(reals, slice(0, HALF))
    odd = transform(imags, slice(HALF, LAGS))

    @pl.when(step == 0)
    def start():
        total[:, :HALF] = total_in[:, :HALF] + even if wave else even
        total[:, HALF:] = total_in[:, HALF:] + odd if wave else odd
        edge[...] = edge_in[...] + edge_part if wave else edge_part

    @pl.when(step > 0)
    def add():
        total[:, :HALF] += even
        total[:, HALF:] += odd
        edge[...] += edge_part

    if wave < WAVES - 1:
        return

    @pl.when(step == pl.num_programs(0) - 1)
    def finish():
        even = total[:, :HALF]
        odd = total[:, HALF:]
        later = (even + odd).astype(jnp.bfloat16)
        mirror = ones(iota((HALF, HALF), 0) + iota((HALF, HALF), 1) == HALF)
        sooner = jnp.dot((even - odd).astype(jnp.bfloat16), mirror, preferred_element_type=jnp.float32)
        least = jnp.sum(edge[...], axis=1, keepdims=True)
        sooner = jnp.where(iota(sooner.shape, 1) == 0, least, sooner).astype(jnp.bfloat16)
        each = NB_SRC * PAIRS
        shape = (each * len(out_refs), PAIRS * count)
        column = iota(shape, 1)
        number = column * PAIRS
        for n in range(1, PAIRS):
            number = number - jnp.where(column >= n * count, count * PAIRS - 1, 0)
        order = ones(iota(shape, 0) == number)
        both = jnp.concatenate([sooner, later], axis=1)
        rows = jnp.dot(order, both, preferred_element_type=jnp.float32)
        for i, out_ref in enumerate(out_refs):
            out_ref[...] = rows[i * each : (i + 1) * each].astype(jnp.bfloat16)


def correlate(panels, table, place, parts, wanted, wave, before):
    per_step = 4
    span = per_step * 2 * LANES
    rows = panels[0].shape[0]
    steps = 2 * table.shape[0] // span // WAVES
    lists = len(wanted)
    count = -(-lists * NB_SRC // 8) * 8
    each = NB_SRC * PAIRS
    turn = np.arange(LANES) * (np.pi / 16)
    ends = np.stack([np.cos(turn), np.sin(turn)]) * (2.0 / np.sqrt(F))
    sums = [
        jax.ShapeDtypeStruct((count * PAIRS, LAGS), jnp.float32),
        jax.ShapeDtypeStruct((count * PAIRS, LANES), jnp.float32),
    ]
    chosen = jax.ShapeDtypeStruct((2 * BLK * WINDOWS * count, rows * parts), jnp.bfloat16)
    whole = lambda array: pl.BlockSpec(array.shape, lambda i, place: (0, 0))
    if wave:
        extra = before
        extra_specs = [whole(array) for array in before]
        outs = [jax.ShapeDtypeStruct((each, LAGS), jnp.bfloat16)] * lists
        scratch = [pltpu.VMEM(array.shape, array.dtype) for array in sums]
    else:
        extra = [panels[d] for d in wanted]
        extra_specs = [pl.BlockSpec((rows, LANES), lambda i, place: (0, steps * span // LANES))] * lists
        outs = [*sums, chosen]
        scratch = []
    return pl.pallas_call(
        functools.partial(corr_kernel, per_step, parts, lists, wave),
        grid_spec=pltpu.PrefetchScalarGridSpec(
            num_scalar_prefetch=1,
            grid=(steps,),
            in_specs=[
                *[pl.BlockSpec((rows, span), lambda i, place: (0, i))] * parts,
                pl.BlockSpec((span // 2, LAGS), lambda i, place: (i + wave * steps, 0)),
                pl.BlockSpec((2, LANES), lambda i, place: (0, 0)),
                *extra_specs,
            ],
            out_specs=[whole(array) for array in outs],
            scratch_shapes=scratch,
        ),
        out_shape=outs,
        compiler_params=pltpu.CompilerParams(vmem_limit_bytes=VMEM_LIMIT),
        cost_estimate=pl.CostEstimate(
            flops=count * PAIRS * steps * span * LAGS,
            bytes_accessed=steps * span * LAGS,
            transcendentals=0,
        ),
        name="correlate",
    )(place[None], *panels, table, jnp.asarray(ends, jnp.float32), *extra)


def settle_kernel(groups, mine_ref, owners_ref, *refs):
    part_refs, out_refs = refs[:-2], refs[-2:]
    rows = groups * ROOM * PAIRS
    slots = rows // PAIRS
    each = NB_SRC * PAIRS
    tall = 24
    spare = jnp.full((1, LANES - NB_SRC), rows, jnp.int32)
    owner = jnp.concatenate([owners_ref[...], spare], axis=1)
    wide = jnp.broadcast_to(owner, (tall, LANES)).astype(jnp.float32)
    line, lane = iota((tall, LANES), 0), iota((tall, LANES), 1)
    other = jnp.sum(jnp.where(line == lane, wide, 0.0), axis=1, keepdims=True)
    earlier = jnp.logical_and(other == wide, line < lane).astype(jnp.float32)
    rank = jnp.sum(earlier, axis=0, keepdims=True)
    turn = jnp.bitwise_xor(owner, mine_ref[0])
    block = lax.shift_right_logical(turn, 1) + jnp.bitwise_and(turn, 1) * (groups // 2)
    slot = jnp.where(owner < groups, block, rows).astype(jnp.float32) * ROOM + rank
    held = ones(iota((slots, LANES), 0).astype(jnp.float32) == slot)
    down = ones(lax.shift_right_logical(iota((rows, slots), 0), 2) == iota((rows, slots), 1))
    over = ones(lax.shift_right_logical(iota((LANES, each), 1), 2) == iota((LANES, each), 0))
    block = jnp.dot(down, held, preferred_element_type=jnp.float32).astype(jnp.bfloat16)
    block = jnp.dot(block, over, preferred_element_type=jnp.float32)
    same = jnp.bitwise_and(iota((rows, each), 0), PAIRS - 1) == jnp.bitwise_and(iota((rows, each), 1), PAIRS - 1)
    chosen = jnp.where(same, block, 0.0).astype(jnp.bfloat16)
    total = sum(ref[...].astype(jnp.float32) for ref in part_refs)
    placed = jnp.dot(chosen, total.astype(jnp.bfloat16), preferred_element_type=jnp.float32)
    for i, out_ref in enumerate(out_refs):
        out_ref[...] = placed[i * rows // 2 : (i + 1) * rows // 2].astype(jnp.bfloat16)


def settle(owners, partials, mine, groups):
    whole = lambda array: pl.BlockSpec(array.shape, lambda i, mine: (0, 0))
    outs = [jax.ShapeDtypeStruct((groups * ROOM * PAIRS // 2, LAGS), jnp.bfloat16)] * 2
    return list(pl.pallas_call(
        functools.partial(settle_kernel, groups),
        grid_spec=pltpu.PrefetchScalarGridSpec(
            num_scalar_prefetch=1,
            grid=(1,),
            in_specs=[whole(array) for array in [owners, *partials]],
            out_specs=[whole(array) for array in outs],
        ),
        out_shape=outs,
        compiler_params=pltpu.CompilerParams(vmem_limit_bytes=VMEM_LIMIT),
        name="settle",
    )(mine[None], owners, *partials))


def bundle_kernel(kept_ref, brought_ref, *out_refs):
    deep = ROOM * PAIRS
    for j, out_ref in enumerate(out_refs):
        out_ref[:deep] = kept_ref[j * deep : (j + 1) * deep]
        out_ref[deep:] = brought_ref[j * deep : (j + 1) * deep]


def bundle(kept, brought):
    count = kept.shape[0] // (ROOM * PAIRS)
    return list(pl.pallas_call(
        bundle_kernel,
        out_shape=[jax.ShapeDtypeStruct((2 * ROOM * PAIRS, LAGS), jnp.bfloat16)] * count,
        compiler_params=pltpu.CompilerParams(vmem_limit_bytes=VMEM_LIMIT),
        name="bundle",
    )(kept, brought))


def widen_kernel(mine_ref, *refs):
    part_refs, out_ref = refs[:-1], refs[-1]
    for j, part_ref in enumerate(part_refs):
        values = part_ref[...].astype(jnp.float32)
        for side in range(2):
            first = jnp.bitwise_xor(mine_ref[0], 2 * j + side) * MOST
            for r in range(MOST):
                at = (side * ROOM + r) * PAIRS
                out_ref[first + r] = values[at : at + PAIRS]


def widen(pieces, mine):
    shape = (2 * len(pieces) * MOST, PAIRS, LAGS)
    return pl.pallas_call(
        widen_kernel,
        grid_spec=pltpu.PrefetchScalarGridSpec(
            num_scalar_prefetch=1,
            grid=(1,),
            in_specs=[pl.BlockSpec(array.shape, lambda i, mine: (0, 0)) for array in pieces],
            out_specs=pl.BlockSpec(shape, lambda i, mine: (0, 0, 0)),
        ),
        out_shape=jax.ShapeDtypeStruct(shape, jnp.float32),
        compiler_params=pltpu.CompilerParams(vmem_limit_bytes=VMEM_LIMIT),
        name="widen",
    )(mine[None], *pieces)


def local(spectra, pair_blocks, owners):
    groups = lax.axis_size("grp")
    parts = lax.axis_size("chan")
    place = lax.axis_index("chan")
    chunks = F // LANES // parts

    def swap(array, d):
        return lax.ppermute(array, "chan", [(i, i ^ d) for i in range(parts)])

    def exchange(panels):
        order = list(reversed(range(1, parts)))
        order.insert(1, order.pop())
        moved = {d: swap(panels[d], d) for d in order}
        return panels[:1] + [moved[d] for d in range(1, parts)]

    first, second = whiten(spectra, pair_blocks[0, 0].T, place, parts)
    first = exchange(first)
    table = tables(place, chunks)
    table, second = lax.optimization_barrier((table, second))
    second = exchange(second)

    order = list(reversed(range(parts)))
    halves = (order[: parts // 2], order[parts // 2 :])
    sums = [correlate(first, table, place, parts, wanted, 0, None) for wanted in halves]
    second, sums = lax.optimization_barrier((second, sums))
    partials = []
    for wanted, before in zip(halves, sums):
        for d, rows in zip(wanted, correlate(second, table, place, parts, wanted, 1, before)):
            partials.append(swap(rows, d) if d else rows)
    mine = lax.axis_index("grp")

    def trade(array, m):
        return lax.ppermute(array, "grp", [(i, i ^ m) for i in range(groups)])

    kept, cross = settle(owners[0, 0].T, partials, mine, groups)
    pieces = bundle(kept, trade(cross, 1))
    for j in reversed(range(1, groups // 2)):
        pieces[j] = trade(pieces[j], 2 * j)
    return widen(pieces, mine)[None, None]


def solution(mesh):
    return jax.shard_map(
        local,
        mesh=mesh,
        in_specs=(
            P(("grp", "chan"), None, None, None),
            P("grp", "chan", None, None),
            P("grp", "chan", None, None),
        ),
        out_specs=P("grp", "chan", None, None, None),
        check_vma=False,
    )
```

```python
import functools

import jax
import jax.numpy as jnp
import numpy as np
from jax import lax
from jax.experimental import pallas as pl
from jax.experimental.pallas import tpu as pltpu
from jax.sharding import PartitionSpec as P

F = 8192
LAGS = 1024
BLK = 2
NB_SRC = 18
MOST = 3
WINDOWS = 2
LANES = 128
PAIRS = BLK * BLK
VMEM_LIMIT = 24 * 1024 * 1024
HALF = LAGS // 2
ROOM = 4
WAVES = 2
LATE = 4


def whiten_kernel(parts, place_ref, spec_ref, pairs_ref, *out_refs):
    blocks = F // LANES
    each = blocks // parts
    late = each // LATE
    place = place_ref[0]

    def values(start):
        span = pl.ds(start, LANES)
        re = spec_ref[0, :, span].astype(jnp.float32)
        im = spec_ref[1, :, span].astype(jnp.float32)
        return re, im, re * re + im * im

    shape = (spec_ref.shape[1], LANES)
    line = lax.broadcasted_iota(jnp.int32, shape, 0)
    spare = jnp.zeros((1, LANES - NB_SRC), jnp.int32)
    wide = lambda row: jnp.broadcast_to(jnp.concatenate([row, spare], axis=1), shape)
    notes = jnp.where(line == 0, wide(pairs_ref[0:1]), wide(pairs_ref[1:2]))
    notes = notes.astype(jnp.float32).astype(jnp.bfloat16)
    for out_ref in out_refs[:parts]:
        out_ref[:, (each - late) * 2 * LANES :] = notes
    sums = [None] * 4
    for k in range(blocks):
        power = values(k * LANES)[2]
        sums[k % 4] = power if k < 4 else sums[k % 4] + power
    total = jnp.sum((sums[0] + sums[1]) + (sums[2] + sums[3]), axis=1, keepdims=True)
    level = 0.1 * (total * (1.0 / F) + 1e-05)
    for index, out_ref in enumerate(out_refs):
        wave, d = divmod(index, parts)
        first = jnp.bitwise_xor(place, d) * each + wave * (each - late)
        for k in range(late if wave else each - late):
            re, im, power = values(pl.multiple_of((first + k) * LANES, LANES))
            scale = lax.rsqrt(power + level)
            at = k * 2 * LANES
            out_ref[:, at : at + LANES] = (re * scale).astype(jnp.bfloat16)
            out_ref[:, at + LANES : at + 2 * LANES] = (im * scale).astype(jnp.bfloat16)


def whiten(spectra, pairs, place, parts):
    rows = spectra.shape[0] * WINDOWS
    planes = jnp.transpose(spectra.reshape(rows, 2, F), (1, 0, 2))
    width = 2 * F // parts
    late = width // LATE
    shapes = [(rows, width - late + LANES)] * parts + [(rows, late)] * parts
    whole = lambda array: pl.BlockSpec(array.shape, lambda i, place: (0,) * array.ndim)
    outs = pl.pallas_call(
        functools.partial(whiten_kernel, parts),
        grid_spec=pltpu.PrefetchScalarGridSpec(
            num_scalar_prefetch=1,
            grid=(1,),
            in_specs=[whole(array) for array in [planes, pairs]],
            out_specs=[pl.BlockSpec(shape, lambda i, place: (0, 0)) for shape in shapes],
        ),
        out_shape=[jax.ShapeDtypeStruct(shape, jnp.bfloat16) for shape in shapes],
        compiler_params=pltpu.CompilerParams(vmem_limit_bytes=VMEM_LIMIT),
        name="whiten",
    )(place[None], planes, pairs)
    return list(outs[:parts]), list(outs[parts:])


def table_kernel(first_ref, hi_cos_ref, hi_sin_ref, mid_cos_ref, mid_sin_ref, lo_cos_ref, lo_sin_ref, out_ref, cos, sin):
    s = pl.program_id(0)
    few = lo_cos_ref.shape[0]

    @pl.when(s == 0)
    def combine():
        lo_cos = lo_cos_ref[...]
        lo_sin = lo_sin_ref[...]
        for i in range(LANES // few):
            mid_cos = mid_cos_ref[i : i + 1]
            mid_sin = mid_sin_ref[i : i + 1]
            cos[i * few : (i + 1) * few] = mid_cos * lo_cos - mid_sin * lo_sin
            sin[i * few : (i + 1) * few] = mid_sin * lo_cos + mid_cos * lo_sin

    hi_cos = hi_cos_ref[pl.ds(s, 1), :]
    hi_sin = hi_sin_ref[pl.ds(s, 1), :]
    minus_cos = -hi_cos
    for i in range(0, LANES, 16):
        lo_cos = cos[i : i + 16]
        lo_sin = sin[i : i + 16]
        out_ref[i : i + 16, :HALF] = (hi_cos * lo_cos - hi_sin * lo_sin).astype(jnp.bfloat16)
        out_ref[i : i + 16, HALF:] = (minus_cos * lo_sin - hi_sin * lo_cos).astype(jnp.bfloat16)

    @pl.when(jnp.logical_and(first_ref[0] == 0, s == 0))
    def zero_bin():
        row = lax.broadcasted_iota(jnp.int32, (16, HALF), 0)
        weight = jnp.where(row == 0, 0.5, 1.0)
        out_ref[0:16, :HALF] = ((hi_cos * cos[0:16] - hi_sin * sin[0:16]) * weight).astype(jnp.bfloat16)


def tables(place, chunks):
    lag = jnp.arange(HALF, dtype=jnp.int32)
    few = 8
    middle = LANES // few
    bins = jnp.concatenate([
        (place * chunks + jnp.arange(chunks, dtype=jnp.int32)) * LANES,
        jnp.arange(middle, dtype=jnp.int32) * few,
        jnp.arange(few, dtype=jnp.int32),
    ])
    phase = bins[:, None] * lag[None, :] % (2 * F)
    angle = phase.astype(jnp.float32) * (jnp.pi / F)
    cos = jnp.cos(angle)
    sin = jnp.sin(angle)
    unit = 2.0 / jnp.sqrt(jnp.float32(F))
    cuts = [slice(0, chunks), slice(chunks, chunks + middle), slice(chunks + middle, None)]
    operands = [cos[cuts[0]] * unit, sin[cuts[0]] * unit, cos[cuts[1]], sin[cuts[1]], cos[cuts[2]], sin[cuts[2]]]
    return pl.pallas_call(
        table_kernel,
        grid_spec=pltpu.PrefetchScalarGridSpec(
            num_scalar_prefetch=1,
            grid=(chunks,),
            in_specs=[pl.BlockSpec(array.shape, lambda s, first: (0, 0)) for array in operands],
            out_specs=pl.BlockSpec((LANES, LAGS), lambda s, first: (s, 0)),
            scratch_shapes=[pltpu.VMEM((LANES, HALF), jnp.float32)] * 2,
        ),
        out_shape=jax.ShapeDtypeStruct((chunks * LANES, LAGS), jnp.bfloat16),
        cost_estimate=pl.CostEstimate(
            flops=chunks * LANES * LAGS * 4, bytes_accessed=chunks * LANES * LAGS * 2, transcendentals=0
        ),
        compiler_params=pltpu.CompilerParams(vmem_limit_bytes=VMEM_LIMIT),
        name="tables",
    )(place[None], *operands)


def iota(shape, axis):
    return lax.broadcasted_iota(jnp.int32, shape, axis)


def ones(hit):
    return hit.astype(jnp.float32).astype(jnp.bfloat16)


def choose_rows(lists, place, packed, rows_ref):
    height = rows_ref.shape[1]
    count = rows_ref.shape[0] // (2 * BLK * WINDOWS)
    deep = packed.shape[0] // lists
    blocks = deep // (BLK * WINDOWS)
    line = iota((count, 1), 0)
    group = jnp.zeros_like(line)
    for z in range(1, lists):
        group = group + jnp.where(line >= z * NB_SRC, 1, 0)
    here = iota((count, LANES), 1) == line - group * NB_SRC

    def column(kind):
        row = ones(iota((count, packed.shape[0]), 1) == group * deep + kind)
        found = jnp.dot(row, packed, preferred_element_type=jnp.float32)
        return jnp.sum(jnp.where(here, found, 0.0), axis=1, keepdims=True).astype(jnp.int32)

    across = iota((count, height), 1)
    picks = []
    for block in (column(0), column(1)):
        first = jnp.bitwise_xor(block, place * blocks) * (BLK * WINDOWS)
        for offset in range(BLK * WINDOWS):
            picks.append((across == first + offset).astype(jnp.float32))
    rows_ref[...] = jnp.concatenate(picks, axis=0).astype(jnp.bfloat16)


def sequence(parts):
    order = list(reversed(range(parts)))
    return [order[0], order[-2], *order[1:-2], order[-1]]


def corr_kernel(per_step, parts, lists, wave, place, *refs):
    panel_refs, (table_ref, ends_ref), refs = dict(zip(sequence(parts), refs)), refs[parts : parts + 2], refs[parts + 2 :]
    step = pl.program_id(0)
    if wave:
        (total_in, edge_in, rows_ref), out_refs, (total, edge) = refs[:3], refs[3:-2], refs[-2:]
    else:
        note_refs, (total, edge, rows_ref) = refs[:lists], refs[lists:]

        @pl.when(step == 0)
        def prepare():
            choose_rows(lists, place[0], jnp.concatenate([ref[...] for ref in note_refs]), rows_ref)

    count = total.shape[0] // PAIRS
    panel = jnp.concatenate([panel_refs[d][...] for d in range(parts)])
    chosen = jnp.dot(rows_ref[...], panel, preferred_element_type=jnp.float32)

    def row(side, channel, window, start):
        first = ((side * BLK + channel) * WINDOWS + window) * count
        return chosen[first : first + count, start : start + LANES]

    reals = []
    imags = []
    lane = iota((1, LANES), 1)
    first_bin = jnp.logical_and(jnp.logical_and(place[0] == 0, step == 0), lane == 0)
    edge_part = 0.0
    for i in range(per_step):
        at = i * 2 * LANES
        real = []
        imag = []
        for p in range(BLK):
            for q in range(BLK):
                re = 0.0
                im = 0.0
                for w in range(WINDOWS):
                    ra, ia = row(0, p, w, at), row(0, p, w, at + LANES)
                    rb, ib = row(1, q, w, at), row(1, q, w, at + LANES)
                    re = re + (ra * rb + ia * ib)
                    im = im + (ia * rb - ra * ib)
                real.append(re * (1.0 / WINDOWS))
                imag.append(im * (1.0 / WINDOWS))
        real = jnp.concatenate(real, axis=0)
        imag = jnp.concatenate(imag, axis=0)
        ends = ends_ref[0:1]
        if i == 0 and wave == 0:
            ends = jnp.where(first_bin, 0.5 * ends, ends)
        edge_part = edge_part + (real * ends + imag * ends_ref[1:2])
        reals.append(real.astype(jnp.bfloat16))
        imags.append(imag.astype(jnp.bfloat16))

    def transform(pieces, columns):
        rows = jnp.concatenate(pieces, axis=1)
        return jnp.dot(rows, table_ref[:, columns], preferred_element_type=jnp.float32)

    even = transform(reals, slice(0, HALF))
    odd = transform(imags, slice(HALF, LAGS))

    @pl.when(step == 0)
    def start():
        total[:, :HALF] = total_in[:, :HALF] + even if wave else even
        total[:, HALF:] = total_in[:, HALF:] + odd if wave else odd
        edge[...] = edge_in[...] + edge_part if wave else edge_part

    @pl.when(step > 0)
    def add():
        total[:, :HALF] += even
        total[:, HALF:] += odd
        edge[...] += edge_part

    if wave < WAVES - 1:
        return

    @pl.when(step == pl.num_programs(0) - 1)
    def finish():
        even = total[:, :HALF]
        odd = total[:, HALF:]
        later = (even + odd).astype(jnp.bfloat16)
        mirror = ones(iota((HALF, HALF), 0) + iota((HALF, HALF), 1) == HALF)
        sooner = jnp.dot((even - odd).astype(jnp.bfloat16), mirror, preferred_element_type=jnp.float32)
        least = jnp.sum(edge[...], axis=1, keepdims=True)
        sooner = jnp.where(iota(sooner.shape, 1) == 0, least, sooner).astype(jnp.bfloat16)
        each = NB_SRC * PAIRS
        shape = (each * len(out_refs), PAIRS * count)
        column = iota(shape, 1)
        number = column * PAIRS
        for n in range(1, PAIRS):
            number = number - jnp.where(column >= n * count, count * PAIRS - 1, 0)
        order = ones(iota(shape, 0) == number)
        both = jnp.concatenate([sooner, later], axis=1)
        rows = jnp.dot(order, both, preferred_element_type=jnp.float32)
        for i, out_ref in enumerate(out_refs):
            out_ref[...] = rows[i * each : (i + 1) * each].astype(jnp.bfloat16)


def correlate(panels, table, place, parts, wanted, wave, before):
    per_step = table.shape[0] // LANES // LATE
    span = per_step * 2 * LANES
    rows = panels[0].shape[0]
    early = LATE - 1
    steps = 1 if wave else early
    lists = len(wanted)
    count = -(-lists * NB_SRC // 8) * 8
    each = NB_SRC * PAIRS
    turn = np.arange(LANES) * (np.pi / 16)
    ends = np.stack([np.cos(turn), np.sin(turn)]) * (2.0 / np.sqrt(F))
    sums = [
        jax.ShapeDtypeStruct((count * PAIRS, LAGS), jnp.float32),
        jax.ShapeDtypeStruct((count * PAIRS, LANES), jnp.float32),
    ]
    chosen = jax.ShapeDtypeStruct((2 * BLK * WINDOWS * count, rows * parts), jnp.bfloat16)
    whole = lambda array: pl.BlockSpec(array.shape, lambda i, place: (0, 0))
    if wave:
        extra = before
        extra_specs = [whole(array) for array in before]
        outs = [jax.ShapeDtypeStruct((each, LAGS), jnp.bfloat16)] * lists
        scratch = [pltpu.VMEM(array.shape, array.dtype) for array in sums]
    else:
        extra = [panels[d] for d in wanted]
        extra_specs = [pl.BlockSpec((rows, LANES), lambda i, place: (0, steps * span // LANES))] * lists
        outs = [*sums, chosen]
        scratch = []
    return pl.pallas_call(
        functools.partial(corr_kernel, per_step, parts, lists, wave),
        grid_spec=pltpu.PrefetchScalarGridSpec(
            num_scalar_prefetch=1,
            grid=(steps,),
            in_specs=[
                *[pl.BlockSpec((rows, span), lambda i, place: (0, i))] * parts,
                pl.BlockSpec((span // 2, LAGS), lambda i, place: (i + wave * early, 0)),
                pl.BlockSpec((2, LANES), lambda i, place: (0, 0)),
                *extra_specs,
            ],
            out_specs=[whole(array) for array in outs],
            scratch_shapes=scratch,
        ),
        out_shape=outs,
        compiler_params=pltpu.CompilerParams(vmem_limit_bytes=VMEM_LIMIT),
        cost_estimate=pl.CostEstimate(
            flops=count * PAIRS * steps * span * LAGS,
            bytes_accessed=steps * span * LAGS,
            transcendentals=0,
        ),
        name="correlate",
    )(place[None], *[panels[d] for d in sequence(parts)], table, jnp.asarray(ends, jnp.float32), *extra)


def settle_kernel(groups, mine_ref, owners_ref, *refs):
    part_refs, out_refs = refs[:-2], refs[-2:]
    rows = groups * ROOM * PAIRS
    slots = rows // PAIRS
    each = NB_SRC * PAIRS
    tall = 24
    spare = jnp.full((1, LANES - NB_SRC), rows, jnp.int32)
    owner = jnp.concatenate([owners_ref[...], spare], axis=1)
    wide = jnp.broadcast_to(owner, (tall, LANES)).astype(jnp.float32)
    line, lane = iota((tall, LANES), 0), iota((tall, LANES), 1)
    other = jnp.sum(jnp.where(line == lane, wide, 0.0), axis=1, keepdims=True)
    earlier = jnp.logical_and(other == wide, line < lane).astype(jnp.float32)
    rank = jnp.sum(earlier, axis=0, keepdims=True)
    turn = jnp.bitwise_xor(owner, mine_ref[0])
    block = lax.shift_right_logical(turn, 1) + jnp.bitwise_and(turn, 1) * (groups // 2)
    slot = jnp.where(owner < groups, block, rows).astype(jnp.float32) * ROOM + rank
    held = ones(iota((slots, LANES), 0).astype(jnp.float32) == slot)
    down = ones(lax.shift_right_logical(iota((rows, slots), 0), 2) == iota((rows, slots), 1))
    over = ones(lax.shift_right_logical(iota((LANES, each), 1), 2) == iota((LANES, each), 0))
    block = jnp.dot(down, held, preferred_element_type=jnp.float32).astype(jnp.bfloat16)
    block = jnp.dot(block, over, preferred_element_type=jnp.float32)
    same = jnp.bitwise_and(iota((rows, each), 0), PAIRS - 1) == jnp.bitwise_and(iota((rows, each), 1), PAIRS - 1)
    chosen = jnp.where(same, block, 0.0).astype(jnp.bfloat16)
    total = sum(ref[...].astype(jnp.float32) for ref in part_refs)
    placed = jnp.dot(chosen, total.astype(jnp.bfloat16), preferred_element_type=jnp.float32)
    for i, out_ref in enumerate(out_refs):
        out_ref[...] = placed[i * rows // 2 : (i + 1) * rows // 2].astype(jnp.bfloat16)


def settle(owners, partials, mine, groups):
    whole = lambda array: pl.BlockSpec(array.shape, lambda i, mine: (0, 0))
    outs = [jax.ShapeDtypeStruct((groups * ROOM * PAIRS // 2, LAGS), jnp.bfloat16)] * 2
    return list(pl.pallas_call(
        functools.partial(settle_kernel, groups),
        grid_spec=pltpu.PrefetchScalarGridSpec(
            num_scalar_prefetch=1,
            grid=(1,),
            in_specs=[whole(array) for array in [owners, *partials]],
            out_specs=[whole(array) for array in outs],
        ),
        out_shape=outs,
        compiler_params=pltpu.CompilerParams(vmem_limit_bytes=VMEM_LIMIT),
        name="settle",
    )(mine[None], owners, *partials))


def bundle_kernel(kept_ref, brought_ref, *out_refs):
    deep = ROOM * PAIRS
    for j, out_ref in enumerate(out_refs):
        out_ref[:deep] = kept_ref[j * deep : (j + 1) * deep]
        out_ref[deep:] = brought_ref[j * deep : (j + 1) * deep]


def bundle(kept, brought):
    count = kept.shape[0] // (ROOM * PAIRS)
    return list(pl.pallas_call(
        bundle_kernel,
        out_shape=[jax.ShapeDtypeStruct((2 * ROOM * PAIRS, LAGS), jnp.bfloat16)] * count,
        compiler_params=pltpu.CompilerParams(vmem_limit_bytes=VMEM_LIMIT),
        name="bundle",
    )(kept, brought))


def widen_kernel(mine_ref, *refs):
    part_refs, out_ref = refs[:-1], refs[-1]
    for j, part_ref in enumerate(part_refs):
        values = part_ref[...].astype(jnp.float32)
        for side in range(2):
            first = jnp.bitwise_xor(mine_ref[0], 2 * j + side) * MOST
            for r in range(MOST):
                at = (side * ROOM + r) * PAIRS
                out_ref[first + r] = values[at : at + PAIRS]


def widen(pieces, mine):
    shape = (2 * len(pieces) * MOST, PAIRS, LAGS)
    return pl.pallas_call(
        widen_kernel,
        grid_spec=pltpu.PrefetchScalarGridSpec(
            num_scalar_prefetch=1,
            grid=(1,),
            in_specs=[pl.BlockSpec(array.shape, lambda i, mine: (0, 0)) for array in pieces],
            out_specs=pl.BlockSpec(shape, lambda i, mine: (0, 0, 0)),
        ),
        out_shape=jax.ShapeDtypeStruct(shape, jnp.float32),
        compiler_params=pltpu.CompilerParams(vmem_limit_bytes=VMEM_LIMIT),
        name="widen",
    )(mine[None], *pieces)


def local(spectra, pair_blocks, owners):
    groups = lax.axis_size("grp")
    parts = lax.axis_size("chan")
    place = lax.axis_index("chan")
    chunks = F // LANES // parts

    def swap(array, d):
        return lax.ppermute(array, "chan", [(i, i ^ d) for i in range(parts)])

    def exchange(panels):
        moved = {d: swap(panels[d], d) for d in sequence(parts)[:-1]}
        return panels[:1] + [moved[d] for d in range(1, parts)]

    first, second = whiten(spectra, pair_blocks[0, 0].T, place, parts)
    first = exchange(first)
    table = tables(place, chunks)
    table, second = lax.optimization_barrier((table, second))
    second = exchange(second)

    order = list(reversed(range(parts)))
    halves = (order[: parts // 2], order[parts // 2 :])
    sums = [correlate(first, table, place, parts, wanted, 0, None) for wanted in halves]
    ordered, sums = lax.optimization_barrier(([second[d] for d in sequence(parts)], sums))
    for d, panel in zip(sequence(parts), ordered):
        second[d] = panel
    partials = []
    for wanted, before in zip(halves, sums):
        for d, rows in zip(wanted, correlate(second, table, place, parts, wanted, 1, before)):
            partials.append(swap(rows, d) if d else rows)
    mine = lax.axis_index("grp")

    def trade(array, m):
        return lax.ppermute(array, "grp", [(i, i ^ m) for i in range(groups)])

    kept, cross = settle(owners[0, 0].T, partials, mine, groups)
    pieces = bundle(kept, trade(cross, 1))
    for j in reversed(range(1, groups // 2)):
        pieces[j] = trade(pieces[j], 2 * j)
    return widen(pieces, mine)[None, None]


def solution(mesh):
    return jax.shard_map(
        local,
        mesh=mesh,
        in_specs=(
            P(("grp", "chan"), None, None, None),
            P("grp", "chan", None, None),
            P("grp", "chan", None, None),
        ),
        out_specs=P("grp", "chan", None, None, None),
        check_vma=False,
    )
```

```python
import functools

import jax
import jax.numpy as jnp
import numpy as np
from jax import lax
from jax.experimental import pallas as pl
from jax.experimental.pallas import tpu as pltpu
from jax.sharding import PartitionSpec as P

F = 8192
LAGS = 1024
BLK = 2
NB_SRC = 18
MOST = 3
WINDOWS = 2
LANES = 128
PAIRS = BLK * BLK
VMEM_LIMIT = 24 * 1024 * 1024
HALF = LAGS // 2
ROOM = 4
WAVES = 2
LATE = 2


def whiten_kernel(parts, place_ref, spec_ref, pairs_ref, *out_refs):
    blocks = F // LANES
    each = blocks // parts
    late = each // LATE
    place = place_ref[0]

    def values(start):
        span = pl.ds(start, LANES)
        re = spec_ref[0, :, span].astype(jnp.float32)
        im = spec_ref[1, :, span].astype(jnp.float32)
        return re, im, re * re + im * im

    shape = (spec_ref.shape[1], LANES)
    line = lax.broadcasted_iota(jnp.int32, shape, 0)
    spare = jnp.zeros((1, LANES - NB_SRC), jnp.int32)
    wide = lambda row: jnp.broadcast_to(jnp.concatenate([row, spare], axis=1), shape)
    notes = jnp.where(line == 0, wide(pairs_ref[0:1]), wide(pairs_ref[1:2]))
    notes = notes.astype(jnp.float32).astype(jnp.bfloat16)
    for out_ref in out_refs[:parts]:
        out_ref[:, (each - late) * 2 * LANES :] = notes
    sums = [None] * 4
    for k in range(blocks):
        power = values(k * LANES)[2]
        sums[k % 4] = power if k < 4 else sums[k % 4] + power
    total = jnp.sum((sums[0] + sums[1]) + (sums[2] + sums[3]), axis=1, keepdims=True)
    level = 0.1 * (total * (1.0 / F) + 1e-05)
    for index, out_ref in enumerate(out_refs):
        wave, d = divmod(index, parts)
        first = jnp.bitwise_xor(place, d) * each + wave * (each - late)
        for k in range(late if wave else each - late):
            re, im, power = values(pl.multiple_of((first + k) * LANES, LANES))
            scale = lax.rsqrt(power + level)
            at = k * 2 * LANES
            out_ref[:, at : at + LANES] = (re * scale).astype(jnp.bfloat16)
            out_ref[:, at + LANES : at + 2 * LANES] = (im * scale).astype(jnp.bfloat16)


def whiten(spectra, pairs, place, parts):
    rows = spectra.shape[0] * WINDOWS
    planes = jnp.transpose(spectra.reshape(rows, 2, F), (1, 0, 2))
    width = 2 * F // parts
    late = width // LATE
    shapes = [(rows, width - late + LANES)] * parts + [(rows, late)] * parts
    whole = lambda array: pl.BlockSpec(array.shape, lambda i, place: (0,) * array.ndim)
    outs = pl.pallas_call(
        functools.partial(whiten_kernel, parts),
        grid_spec=pltpu.PrefetchScalarGridSpec(
            num_scalar_prefetch=1,
            grid=(1,),
            in_specs=[whole(array) for array in [planes, pairs]],
            out_specs=[pl.BlockSpec(shape, lambda i, place: (0, 0)) for shape in shapes],
        ),
        out_shape=[jax.ShapeDtypeStruct(shape, jnp.bfloat16) for shape in shapes],
        compiler_params=pltpu.CompilerParams(vmem_limit_bytes=VMEM_LIMIT),
        name="whiten",
    )(place[None], planes, pairs)
    return list(outs[:parts]), list(outs[parts:])


def table_kernel(first_ref, hi_cos_ref, hi_sin_ref, mid_cos_ref, mid_sin_ref, lo_cos_ref, lo_sin_ref, out_ref, cos, sin):
    s = pl.program_id(0)
    few = lo_cos_ref.shape[0]

    @pl.when(s == 0)
    def combine():
        lo_cos = lo_cos_ref[...]
        lo_sin = lo_sin_ref[...]
        for i in range(LANES // few):
            mid_cos = mid_cos_ref[i : i + 1]
            mid_sin = mid_sin_ref[i : i + 1]
            cos[i * few : (i + 1) * few] = mid_cos * lo_cos - mid_sin * lo_sin
            sin[i * few : (i + 1) * few] = mid_sin * lo_cos + mid_cos * lo_sin

    hi_cos = hi_cos_ref[pl.ds(s, 1), :]
    hi_sin = hi_sin_ref[pl.ds(s, 1), :]
    minus_cos = -hi_cos
    for i in range(0, LANES, 16):
        lo_cos = cos[i : i + 16]
        lo_sin = sin[i : i + 16]
        out_ref[i : i + 16, :HALF] = (hi_cos * lo_cos - hi_sin * lo_sin).astype(jnp.bfloat16)
        out_ref[i : i + 16, HALF:] = (minus_cos * lo_sin - hi_sin * lo_cos).astype(jnp.bfloat16)

    @pl.when(jnp.logical_and(first_ref[0] == 0, s == 0))
    def zero_bin():
        row = lax.broadcasted_iota(jnp.int32, (16, HALF), 0)
        weight = jnp.where(row == 0, 0.5, 1.0)
        out_ref[0:16, :HALF] = ((hi_cos * cos[0:16] - hi_sin * sin[0:16]) * weight).astype(jnp.bfloat16)


def tables(place, chunks):
    lag = jnp.arange(HALF, dtype=jnp.int32)
    few = 8
    middle = LANES // few
    bins = jnp.concatenate([
        (place * chunks + jnp.arange(chunks, dtype=jnp.int32)) * LANES,
        jnp.arange(middle, dtype=jnp.int32) * few,
        jnp.arange(few, dtype=jnp.int32),
    ])
    phase = bins[:, None] * lag[None, :] % (2 * F)
    angle = phase.astype(jnp.float32) * (jnp.pi / F)
    cos = jnp.cos(angle)
    sin = jnp.sin(angle)
    unit = 2.0 / jnp.sqrt(jnp.float32(F))
    cuts = [slice(0, chunks), slice(chunks, chunks + middle), slice(chunks + middle, None)]
    operands = [cos[cuts[0]] * unit, sin[cuts[0]] * unit, cos[cuts[1]], sin[cuts[1]], cos[cuts[2]], sin[cuts[2]]]
    return pl.pallas_call(
        table_kernel,
        grid_spec=pltpu.PrefetchScalarGridSpec(
            num_scalar_prefetch=1,
            grid=(chunks,),
            in_specs=[pl.BlockSpec(array.shape, lambda s, first: (0, 0)) for array in operands],
            out_specs=pl.BlockSpec((LANES, LAGS), lambda s, first: (s, 0)),
            scratch_shapes=[pltpu.VMEM((LANES, HALF), jnp.float32)] * 2,
        ),
        out_shape=jax.ShapeDtypeStruct((chunks * LANES, LAGS), jnp.bfloat16),
        cost_estimate=pl.CostEstimate(
            flops=chunks * LANES * LAGS * 4, bytes_accessed=chunks * LANES * LAGS * 2, transcendentals=0
        ),
        compiler_params=pltpu.CompilerParams(vmem_limit_bytes=VMEM_LIMIT),
        name="tables",
    )(place[None], *operands)


def iota(shape, axis):
    return lax.broadcasted_iota(jnp.int32, shape, axis)


def ones(hit):
    return hit.astype(jnp.float32).astype(jnp.bfloat16)


def choose_rows(lists, place, packed, rows_ref):
    height = rows_ref.shape[1]
    count = rows_ref.shape[0] // (2 * BLK * WINDOWS)
    deep = packed.shape[0] // lists
    blocks = deep // (BLK * WINDOWS)
    line = iota((count, 1), 0)
    group = jnp.zeros_like(line)
    for z in range(1, lists):
        group = group + jnp.where(line >= z * NB_SRC, 1, 0)
    here = iota((count, LANES), 1) == line - group * NB_SRC

    def column(kind):
        row = ones(iota((count, packed.shape[0]), 1) == group * deep + kind)
        found = jnp.dot(row, packed, preferred_element_type=jnp.float32)
        return jnp.sum(jnp.where(here, found, 0.0), axis=1, keepdims=True).astype(jnp.int32)

    across = iota((count, height), 1)
    picks = []
    for block in (column(0), column(1)):
        first = jnp.bitwise_xor(block, place * blocks) * (BLK * WINDOWS)
        for offset in range(BLK * WINDOWS):
            picks.append((across == first + offset).astype(jnp.float32))
    rows_ref[...] = jnp.concatenate(picks, axis=0).astype(jnp.bfloat16)


def sequence(parts):
    order = list(reversed(range(parts)))
    return [order[0], order[-2], *order[1:-2], order[-1]]


def corr_kernel(per_step, parts, lists, wave, place, *refs):
    panel_refs, (table_ref, ends_ref), refs = dict(zip(sequence(parts), refs)), refs[parts : parts + 2], refs[parts + 2 :]
    step = pl.program_id(0)
    if wave:
        (total_in, edge_in, rows_ref), out_refs, (total, edge) = refs[:3], refs[3:-2], refs[-2:]
    else:
        note_refs, (total, edge, rows_ref) = refs[:lists], refs[lists:]

        @pl.when(step == 0)
        def prepare():
            choose_rows(lists, place[0], jnp.concatenate([ref[...] for ref in note_refs]), rows_ref)

    count = total.shape[0] // PAIRS
    panel = jnp.concatenate([panel_refs[d][...] for d in range(parts)])
    chosen = jnp.dot(rows_ref[...], panel, preferred_element_type=jnp.float32)

    def row(side, channel, window, start):
        first = ((side * BLK + channel) * WINDOWS + window) * count
        return chosen[first : first + count, start : start + LANES]

    reals = []
    imags = []
    lane = iota((1, LANES), 1)
    first_bin = jnp.logical_and(jnp.logical_and(place[0] == 0, step == 0), lane == 0)
    edge_part = 0.0
    for i in range(per_step):
        at = i * 2 * LANES
        real = []
        imag = []
        for p in range(BLK):
            for q in range(BLK):
                re = 0.0
                im = 0.0
                for w in range(WINDOWS):
                    ra, ia = row(0, p, w, at), row(0, p, w, at + LANES)
                    rb, ib = row(1, q, w, at), row(1, q, w, at + LANES)
                    re = re + (ra * rb + ia * ib)
                    im = im + (ia * rb - ra * ib)
                real.append(re * (1.0 / WINDOWS))
                imag.append(im * (1.0 / WINDOWS))
        real = jnp.concatenate(real, axis=0)
        imag = jnp.concatenate(imag, axis=0)
        ends = ends_ref[0:1]
        if i == 0 and wave == 0:
            ends = jnp.where(first_bin, 0.5 * ends, ends)
        edge_part = edge_part + (real * ends + imag * ends_ref[1:2])
        reals.append(real.astype(jnp.bfloat16))
        imags.append(imag.astype(jnp.bfloat16))

    def transform(pieces, columns):
        rows = jnp.concatenate(pieces, axis=1)
        return jnp.dot(rows, table_ref[:, columns], preferred_element_type=jnp.float32)

    even = transform(reals, slice(0, HALF))
    odd = transform(imags, slice(HALF, LAGS))

    @pl.when(step == 0)
    def start():
        total[:, :HALF] = total_in[:, :HALF] + even if wave else even
        total[:, HALF:] = total_in[:, HALF:] + odd if wave else odd
        edge[...] = edge_in[...] + edge_part if wave else edge_part

    @pl.when(step > 0)
    def add():
        total[:, :HALF] += even
        total[:, HALF:] += odd
        edge[...] += edge_part

    if wave < WAVES - 1:
        return

    @pl.when(step == pl.num_programs(0) - 1)
    def finish():
        even = total[:, :HALF]
        odd = total[:, HALF:]
        later = (even + odd).astype(jnp.bfloat16)
        mirror = ones(iota((HALF, HALF), 0) + iota((HALF, HALF), 1) == HALF)
        sooner = jnp.dot((even - odd).astype(jnp.bfloat16), mirror, preferred_element_type=jnp.float32)
        least = jnp.sum(edge[...], axis=1, keepdims=True)
        sooner = jnp.where(iota(sooner.shape, 1) == 0, least, sooner).astype(jnp.bfloat16)
        each = NB_SRC * PAIRS
        shape = (each * len(out_refs), PAIRS * count)
        column = iota(shape, 1)
        number = column * PAIRS
        for n in range(1, PAIRS):
            number = number - jnp.where(column >= n * count, count * PAIRS - 1, 0)
        order = ones(iota(shape, 0) == number)
        both = jnp.concatenate([sooner, later], axis=1)
        rows = jnp.dot(order, both, preferred_element_type=jnp.float32)
        for i, out_ref in enumerate(out_refs):
            out_ref[...] = rows[i * each : (i + 1) * each].astype(jnp.bfloat16)


def correlate(panels, table, place, parts, wanted, wave, before):
    chunks = table.shape[0] // LANES
    per_step = min(4, chunks // LATE)
    span = per_step * 2 * LANES
    rows = panels[0].shape[0]
    late = chunks // LATE // per_step
    early = chunks // per_step - late
    steps = late if wave else early
    lists = len(wanted)
    count = -(-lists * NB_SRC // 8) * 8
    each = NB_SRC * PAIRS
    turn = np.arange(LANES) * (np.pi / 16)
    ends = np.stack([np.cos(turn), np.sin(turn)]) * (2.0 / np.sqrt(F))
    sums = [
        jax.ShapeDtypeStruct((count * PAIRS, LAGS), jnp.float32),
        jax.ShapeDtypeStruct((count * PAIRS, LANES), jnp.float32),
    ]
    chosen = jax.ShapeDtypeStruct((2 * BLK * WINDOWS * count, rows * parts), jnp.bfloat16)
    whole = lambda array: pl.BlockSpec(array.shape, lambda i, place: (0, 0))
    if wave:
        extra = before
        extra_specs = [whole(array) for array in before]
        outs = [jax.ShapeDtypeStruct((each, LAGS), jnp.bfloat16)] * lists
        scratch = [pltpu.VMEM(array.shape, array.dtype) for array in sums]
    else:
        extra = [panels[d] for d in wanted]
        extra_specs = [pl.BlockSpec((rows, LANES), lambda i, place: (0, steps * span // LANES))] * lists
        outs = [*sums, chosen]
        scratch = []
    return pl.pallas_call(
        functools.partial(corr_kernel, per_step, parts, lists, wave),
        grid_spec=pltpu.PrefetchScalarGridSpec(
            num_scalar_prefetch=1,
            grid=(steps,),
            in_specs=[
                *[pl.BlockSpec((rows, span), lambda i, place: (0, i))] * parts,
                pl.BlockSpec((span // 2, LAGS), lambda i, place: (i + wave * early, 0)),
                pl.BlockSpec((2, LANES), lambda i, place: (0, 0)),
                *extra_specs,
            ],
            out_specs=[whole(array) for array in outs],
            scratch_shapes=scratch,
        ),
        out_shape=outs,
        compiler_params=pltpu.CompilerParams(vmem_limit_bytes=VMEM_LIMIT),
        cost_estimate=pl.CostEstimate(
            flops=count * PAIRS * steps * span * LAGS,
            bytes_accessed=steps * span * LAGS,
            transcendentals=0,
        ),
        name="correlate",
    )(place[None], *[panels[d] for d in sequence(parts)], table, jnp.asarray(ends, jnp.float32), *extra)


def settle_kernel(groups, mine_ref, owners_ref, *refs):
    part_refs, out_refs = refs[:-2], refs[-2:]
    rows = groups * ROOM * PAIRS
    slots = rows // PAIRS
    each = NB_SRC * PAIRS
    tall = 24
    spare = jnp.full((1, LANES - NB_SRC), rows, jnp.int32)
    owner = jnp.concatenate([owners_ref[...], spare], axis=1)
    wide = jnp.broadcast_to(owner, (tall, LANES)).astype(jnp.float32)
    line, lane = iota((tall, LANES), 0), iota((tall, LANES), 1)
    other = jnp.sum(jnp.where(line == lane, wide, 0.0), axis=1, keepdims=True)
    earlier = jnp.logical_and(other == wide, line < lane).astype(jnp.float32)
    rank = jnp.sum(earlier, axis=0, keepdims=True)
    turn = jnp.bitwise_xor(owner, mine_ref[0])
    block = lax.shift_right_logical(turn, 1) + jnp.bitwise_and(turn, 1) * (groups // 2)
    slot = jnp.where(owner < groups, block, rows).astype(jnp.float32) * ROOM + rank
    held = ones(iota((slots, LANES), 0).astype(jnp.float32) == slot)
    down = ones(lax.shift_right_logical(iota((rows, slots), 0), 2) == iota((rows, slots), 1))
    over = ones(lax.shift_right_logical(iota((LANES, each), 1), 2) == iota((LANES, each), 0))
    block = jnp.dot(down, held, preferred_element_type=jnp.float32).astype(jnp.bfloat16)
    block = jnp.dot(block, over, preferred_element_type=jnp.float32)
    same = jnp.bitwise_and(iota((rows, each), 0), PAIRS - 1) == jnp.bitwise_and(iota((rows, each), 1), PAIRS - 1)
    chosen = jnp.where(same, block, 0.0).astype(jnp.bfloat16)
    total = sum(ref[...].astype(jnp.float32) for ref in part_refs)
    placed = jnp.dot(chosen, total.astype(jnp.bfloat16), preferred_element_type=jnp.float32)
    for i, out_ref in enumerate(out_refs):
        out_ref[...] = placed[i * rows // 2 : (i + 1) * rows // 2].astype(jnp.bfloat16)


def settle(owners, partials, mine, groups):
    whole = lambda array: pl.BlockSpec(array.shape, lambda i, mine: (0, 0))
    outs = [jax.ShapeDtypeStruct((groups * ROOM * PAIRS // 2, LAGS), jnp.bfloat16)] * 2
    return list(pl.pallas_call(
        functools.partial(settle_kernel, groups),
        grid_spec=pltpu.PrefetchScalarGridSpec(
            num_scalar_prefetch=1,
            grid=(1,),
            in_specs=[whole(array) for array in [owners, *partials]],
            out_specs=[whole(array) for array in outs],
        ),
        out_shape=outs,
        compiler_params=pltpu.CompilerParams(vmem_limit_bytes=VMEM_LIMIT),
        name="settle",
    )(mine[None], owners, *partials))


def bundle_kernel(kept_ref, brought_ref, *out_refs):
    deep = ROOM * PAIRS
    for j, out_ref in enumerate(out_refs):
        out_ref[:deep] = kept_ref[j * deep : (j + 1) * deep]
        out_ref[deep:] = brought_ref[j * deep : (j + 1) * deep]


def bundle(kept, brought):
    count = kept.shape[0] // (ROOM * PAIRS)
    return list(pl.pallas_call(
        bundle_kernel,
        out_shape=[jax.ShapeDtypeStruct((2 * ROOM * PAIRS, LAGS), jnp.bfloat16)] * count,
        compiler_params=pltpu.CompilerParams(vmem_limit_bytes=VMEM_LIMIT),
        name="bundle",
    )(kept, brought))


def widen_kernel(mine_ref, *refs):
    part_refs, out_ref = refs[:-1], refs[-1]
    for j, part_ref in enumerate(part_refs):
        values = part_ref[...].astype(jnp.float32)
        for side in range(2):
            first = jnp.bitwise_xor(mine_ref[0], 2 * j + side) * MOST
            for r in range(MOST):
                at = (side * ROOM + r) * PAIRS
                out_ref[first + r] = values[at : at + PAIRS]


def widen(pieces, mine):
    shape = (2 * len(pieces) * MOST, PAIRS, LAGS)
    return pl.pallas_call(
        widen_kernel,
        grid_spec=pltpu.PrefetchScalarGridSpec(
            num_scalar_prefetch=1,
            grid=(1,),
            in_specs=[pl.BlockSpec(array.shape, lambda i, mine: (0, 0)) for array in pieces],
            out_specs=pl.BlockSpec(shape, lambda i, mine: (0, 0, 0)),
        ),
        out_shape=jax.ShapeDtypeStruct(shape, jnp.float32),
        compiler_params=pltpu.CompilerParams(vmem_limit_bytes=VMEM_LIMIT),
        name="widen",
    )(mine[None], *pieces)


def local(spectra, pair_blocks, owners):
    groups = lax.axis_size("grp")
    parts = lax.axis_size("chan")
    place = lax.axis_index("chan")
    chunks = F // LANES // parts

    def swap(array, d):
        return lax.ppermute(array, "chan", [(i, i ^ d) for i in range(parts)])

    def exchange(panels):
        moved = {d: swap(panels[d], d) for d in sequence(parts)[:-1]}
        return panels[:1] + [moved[d] for d in range(1, parts)]

    first, second = whiten(spectra, pair_blocks[0, 0].T, place, parts)
    first = exchange(first)
    table = tables(place, chunks)
    gates = [d for d in sequence(parts)[:2] if d]
    here, second = lax.optimization_barrier(([first[d] for d in gates], second))
    for d, panel in zip(gates, here):
        first[d] = panel
    second = exchange(second)

    order = list(reversed(range(parts)))
    halves = (order[: parts // 2], order[parts // 2 :])
    sums = [correlate(first, table, place, parts, wanted, 0, None) for wanted in halves]
    ordered, sums = lax.optimization_barrier(([second[d] for d in sequence(parts)], sums))
    for d, panel in zip(sequence(parts), ordered):
        second[d] = panel
    partials = []
    for wanted, before in zip(halves, sums):
        for d, rows in zip(wanted, correlate(second, table, place, parts, wanted, 1, before)):
            partials.append(swap(rows, d) if d else rows)
    mine = lax.axis_index("grp")

    def trade(array, m):
        return lax.ppermute(array, "grp", [(i, i ^ m) for i in range(groups)])

    kept, cross = settle(owners[0, 0].T, partials, mine, groups)
    pieces = bundle(kept, trade(cross, 1))
    for j in reversed(range(1, groups // 2)):
        pieces[j] = trade(pieces[j], 2 * j)
    return widen(pieces, mine)[None, None]


def solution(mesh):
    return jax.shard_map(
        local,
        mesh=mesh,
        in_specs=(
            P(("grp", "chan"), None, None, None),
            P("grp", "chan", None, None),
            P("grp", "chan", None, None),
        ),
        out_specs=P("grp", "chan", None, None, None),
        check_vma=False,
    )
```

```python
import functools

import jax
import jax.numpy as jnp
import numpy as np
from jax import lax
from jax.experimental import pallas as pl
from jax.experimental.pallas import tpu as pltpu
from jax.sharding import PartitionSpec as P

F = 8192
LAGS = 1024
BLK = 2
NB_SRC = 18
MOST = 3
WINDOWS = 2
LANES = 128
PAIRS = BLK * BLK
VMEM_LIMIT = 24 * 1024 * 1024
HALF = LAGS // 2
ROOM = 4
WAVES = 2
LATE = 2


def works(place):
    return bool((place ^ (place >> 1)) & 1)


def whiten_kernel(parts, place_ref, spec_ref, pairs_ref, *out_refs):
    blocks = F // LANES
    each = blocks // (parts // 2)
    late = each // LATE
    place = place_ref[0]

    def values(start):
        span = pl.ds(start, LANES)
        re = spec_ref[0, :, span].astype(jnp.float32)
        im = spec_ref[1, :, span].astype(jnp.float32)
        return re, im, re * re + im * im

    shape = (spec_ref.shape[1], LANES)
    line = lax.broadcasted_iota(jnp.int32, shape, 0)
    spare = jnp.zeros((1, LANES - NB_SRC), jnp.int32)
    wide = lambda row: jnp.broadcast_to(jnp.concatenate([row, spare], axis=1), shape)
    notes = jnp.where(line == 0, wide(pairs_ref[0:1]), wide(pairs_ref[1:2]))
    notes = notes.astype(jnp.float32).astype(jnp.bfloat16)
    for out_ref in out_refs[:parts]:
        out_ref[:, (each - late) * 2 * LANES :] = notes
    sums = [None] * 4
    for k in range(blocks):
        power = values(k * LANES)[2]
        sums[k % 4] = power if k < 4 else sums[k % 4] + power
    total = jnp.sum((sums[0] + sums[1]) + (sums[2] + sums[3]), axis=1, keepdims=True)
    level = 0.1 * (total * (1.0 / F) + 1e-05)
    for index, out_ref in enumerate(out_refs):
        wave, d = divmod(index, parts)
        first = lax.shift_right_logical(jnp.bitwise_xor(place, d), 1) * each + wave * (each - late)
        for k in range(late if wave else each - late):
            re, im, power = values(pl.multiple_of((first + k) * LANES, LANES))
            scale = lax.rsqrt(power + level)
            at = k * 2 * LANES
            out_ref[:, at : at + LANES] = (re * scale).astype(jnp.bfloat16)
            out_ref[:, at + LANES : at + 2 * LANES] = (im * scale).astype(jnp.bfloat16)


def whiten(spectra, pairs, place, parts):
    rows = spectra.shape[0] * WINDOWS
    planes = jnp.transpose(spectra.reshape(rows, 2, F), (1, 0, 2))
    width = 2 * F // (parts // 2)
    late = width // LATE
    shapes = [(rows, width - late + LANES)] * parts + [(rows, late)] * parts
    whole = lambda array: pl.BlockSpec(array.shape, lambda i, place: (0,) * array.ndim)
    outs = pl.pallas_call(
        functools.partial(whiten_kernel, parts),
        grid_spec=pltpu.PrefetchScalarGridSpec(
            num_scalar_prefetch=1,
            grid=(1,),
            in_specs=[whole(array) for array in [planes, pairs]],
            out_specs=[pl.BlockSpec(shape, lambda i, place: (0, 0)) for shape in shapes],
        ),
        out_shape=[jax.ShapeDtypeStruct(shape, jnp.bfloat16) for shape in shapes],
        compiler_params=pltpu.CompilerParams(vmem_limit_bytes=VMEM_LIMIT),
        name="whiten",
    )(place[None], planes, pairs)
    return list(outs[:parts]), list(outs[parts:])


def table_kernel(first_ref, hi_cos_ref, hi_sin_ref, mid_cos_ref, mid_sin_ref, lo_cos_ref, lo_sin_ref, out_ref, cos, sin):
    s = pl.program_id(0)
    few = lo_cos_ref.shape[0]

    @pl.when(s == 0)
    def combine():
        lo_cos = lo_cos_ref[...]
        lo_sin = lo_sin_ref[...]
        for i in range(LANES // few):
            mid_cos = mid_cos_ref[i : i + 1]
            mid_sin = mid_sin_ref[i : i + 1]
            cos[i * few : (i + 1) * few] = mid_cos * lo_cos - mid_sin * lo_sin
            sin[i * few : (i + 1) * few] = mid_sin * lo_cos + mid_cos * lo_sin

    hi_cos = hi_cos_ref[pl.ds(s, 1), :]
    hi_sin = hi_sin_ref[pl.ds(s, 1), :]
    minus_cos = -hi_cos
    for i in range(0, LANES, 16):
        lo_cos = cos[i : i + 16]
        lo_sin = sin[i : i + 16]
        out_ref[i : i + 16, :HALF] = (hi_cos * lo_cos - hi_sin * lo_sin).astype(jnp.bfloat16)
        out_ref[i : i + 16, HALF:] = (minus_cos * lo_sin - hi_sin * lo_cos).astype(jnp.bfloat16)

    @pl.when(jnp.logical_and(first_ref[0] == 0, s == 0))
    def zero_bin():
        row = lax.broadcasted_iota(jnp.int32, (16, HALF), 0)
        weight = jnp.where(row == 0, 0.5, 1.0)
        out_ref[0:16, :HALF] = ((hi_cos * cos[0:16] - hi_sin * sin[0:16]) * weight).astype(jnp.bfloat16)


def tables(place, chunks):
    lag = jnp.arange(HALF, dtype=jnp.int32)
    few = 8
    middle = LANES // few
    bins = jnp.concatenate([
        (place * chunks + jnp.arange(chunks, dtype=jnp.int32)) * LANES,
        jnp.arange(middle, dtype=jnp.int32) * few,
        jnp.arange(few, dtype=jnp.int32),
    ])
    phase = bins[:, None] * lag[None, :] % (2 * F)
    angle = phase.astype(jnp.float32) * (jnp.pi / F)
    cos = jnp.cos(angle)
    sin = jnp.sin(angle)
    unit = 2.0 / jnp.sqrt(jnp.float32(F))
    cuts = [slice(0, chunks), slice(chunks, chunks + middle), slice(chunks + middle, None)]
    operands = [cos[cuts[0]] * unit, sin[cuts[0]] * unit, cos[cuts[1]], sin[cuts[1]], cos[cuts[2]], sin[cuts[2]]]
    return pl.pallas_call(
        table_kernel,
        grid_spec=pltpu.PrefetchScalarGridSpec(
            num_scalar_prefetch=1,
            grid=(chunks,),
            in_specs=[pl.BlockSpec(array.shape, lambda s, first: (0, 0)) for array in operands],
            out_specs=pl.BlockSpec((LANES, LAGS), lambda s, first: (s, 0)),
            scratch_shapes=[pltpu.VMEM((LANES, HALF), jnp.float32)] * 2,
        ),
        out_shape=jax.ShapeDtypeStruct((chunks * LANES, LAGS), jnp.bfloat16),
        cost_estimate=pl.CostEstimate(
            flops=chunks * LANES * LAGS * 4, bytes_accessed=chunks * LANES * LAGS * 2, transcendentals=0
        ),
        compiler_params=pltpu.CompilerParams(vmem_limit_bytes=VMEM_LIMIT),
        name="tables",
    )(place[None], *operands)


def iota(shape, axis):
    return lax.broadcasted_iota(jnp.int32, shape, axis)


def ones(hit):
    return hit.astype(jnp.float32).astype(jnp.bfloat16)


def choose_rows(lists, place, packed, rows_ref):
    height = rows_ref.shape[1]
    count = rows_ref.shape[0] // (2 * BLK * WINDOWS)
    deep = packed.shape[0] // lists
    blocks = deep // (BLK * WINDOWS)
    line = iota((count, 1), 0)
    group = jnp.zeros_like(line)
    for z in range(1, lists):
        group = group + jnp.where(line >= z * NB_SRC, 1, 0)
    here = iota((count, LANES), 1) == line - group * NB_SRC

    def column(kind):
        row = ones(iota((count, packed.shape[0]), 1) == group * deep + kind)
        found = jnp.dot(row, packed, preferred_element_type=jnp.float32)
        return jnp.sum(jnp.where(here, found, 0.0), axis=1, keepdims=True).astype(jnp.int32)

    across = iota((count, height), 1)
    picks = []
    for block in (column(0), column(1)):
        first = jnp.bitwise_xor(block, place * blocks) * (BLK * WINDOWS)
        for offset in range(BLK * WINDOWS):
            picks.append((across == first + offset).astype(jnp.float32))
    rows_ref[...] = jnp.concatenate(picks, axis=0).astype(jnp.bfloat16)


def sequence(parts):
    order = list(reversed(range(parts)))
    return [order[0], order[-2], *order[1:-2], order[-1]]


def corr_kernel(per_step, parts, lists, wave, place, *refs):
    panel_refs, (table_ref, ends_ref), refs = dict(zip(sequence(parts), refs)), refs[parts : parts + 2], refs[parts + 2 :]
    step = pl.program_id(0)
    if wave:
        (total_in, edge_in, rows_ref), out_refs, (total, edge) = refs[:3], refs[3:-2], refs[-2:]
    else:
        note_refs, (total, edge, rows_ref) = refs[:lists], refs[lists:]

        @pl.when(step == 0)
        def prepare():
            choose_rows(lists, place[0], jnp.concatenate([ref[...] for ref in note_refs]), rows_ref)

    count = total.shape[0] // PAIRS
    panel = jnp.concatenate([panel_refs[d][...] for d in range(parts)])
    chosen = jnp.dot(rows_ref[...], panel, preferred_element_type=jnp.float32)

    def row(side, channel, window, start):
        first = ((side * BLK + channel) * WINDOWS + window) * count
        return chosen[first : first + count, start : start + LANES]

    reals = []
    imags = []
    lane = iota((1, LANES), 1)
    first_bin = jnp.logical_and(jnp.logical_and(place[0] < 2, step == 0), lane == 0)
    edge_part = 0.0
    for i in range(per_step):
        at = i * 2 * LANES
        real = []
        imag = []
        for p in range(BLK):
            for q in range(BLK):
                re = 0.0
                im = 0.0
                for w in range(WINDOWS):
                    ra, ia = row(0, p, w, at), row(0, p, w, at + LANES)
                    rb, ib = row(1, q, w, at), row(1, q, w, at + LANES)
                    re = re + (ra * rb + ia * ib)
                    im = im + (ia * rb - ra * ib)
                real.append(re * (1.0 / WINDOWS))
                imag.append(im * (1.0 / WINDOWS))
        real = jnp.concatenate(real, axis=0)
        imag = jnp.concatenate(imag, axis=0)
        ends = ends_ref[0:1]
        if i == 0 and wave == 0:
            ends = jnp.where(first_bin, 0.5 * ends, ends)
        edge_part = edge_part + (real * ends + imag * ends_ref[1:2])
        reals.append(real.astype(jnp.bfloat16))
        imags.append(imag.astype(jnp.bfloat16))

    def transform(pieces, columns):
        rows = jnp.concatenate(pieces, axis=1)
        return jnp.dot(rows, table_ref[:, columns], preferred_element_type=jnp.float32)

    even = transform(reals, slice(0, HALF))
    odd = transform(imags, slice(HALF, LAGS))

    @pl.when(step == 0)
    def start():
        total[:, :HALF] = total_in[:, :HALF] + even if wave else even
        total[:, HALF:] = total_in[:, HALF:] + odd if wave else odd
        edge[...] = edge_in[...] + edge_part if wave else edge_part

    @pl.when(step > 0)
    def add():
        total[:, :HALF] += even
        total[:, HALF:] += odd
        edge[...] += edge_part

    if wave < WAVES - 1:
        return

    @pl.when(step == pl.num_programs(0) - 1)
    def finish():
        even = total[:, :HALF]
        odd = total[:, HALF:]
        later = (even + odd).astype(jnp.bfloat16)
        mirror = ones(iota((HALF, HALF), 0) + iota((HALF, HALF), 1) == HALF)
        sooner = jnp.dot((even - odd).astype(jnp.bfloat16), mirror, preferred_element_type=jnp.float32)
        least = jnp.sum(edge[...], axis=1, keepdims=True)
        sooner = jnp.where(iota(sooner.shape, 1) == 0, least, sooner).astype(jnp.bfloat16)
        each = NB_SRC * PAIRS
        shape = (each * len(out_refs), PAIRS * count)
        column = iota(shape, 1)
        number = column * PAIRS
        for n in range(1, PAIRS):
            number = number - jnp.where(column >= n * count, count * PAIRS - 1, 0)
        order = ones(iota(shape, 0) == number)
        both = jnp.concatenate([sooner, later], axis=1)
        rows = jnp.dot(order, both, preferred_element_type=jnp.float32)
        for i, out_ref in enumerate(out_refs):
            out_ref[...] = rows[i * each : (i + 1) * each].astype(jnp.bfloat16)


def correlate(panels, table, place, parts, wanted, wave, before):
    chunks = table.shape[0] // LANES
    per_step = min(4, chunks // LATE)
    span = per_step * 2 * LANES
    rows = panels[0].shape[0]
    late = chunks // LATE // per_step
    early = chunks // per_step - late
    steps = late if wave else early
    lists = len(wanted)
    count = -(-lists * NB_SRC // 8) * 8
    each = NB_SRC * PAIRS
    turn = np.arange(LANES) * (np.pi / 16)
    ends = np.stack([np.cos(turn), np.sin(turn)]) * (2.0 / np.sqrt(F))
    sums = [
        jax.ShapeDtypeStruct((count * PAIRS, LAGS), jnp.float32),
        jax.ShapeDtypeStruct((count * PAIRS, LANES), jnp.float32),
    ]
    chosen = jax.ShapeDtypeStruct((2 * BLK * WINDOWS * count, rows * parts), jnp.bfloat16)
    whole = lambda array: pl.BlockSpec(array.shape, lambda i, place: (0, 0))
    if wave:
        extra = before
        extra_specs = [whole(array) for array in before]
        outs = [jax.ShapeDtypeStruct((each, LAGS), jnp.bfloat16)] * lists
        scratch = [pltpu.VMEM(array.shape, array.dtype) for array in sums]
    else:
        extra = [panels[d] for d in wanted]
        extra_specs = [pl.BlockSpec((rows, LANES), lambda i, place: (0, steps * span // LANES))] * lists
        outs = [*sums, chosen]
        scratch = []
    return pl.pallas_call(
        functools.partial(corr_kernel, per_step, parts, lists, wave),
        grid_spec=pltpu.PrefetchScalarGridSpec(
            num_scalar_prefetch=1,
            grid=(steps,),
            in_specs=[
                *[pl.BlockSpec((rows, span), lambda i, place: (0, i))] * parts,
                pl.BlockSpec((span // 2, LAGS), lambda i, place: (i + wave * early, 0)),
                pl.BlockSpec((2, LANES), lambda i, place: (0, 0)),
                *extra_specs,
            ],
            out_specs=[whole(array) for array in outs],
            scratch_shapes=scratch,
        ),
        out_shape=outs,
        compiler_params=pltpu.CompilerParams(vmem_limit_bytes=VMEM_LIMIT),
        cost_estimate=pl.CostEstimate(
            flops=count * PAIRS * steps * span * LAGS,
            bytes_accessed=steps * span * LAGS,
            transcendentals=0,
        ),
        name="correlate",
    )(place[None], *[panels[d] for d in sequence(parts)], table, jnp.asarray(ends, jnp.float32), *extra)


def settle_kernel(groups, mine_ref, owners_ref, *refs):
    part_refs, out_refs = refs[:-2], refs[-2:]
    rows = groups * ROOM * PAIRS
    slots = rows // PAIRS
    each = NB_SRC * PAIRS
    tall = 24
    spare = jnp.full((1, LANES - NB_SRC), rows, jnp.int32)
    owner = jnp.concatenate([owners_ref[...], spare], axis=1)
    wide = jnp.broadcast_to(owner, (tall, LANES)).astype(jnp.float32)
    line, lane = iota((tall, LANES), 0), iota((tall, LANES), 1)
    other = jnp.sum(jnp.where(line == lane, wide, 0.0), axis=1, keepdims=True)
    earlier = jnp.logical_and(other == wide, line < lane).astype(jnp.float32)
    rank = jnp.sum(earlier, axis=0, keepdims=True)
    turn = jnp.bitwise_xor(owner, mine_ref[0])
    block = lax.shift_right_logical(turn, 1) + jnp.bitwise_and(turn, 1) * (groups // 2)
    slot = jnp.where(owner < groups, block, rows).astype(jnp.float32) * ROOM + rank
    held = ones(iota((slots, LANES), 0).astype(jnp.float32) == slot)
    down = ones(lax.shift_right_logical(iota((rows, slots), 0), 2) == iota((rows, slots), 1))
    over = ones(lax.shift_right_logical(iota((LANES, each), 1), 2) == iota((LANES, each), 0))
    block = jnp.dot(down, held, preferred_element_type=jnp.float32).astype(jnp.bfloat16)
    block = jnp.dot(block, over, preferred_element_type=jnp.float32)
    same = jnp.bitwise_and(iota((rows, each), 0), PAIRS - 1) == jnp.bitwise_and(iota((rows, each), 1), PAIRS - 1)
    chosen = jnp.where(same, block, 0.0).astype(jnp.bfloat16)
    total = jnp.where(mine_ref[1] == 1, part_refs[-1][...].astype(jnp.float32), 0.0)
    for ref in part_refs[:-1]:
        total = total + ref[...].astype(jnp.float32)
    placed = jnp.dot(chosen, total.astype(jnp.bfloat16), preferred_element_type=jnp.float32)
    for i, out_ref in enumerate(out_refs):
        out_ref[...] = placed[i * rows // 2 : (i + 1) * rows // 2].astype(jnp.bfloat16)


def settle(owners, partials, mine, working, groups):
    whole = lambda array: pl.BlockSpec(array.shape, lambda i, mine: (0, 0))
    outs = [jax.ShapeDtypeStruct((groups * ROOM * PAIRS // 2, LAGS), jnp.bfloat16)] * 2
    return list(pl.pallas_call(
        functools.partial(settle_kernel, groups),
        grid_spec=pltpu.PrefetchScalarGridSpec(
            num_scalar_prefetch=1,
            grid=(1,),
            in_specs=[whole(array) for array in [owners, *partials]],
            out_specs=[whole(array) for array in outs],
        ),
        out_shape=outs,
        compiler_params=pltpu.CompilerParams(vmem_limit_bytes=VMEM_LIMIT),
        name="settle",
    )(jnp.stack([mine, working]), owners, *partials))


def bundle_kernel(kept_ref, brought_ref, *out_refs):
    deep = ROOM * PAIRS
    for j, out_ref in enumerate(out_refs):
        out_ref[:deep] = kept_ref[j * deep : (j + 1) * deep]
        out_ref[deep:] = brought_ref[j * deep : (j + 1) * deep]


def bundle(kept, brought):
    count = kept.shape[0] // (ROOM * PAIRS)
    return list(pl.pallas_call(
        bundle_kernel,
        out_shape=[jax.ShapeDtypeStruct((2 * ROOM * PAIRS, LAGS), jnp.bfloat16)] * count,
        compiler_params=pltpu.CompilerParams(vmem_limit_bytes=VMEM_LIMIT),
        name="bundle",
    )(kept, brought))


def widen_kernel(mine_ref, *refs):
    part_refs, out_ref = refs[:-1], refs[-1]
    for j, part_ref in enumerate(part_refs):
        values = part_ref[...].astype(jnp.float32)
        for side in range(2):
            first = jnp.bitwise_xor(mine_ref[0], 2 * j + side) * MOST
            for r in range(MOST):
                at = (side * ROOM + r) * PAIRS
                out_ref[first + r] = values[at : at + PAIRS]


def widen(pieces, mine):
    shape = (2 * len(pieces) * MOST, PAIRS, LAGS)
    return pl.pallas_call(
        widen_kernel,
        grid_spec=pltpu.PrefetchScalarGridSpec(
            num_scalar_prefetch=1,
            grid=(1,),
            in_specs=[pl.BlockSpec(array.shape, lambda i, mine: (0, 0)) for array in pieces],
            out_specs=pl.BlockSpec(shape, lambda i, mine: (0, 0, 0)),
        ),
        out_shape=jax.ShapeDtypeStruct(shape, jnp.float32),
        compiler_params=pltpu.CompilerParams(vmem_limit_bytes=VMEM_LIMIT),
        name="widen",
    )(mine[None], *pieces)


def local(spectra, pair_blocks, owners):
    groups = lax.axis_size("grp")
    parts = lax.axis_size("chan")
    place = lax.axis_index("chan")
    chunks = F // LANES // (parts // 2)
    rank = lax.shift_right_logical(place, 1)
    working = jnp.bitwise_and(jnp.bitwise_xor(place, rank), 1)

    def swap(array, d, back):
        pairs = [(i, i ^ d) for i in range(parts) if works(i if back else i ^ d)]
        return lax.ppermute(array, "chan", pairs)

    def exchange(panels):
        moved = {d: swap(panels[d], d, False) for d in sequence(parts)[:-1]}
        return panels[:1] + [moved[d] for d in range(1, parts)]

    first, second = whiten(spectra, pair_blocks[0, 0].T, place, parts)
    first = exchange(first)
    table = tables(rank, chunks)
    gates = [d for d in sequence(parts)[:2] if d]
    here, second = lax.optimization_barrier(([first[d] for d in gates], second))
    for d, panel in zip(gates, here):
        first[d] = panel
    second = exchange(second)

    order = list(reversed(range(parts)))
    halves = (order[: parts // 2], order[parts // 2 :])
    sums = [correlate(first, table, place, parts, wanted, 0, None) for wanted in halves]
    ordered, sums = lax.optimization_barrier(([second[d] for d in sequence(parts)], sums))
    for d, panel in zip(sequence(parts), ordered):
        second[d] = panel
    partials = []
    for wanted, before in zip(halves, sums):
        for d, rows in zip(wanted, correlate(second, table, place, parts, wanted, 1, before)):
            partials.append(swap(rows, d, True) if d else rows)
    mine = lax.axis_index("grp")

    def trade(array, m):
        return lax.ppermute(array, "grp", [(i, i ^ m) for i in range(groups)])

    kept, cross = settle(owners[0, 0].T, partials, mine, working, groups)
    pieces = bundle(kept, trade(cross, 1))
    for j in reversed(range(1, groups // 2)):
        pieces[j] = trade(pieces[j], 2 * j)
    return widen(pieces, mine)[None, None]


def solution(mesh):
    return jax.shard_map(
        local,
        mesh=mesh,
        in_specs=(
            P(("grp", "chan"), None, None, None),
            P("grp", "chan", None, None),
            P("grp", "chan", None, None),
        ),
        out_specs=P("grp", "chan", None, None, None),
        check_vma=False,
    )
```

```python
import functools

import jax
import jax.numpy as jnp
import numpy as np
from jax import lax
from jax.experimental import pallas as pl
from jax.experimental.pallas import tpu as pltpu
from jax.sharding import PartitionSpec as P

F = 8192
LAGS = 1024
BLK = 2
NB_SRC = 18
MOST = 3
WINDOWS = 2
LANES = 128
PAIRS = BLK * BLK
VMEM_LIMIT = 24 * 1024 * 1024
HALF = LAGS // 2
ROOM = 4
WAVES = (0, 2, 3, 4)


def works(place):
    return bool((place ^ (place >> 1)) & 1)


def whiten_kernel(parts, place_ref, spec_ref, pairs_ref, *out_refs):
    blocks = F // LANES
    each = blocks // (parts // 2)
    bounds = [each * quarter // 4 for quarter in WAVES]
    place = place_ref[0]

    def values(start):
        span = pl.ds(start, LANES)
        re = spec_ref[0, :, span].astype(jnp.float32)
        im = spec_ref[1, :, span].astype(jnp.float32)
        return re, im, re * re + im * im

    shape = (spec_ref.shape[1], LANES)
    line = lax.broadcasted_iota(jnp.int32, shape, 0)
    spare = jnp.zeros((1, LANES - NB_SRC), jnp.int32)
    wide = lambda row: jnp.broadcast_to(jnp.concatenate([row, spare], axis=1), shape)
    notes = jnp.where(line == 0, wide(pairs_ref[0:1]), wide(pairs_ref[1:2]))
    notes = notes.astype(jnp.float32).astype(jnp.bfloat16)
    for out_ref in out_refs[:parts]:
        out_ref[:, bounds[1] * 2 * LANES :] = notes
    sums = [None] * 4
    for k in range(blocks):
        power = values(k * LANES)[2]
        sums[k % 4] = power if k < 4 else sums[k % 4] + power
    total = jnp.sum((sums[0] + sums[1]) + (sums[2] + sums[3]), axis=1, keepdims=True)
    level = 0.1 * (total * (1.0 / F) + 1e-05)
    for index, out_ref in enumerate(out_refs):
        wave, d = divmod(index, parts)
        first = lax.shift_right_logical(jnp.bitwise_xor(place, d), 1) * each + bounds[wave]
        for k in range(bounds[wave + 1] - bounds[wave]):
            re, im, power = values(pl.multiple_of((first + k) * LANES, LANES))
            scale = lax.rsqrt(power + level)
            at = k * 2 * LANES
            out_ref[:, at : at + LANES] = (re * scale).astype(jnp.bfloat16)
            out_ref[:, at + LANES : at + 2 * LANES] = (im * scale).astype(jnp.bfloat16)


def whiten(spectra, pairs, place, parts):
    rows = spectra.shape[0] * WINDOWS
    planes = jnp.transpose(spectra.reshape(rows, 2, F), (1, 0, 2))
    width = 2 * F // (parts // 2)
    bounds = [width * quarter // 4 for quarter in WAVES]
    shapes = []
    for wave in range(len(WAVES) - 1):
        shapes += [(rows, bounds[wave + 1] - bounds[wave] + (0 if wave else LANES))] * parts
    whole = lambda array: pl.BlockSpec(array.shape, lambda i, place: (0,) * array.ndim)
    outs = pl.pallas_call(
        functools.partial(whiten_kernel, parts),
        grid_spec=pltpu.PrefetchScalarGridSpec(
            num_scalar_prefetch=1,
            grid=(1,),
            in_specs=[whole(array) for array in [planes, pairs]],
            out_specs=[pl.BlockSpec(shape, lambda i, place: (0, 0)) for shape in shapes],
        ),
        out_shape=[jax.ShapeDtypeStruct(shape, jnp.bfloat16) for shape in shapes],
        compiler_params=pltpu.CompilerParams(vmem_limit_bytes=VMEM_LIMIT),
        name="whiten",
    )(place[None], planes, pairs)
    return [list(outs[i : i + parts]) for i in range(0, len(outs), parts)]


def table_kernel(first_ref, hi_cos_ref, hi_sin_ref, mid_cos_ref, mid_sin_ref, lo_cos_ref, lo_sin_ref, out_ref, cos, sin):
    s = pl.program_id(0)
    few = lo_cos_ref.shape[0]

    @pl.when(s == 0)
    def combine():
        lo_cos = lo_cos_ref[...]
        lo_sin = lo_sin_ref[...]
        for i in range(LANES // few):
            mid_cos = mid_cos_ref[i : i + 1]
            mid_sin = mid_sin_ref[i : i + 1]
            cos[i * few : (i + 1) * few] = mid_cos * lo_cos - mid_sin * lo_sin
            sin[i * few : (i + 1) * few] = mid_sin * lo_cos + mid_cos * lo_sin

    hi_cos = hi_cos_ref[pl.ds(s, 1), :]
    hi_sin = hi_sin_ref[pl.ds(s, 1), :]
    minus_cos = -hi_cos
    for i in range(0, LANES, 16):
        lo_cos = cos[i : i + 16]
        lo_sin = sin[i : i + 16]
        out_ref[i : i + 16, :HALF] = (hi_cos * lo_cos - hi_sin * lo_sin).astype(jnp.bfloat16)
        out_ref[i : i + 16, HALF:] = (minus_cos * lo_sin - hi_sin * lo_cos).astype(jnp.bfloat16)

    @pl.when(jnp.logical_and(first_ref[0] == 0, s == 0))
    def zero_bin():
        row = lax.broadcasted_iota(jnp.int32, (16, HALF), 0)
        weight = jnp.where(row == 0, 0.5, 1.0)
        out_ref[0:16, :HALF] = ((hi_cos * cos[0:16] - hi_sin * sin[0:16]) * weight).astype(jnp.bfloat16)


def tables(place, chunks):
    lag = jnp.arange(HALF, dtype=jnp.int32)
    few = 8
    middle = LANES // few
    bins = jnp.concatenate([
        (place * chunks + jnp.arange(chunks, dtype=jnp.int32)) * LANES,
        jnp.arange(middle, dtype=jnp.int32) * few,
        jnp.arange(few, dtype=jnp.int32),
    ])
    phase = bins[:, None] * lag[None, :] % (2 * F)
    angle = phase.astype(jnp.float32) * (jnp.pi / F)
    cos = jnp.cos(angle)
    sin = jnp.sin(angle)
    unit = 2.0 / jnp.sqrt(jnp.float32(F))
    cuts = [slice(0, chunks), slice(chunks, chunks + middle), slice(chunks + middle, None)]
    operands = [cos[cuts[0]] * unit, sin[cuts[0]] * unit, cos[cuts[1]], sin[cuts[1]], cos[cuts[2]], sin[cuts[2]]]
    return pl.pallas_call(
        table_kernel,
        grid_spec=pltpu.PrefetchScalarGridSpec(
            num_scalar_prefetch=1,
            grid=(chunks,),
            in_specs=[pl.BlockSpec(array.shape, lambda s, first: (0, 0)) for array in operands],
            out_specs=pl.BlockSpec((LANES, LAGS), lambda s, first: (s, 0)),
            scratch_shapes=[pltpu.VMEM((LANES, HALF), jnp.float32)] * 2,
        ),
        out_shape=jax.ShapeDtypeStruct((chunks * LANES, LAGS), jnp.bfloat16),
        cost_estimate=pl.CostEstimate(
            flops=chunks * LANES * LAGS * 4, bytes_accessed=chunks * LANES * LAGS * 2, transcendentals=0
        ),
        compiler_params=pltpu.CompilerParams(vmem_limit_bytes=VMEM_LIMIT),
        name="tables",
    )(place[None], *operands)


def iota(shape, axis):
    return lax.broadcasted_iota(jnp.int32, shape, axis)


def ones(hit):
    return hit.astype(jnp.float32).astype(jnp.bfloat16)


def choose_rows(lists, place, packed, rows_ref):
    height = rows_ref.shape[1]
    count = rows_ref.shape[0] // (2 * BLK * WINDOWS)
    deep = packed.shape[0] // lists
    blocks = deep // (BLK * WINDOWS)
    line = iota((count, 1), 0)
    group = jnp.zeros_like(line)
    for z in range(1, lists):
        group = group + jnp.where(line >= z * NB_SRC, 1, 0)
    here = iota((count, LANES), 1) == line - group * NB_SRC

    def column(kind):
        row = ones(iota((count, packed.shape[0]), 1) == group * deep + kind)
        found = jnp.dot(row, packed, preferred_element_type=jnp.float32)
        return jnp.sum(jnp.where(here, found, 0.0), axis=1, keepdims=True).astype(jnp.int32)

    across = iota((count, height), 1)
    picks = []
    for block in (column(0), column(1)):
        first = jnp.bitwise_xor(block, place * blocks) * (BLK * WINDOWS)
        for offset in range(BLK * WINDOWS):
            picks.append((across == first + offset).astype(jnp.float32))
    rows_ref[...] = jnp.concatenate(picks, axis=0).astype(jnp.bfloat16)


def sequence(parts):
    order = list(reversed(range(parts)))
    return [order[0], order[-2], *order[1:-2], order[-1]]


def corr_kernel(per_step, parts, lists, wave, place, *refs):
    last = wave == len(WAVES) - 2
    panel_refs, (table_ref, ends_ref), refs = dict(zip(sequence(parts), refs)), refs[parts : parts + 2], refs[parts + 2 :]
    step = pl.program_id(0)
    if wave:
        (total_in, edge_in, rows_ref), out_refs, (total, edge) = refs[:3], refs[3:-2], refs[-2:]
    else:
        note_refs, (total, edge, rows_ref) = refs[:lists], refs[lists:]

        @pl.when(step == 0)
        def prepare():
            choose_rows(lists, place[0], jnp.concatenate([ref[...] for ref in note_refs]), rows_ref)

    count = total.shape[0] // PAIRS
    panel = jnp.concatenate([panel_refs[d][...] for d in range(parts)])
    chosen = jnp.dot(rows_ref[...], panel, preferred_element_type=jnp.float32)

    def row(side, channel, window, start):
        first = ((side * BLK + channel) * WINDOWS + window) * count
        return chosen[first : first + count, start : start + LANES]

    reals = []
    imags = []
    lane = iota((1, LANES), 1)
    first_bin = jnp.logical_and(jnp.logical_and(place[0] < 2, step == 0), lane == 0)
    edge_part = 0.0
    for i in range(per_step):
        at = i * 2 * LANES
        real = []
        imag = []
        for p in range(BLK):
            for q in range(BLK):
                re = 0.0
                im = 0.0
                for w in range(WINDOWS):
                    ra, ia = row(0, p, w, at), row(0, p, w, at + LANES)
                    rb, ib = row(1, q, w, at), row(1, q, w, at + LANES)
                    re = re + (ra * rb + ia * ib)
                    im = im + (ia * rb - ra * ib)
                real.append(re * (1.0 / WINDOWS))
                imag.append(im * (1.0 / WINDOWS))
        real = jnp.concatenate(real, axis=0)
        imag = jnp.concatenate(imag, axis=0)
        ends = ends_ref[0:1]
        if i == 0 and wave == 0:
            ends = jnp.where(first_bin, 0.5 * ends, ends)
        edge_part = edge_part + (real * ends + imag * ends_ref[1:2])
        reals.append(real.astype(jnp.bfloat16))
        imags.append(imag.astype(jnp.bfloat16))

    def transform(pieces, columns):
        rows = jnp.concatenate(pieces, axis=1)
        return jnp.dot(rows, table_ref[:, columns], preferred_element_type=jnp.float32)

    even = transform(reals, slice(0, HALF))
    odd = transform(imags, slice(HALF, LAGS))

    @pl.when(step == 0)
    def start():
        total[:, :HALF] = total_in[:, :HALF] + even if wave else even
        total[:, HALF:] = total_in[:, HALF:] + odd if wave else odd
        edge[...] = edge_in[...] + edge_part if wave else edge_part

    @pl.when(step > 0)
    def add():
        total[:, :HALF] += even
        total[:, HALF:] += odd
        edge[...] += edge_part

    if not last:
        return

    @pl.when(step == pl.num_programs(0) - 1)
    def finish():
        even = total[:, :HALF]
        odd = total[:, HALF:]
        later = (even + odd).astype(jnp.bfloat16)
        mirror = ones(iota((HALF, HALF), 0) + iota((HALF, HALF), 1) == HALF)
        sooner = jnp.dot((even - odd).astype(jnp.bfloat16), mirror, preferred_element_type=jnp.float32)
        least = jnp.sum(edge[...], axis=1, keepdims=True)
        sooner = jnp.where(iota(sooner.shape, 1) == 0, least, sooner).astype(jnp.bfloat16)
        each = NB_SRC * PAIRS
        shape = (each * len(out_refs), PAIRS * count)
        column = iota(shape, 1)
        number = column * PAIRS
        for n in range(1, PAIRS):
            number = number - jnp.where(column >= n * count, count * PAIRS - 1, 0)
        order = ones(iota(shape, 0) == number)
        both = jnp.concatenate([sooner, later], axis=1)
        rows = jnp.dot(order, both, preferred_element_type=jnp.float32)
        for i, out_ref in enumerate(out_refs):
            out_ref[...] = rows[i * each : (i + 1) * each].astype(jnp.bfloat16)


def correlate(panels, table, place, parts, wanted, wave, before):
    chunks = table.shape[0] // LANES
    per_step = min(4, chunks // 4)
    span = per_step * 2 * LANES
    rows = panels[0].shape[0]
    base = chunks * WAVES[wave] // 4 // per_step
    steps = chunks * WAVES[wave + 1] // 4 // per_step - base
    lists = len(wanted)
    count = -(-lists * NB_SRC // 8) * 8
    each = NB_SRC * PAIRS
    turn = np.arange(LANES) * (np.pi / 16)
    ends = np.stack([np.cos(turn), np.sin(turn)]) * (2.0 / np.sqrt(F))
    sums = [
        jax.ShapeDtypeStruct((count * PAIRS, LAGS), jnp.float32),
        jax.ShapeDtypeStruct((count * PAIRS, LANES), jnp.float32),
    ]
    chosen = jax.ShapeDtypeStruct((2 * BLK * WINDOWS * count, rows * parts), jnp.bfloat16)
    whole = lambda array: pl.BlockSpec(array.shape, lambda i, place: (0, 0))
    if wave:
        extra = before
        extra_specs = [whole(array) for array in before]
        last = wave == len(WAVES) - 2
        outs = [jax.ShapeDtypeStruct((each, LAGS), jnp.bfloat16)] * lists if last else sums
        scratch = [pltpu.VMEM(array.shape, array.dtype) for array in sums] if last else []
    else:
        extra = [panels[d] for d in wanted]
        extra_specs = [pl.BlockSpec((rows, LANES), lambda i, place: (0, steps * span // LANES))] * lists
        outs = [*sums, chosen]
        scratch = []
    return pl.pallas_call(
        functools.partial(corr_kernel, per_step, parts, lists, wave),
        grid_spec=pltpu.PrefetchScalarGridSpec(
            num_scalar_prefetch=1,
            grid=(steps,),
            in_specs=[
                *[pl.BlockSpec((rows, span), lambda i, place: (0, i))] * parts,
                pl.BlockSpec((span // 2, LAGS), lambda i, place: (i + base, 0)),
                pl.BlockSpec((2, LANES), lambda i, place: (0, 0)),
                *extra_specs,
            ],
            out_specs=[whole(array) for array in outs],
            scratch_shapes=scratch,
        ),
        out_shape=outs,
        compiler_params=pltpu.CompilerParams(vmem_limit_bytes=VMEM_LIMIT),
        cost_estimate=pl.CostEstimate(
            flops=count * PAIRS * steps * span * LAGS,
            bytes_accessed=steps * span * LAGS,
            transcendentals=0,
        ),
        name="correlate",
    )(place[None], *[panels[d] for d in sequence(parts)], table, jnp.asarray(ends, jnp.float32), *extra)


def settle_kernel(groups, mine_ref, owners_ref, *refs):
    part_refs, out_refs = refs[:-2], refs[-2:]
    rows = groups * ROOM * PAIRS
    slots = rows // PAIRS
    each = NB_SRC * PAIRS
    tall = 24
    spare = jnp.full((1, LANES - NB_SRC), rows, jnp.int32)
    owner = jnp.concatenate([owners_ref[...], spare], axis=1)
    wide = jnp.broadcast_to(owner, (tall, LANES)).astype(jnp.float32)
    line, lane = iota((tall, LANES), 0), iota((tall, LANES), 1)
    other = jnp.sum(jnp.where(line == lane, wide, 0.0), axis=1, keepdims=True)
    earlier = jnp.logical_and(other == wide, line < lane).astype(jnp.float32)
    rank = jnp.sum(earlier, axis=0, keepdims=True)
    turn = jnp.bitwise_xor(owner, mine_ref[0])
    block = lax.shift_right_logical(turn, 1) + jnp.bitwise_and(turn, 1) * (groups // 2)
    slot = jnp.where(owner < groups, block, rows).astype(jnp.float32) * ROOM + rank
    held = ones(iota((slots, LANES), 0).astype(jnp.float32) == slot)
    down = ones(lax.shift_right_logical(iota((rows, slots), 0), 2) == iota((rows, slots), 1))
    over = ones(lax.shift_right_logical(iota((LANES, each), 1), 2) == iota((LANES, each), 0))
    block = jnp.dot(down, held, preferred_element_type=jnp.float32).astype(jnp.bfloat16)
    block = jnp.dot(block, over, preferred_element_type=jnp.float32)
    same = jnp.bitwise_and(iota((rows, each), 0), PAIRS - 1) == jnp.bitwise_and(iota((rows, each), 1), PAIRS - 1)
    chosen = jnp.where(same, block, 0.0).astype(jnp.bfloat16)
    total = jnp.where(mine_ref[1] == 1, part_refs[-1][...].astype(jnp.float32), 0.0)
    for ref in part_refs[:-1]:
        total = total + ref[...].astype(jnp.float32)
    placed = jnp.dot(chosen, total.astype(jnp.bfloat16), preferred_element_type=jnp.float32)
    for i, out_ref in enumerate(out_refs):
        out_ref[...] = placed[i * rows // 2 : (i + 1) * rows // 2].astype(jnp.bfloat16)


def settle(owners, partials, mine, working, groups):
    whole = lambda array: pl.BlockSpec(array.shape, lambda i, mine: (0, 0))
    outs = [jax.ShapeDtypeStruct((groups * ROOM * PAIRS // 2, LAGS), jnp.bfloat16)] * 2
    return list(pl.pallas_call(
        functools.partial(settle_kernel, groups),
        grid_spec=pltpu.PrefetchScalarGridSpec(
            num_scalar_prefetch=1,
            grid=(1,),
            in_specs=[whole(array) for array in [owners, *partials]],
            out_specs=[whole(array) for array in outs],
        ),
        out_shape=outs,
        compiler_params=pltpu.CompilerParams(vmem_limit_bytes=VMEM_LIMIT),
        name="settle",
    )(jnp.stack([mine, working]), owners, *partials))


def bundle_kernel(kept_ref, brought_ref, *out_refs):
    deep = ROOM * PAIRS
    for j, out_ref in enumerate(out_refs):
        out_ref[:deep] = kept_ref[j * deep : (j + 1) * deep]
        out_ref[deep:] = brought_ref[j * deep : (j + 1) * deep]


def bundle(kept, brought):
    count = kept.shape[0] // (ROOM * PAIRS)
    return list(pl.pallas_call(
        bundle_kernel,
        out_shape=[jax.ShapeDtypeStruct((2 * ROOM * PAIRS, LAGS), jnp.bfloat16)] * count,
        compiler_params=pltpu.CompilerParams(vmem_limit_bytes=VMEM_LIMIT),
        name="bundle",
    )(kept, brought))


def widen_kernel(mine_ref, *refs):
    part_refs, out_ref = refs[:-1], refs[-1]
    for j, part_ref in enumerate(part_refs):
        values = part_ref[...].astype(jnp.float32)
        for side in range(2):
            first = jnp.bitwise_xor(mine_ref[0], 2 * j + side) * MOST
            for r in range(MOST):
                at = (side * ROOM + r) * PAIRS
                out_ref[first + r] = values[at : at + PAIRS]


def widen(pieces, mine):
    shape = (2 * len(pieces) * MOST, PAIRS, LAGS)
    return pl.pallas_call(
        widen_kernel,
        grid_spec=pltpu.PrefetchScalarGridSpec(
            num_scalar_prefetch=1,
            grid=(1,),
            in_specs=[pl.BlockSpec(array.shape, lambda i, mine: (0, 0)) for array in pieces],
            out_specs=pl.BlockSpec(shape, lambda i, mine: (0, 0, 0)),
        ),
        out_shape=jax.ShapeDtypeStruct(shape, jnp.float32),
        compiler_params=pltpu.CompilerParams(vmem_limit_bytes=VMEM_LIMIT),
        name="widen",
    )(mine[None], *pieces)


def local(spectra, pair_blocks, owners):
    groups = lax.axis_size("grp")
    parts = lax.axis_size("chan")
    place = lax.axis_index("chan")
    chunks = F // LANES // (parts // 2)
    rank = lax.shift_right_logical(place, 1)
    working = jnp.bitwise_and(jnp.bitwise_xor(place, rank), 1)

    def swap(array, d, back):
        pairs = [(i, i ^ d) for i in range(parts) if works(i if back else i ^ d)]
        return lax.ppermute(array, "chan", pairs)

    def exchange(panels):
        moved = {d: swap(panels[d], d, False) for d in sequence(parts)[:-1]}
        return panels[:1] + [moved[d] for d in range(1, parts)]

    def hold(panels, other):
        ordered, other = lax.optimization_barrier(([panels[d] for d in sequence(parts)], other))
        held = dict(zip(sequence(parts), ordered))
        return [held[d] for d in range(parts)], other

    first, second, third = whiten(spectra, pair_blocks[0, 0].T, place, parts)
    first = exchange(first)
    table = tables(rank, chunks)
    second, table = hold(second, table)
    second = exchange(second)
    order = list(reversed(range(parts)))
    halves = (order[: parts // 2], order[parts // 2 :])
    sums = [correlate(first, table, place, parts, halves[0], 0, None)]
    third, sums = hold(third, sums)
    third = exchange(third)
    sums.append(correlate(first, table, place, parts, halves[1], 0, None))
    second, sums = hold(second, sums)
    sums = [
        [*correlate(second, table, place, parts, wanted, 1, before), before[2]]
        for wanted, before in zip(halves, sums)
    ]
    third, sums = hold(third, sums)
    partials = []
    for wanted, before in zip(halves, sums):
        for d, rows in zip(wanted, correlate(third, table, place, parts, wanted, 2, before)):
            partials.append(swap(rows, d, True) if d else rows)
    mine = lax.axis_index("grp")

    def trade(array, m):
        return lax.ppermute(array, "grp", [(i, i ^ m) for i in range(groups)])

    kept, cross = settle(owners[0, 0].T, partials, mine, working, groups)
    pieces = bundle(kept, trade(cross, 1))
    for j in reversed(range(1, groups // 2)):
        pieces[j] = trade(pieces[j], 2 * j)
    return widen(pieces, mine)[None, None]


def solution(mesh):
    return jax.shard_map(
        local,
        mesh=mesh,
        in_specs=(
            P(("grp", "chan"), None, None, None),
            P("grp", "chan", None, None),
            P("grp", "chan", None, None),
        ),
        out_specs=P("grp", "chan", None, None, None),
        check_vma=False,
    )
```

```python
import functools

import jax
import jax.numpy as jnp
import numpy as np
from jax import lax
from jax.experimental import pallas as pl
from jax.experimental.pallas import tpu as pltpu
from jax.sharding import PartitionSpec as P

F = 8192
LAGS = 1024
BLK = 2
NB_SRC = 18
MOST = 3
WINDOWS = 2
LANES = 128
PAIRS = BLK * BLK
VMEM_LIMIT = 24 * 1024 * 1024
HALF = LAGS // 2
ROOM = 4
WAVES = 2
LATE = 2


def whiten_kernel(parts, place_ref, spec_ref, pairs_ref, *out_refs):
    blocks = F // LANES
    each = blocks // parts
    late = each // LATE
    place = place_ref[0]

    def values(start):
        span = pl.ds(start, LANES)
        re = spec_ref[0, :, span].astype(jnp.float32)
        im = spec_ref[1, :, span].astype(jnp.float32)
        return re, im, re * re + im * im

    shape = (spec_ref.shape[1], LANES)
    line = lax.broadcasted_iota(jnp.int32, shape, 0)
    spare = jnp.zeros((1, LANES - NB_SRC), jnp.int32)
    wide = lambda row: jnp.broadcast_to(jnp.concatenate([row, spare], axis=1), shape)
    notes = jnp.where(line == 0, wide(pairs_ref[0:1]), wide(pairs_ref[1:2]))
    notes = notes.astype(jnp.float32).astype(jnp.bfloat16)
    for out_ref in out_refs[:parts]:
        out_ref[:, (each - late) * 2 * LANES :] = notes
    sums = [None] * 4
    for k in range(blocks):
        power = values(k * LANES)[2]
        sums[k % 4] = power if k < 4 else sums[k % 4] + power
    total = jnp.sum((sums[0] + sums[1]) + (sums[2] + sums[3]), axis=1, keepdims=True)
    level = 0.1 * (total * (1.0 / F) + 1e-05)
    for index, out_ref in enumerate(out_refs):
        wave, d = divmod(index, parts)
        first = jnp.bitwise_xor(place, d) * each + wave * (each - late)
        for k in range(late if wave else each - late):
            re, im, power = values(pl.multiple_of((first + k) * LANES, LANES))
            scale = lax.rsqrt(power + level)
            at = k * 2 * LANES
            out_ref[:, at : at + LANES] = (re * scale).astype(jnp.bfloat16)
            out_ref[:, at + LANES : at + 2 * LANES] = (im * scale).astype(jnp.bfloat16)


def whiten(spectra, pairs, place, parts):
    rows = spectra.shape[0] * WINDOWS
    planes = jnp.transpose(spectra.reshape(rows, 2, F), (1, 0, 2))
    width = 2 * F // parts
    late = width // LATE
    shapes = [(rows, width - late + LANES)] * parts + [(rows, late)] * parts
    whole = lambda array: pl.BlockSpec(array.shape, lambda i, place: (0,) * array.ndim)
    outs = pl.pallas_call(
        functools.partial(whiten_kernel, parts),
        grid_spec=pltpu.PrefetchScalarGridSpec(
            num_scalar_prefetch=1,
            grid=(1,),
            in_specs=[whole(array) for array in [planes, pairs]],
            out_specs=[pl.BlockSpec(shape, lambda i, place: (0, 0)) for shape in shapes],
        ),
        out_shape=[jax.ShapeDtypeStruct(shape, jnp.bfloat16) for shape in shapes],
        compiler_params=pltpu.CompilerParams(vmem_limit_bytes=VMEM_LIMIT),
        name="whiten",
    )(place[None], planes, pairs)
    return list(outs[:parts]), list(outs[parts:])


def table_kernel(first_ref, hi_cos_ref, hi_sin_ref, mid_cos_ref, mid_sin_ref, lo_cos_ref, lo_sin_ref, out_ref, cos, sin):
    s = pl.program_id(0)
    few = lo_cos_ref.shape[0]

    @pl.when(s == 0)
    def combine():
        lo_cos = lo_cos_ref[...]
        lo_sin = lo_sin_ref[...]
        for i in range(LANES // few):
            mid_cos = mid_cos_ref[i : i + 1]
            mid_sin = mid_sin_ref[i : i + 1]
            cos[i * few : (i + 1) * few] = mid_cos * lo_cos - mid_sin * lo_sin
            sin[i * few : (i + 1) * few] = mid_sin * lo_cos + mid_cos * lo_sin

    hi_cos = hi_cos_ref[pl.ds(s, 1), :]
    hi_sin = hi_sin_ref[pl.ds(s, 1), :]
    minus_cos = -hi_cos
    for i in range(0, LANES, 16):
        lo_cos = cos[i : i + 16]
        lo_sin = sin[i : i + 16]
        out_ref[i : i + 16, :HALF] = (hi_cos * lo_cos - hi_sin * lo_sin).astype(jnp.bfloat16)
        out_ref[i : i + 16, HALF:] = (minus_cos * lo_sin - hi_sin * lo_cos).astype(jnp.bfloat16)

    @pl.when(jnp.logical_and(first_ref[0] == 0, s == 0))
    def zero_bin():
        row = lax.broadcasted_iota(jnp.int32, (16, HALF), 0)
        weight = jnp.where(row == 0, 0.5, 1.0)
        out_ref[0:16, :HALF] = ((hi_cos * cos[0:16] - hi_sin * sin[0:16]) * weight).astype(jnp.bfloat16)


def tables(place, chunks):
    lag = jnp.arange(HALF, dtype=jnp.int32)
    few = 8
    middle = LANES // few
    bins = jnp.concatenate([
        (place * chunks + jnp.arange(chunks, dtype=jnp.int32)) * LANES,
        jnp.arange(middle, dtype=jnp.int32) * few,
        jnp.arange(few, dtype=jnp.int32),
    ])
    phase = bins[:, None] * lag[None, :] % (2 * F)
    angle = phase.astype(jnp.float32) * (jnp.pi / F)
    cos = jnp.cos(angle)
    sin = jnp.sin(angle)
    unit = 2.0 / jnp.sqrt(jnp.float32(F))
    cuts = [slice(0, chunks), slice(chunks, chunks + middle), slice(chunks + middle, None)]
    operands = [cos[cuts[0]] * unit, sin[cuts[0]] * unit, cos[cuts[1]], sin[cuts[1]], cos[cuts[2]], sin[cuts[2]]]
    return pl.pallas_call(
        table_kernel,
        grid_spec=pltpu.PrefetchScalarGridSpec(
            num_scalar_prefetch=1,
            grid=(chunks,),
            in_specs=[pl.BlockSpec(array.shape, lambda s, first: (0, 0)) for array in operands],
            out_specs=pl.BlockSpec((LANES, LAGS), lambda s, first: (s, 0)),
            scratch_shapes=[pltpu.VMEM((LANES, HALF), jnp.float32)] * 2,
        ),
        out_shape=jax.ShapeDtypeStruct((chunks * LANES, LAGS), jnp.bfloat16),
        cost_estimate=pl.CostEstimate(
            flops=chunks * LANES * LAGS * 4, bytes_accessed=chunks * LANES * LAGS * 2, transcendentals=0
        ),
        compiler_params=pltpu.CompilerParams(vmem_limit_bytes=VMEM_LIMIT),
        name="tables",
    )(place[None], *operands)


def iota(shape, axis):
    return lax.broadcasted_iota(jnp.int32, shape, axis)


def ones(hit):
    return hit.astype(jnp.float32).astype(jnp.bfloat16)


def choose_rows(lists, place, packed, rows_ref):
    height = rows_ref.shape[1]
    count = rows_ref.shape[0] // (2 * BLK * WINDOWS)
    deep = packed.shape[0] // lists
    blocks = deep // (BLK * WINDOWS)
    line = iota((count, 1), 0)
    group = jnp.zeros_like(line)
    for z in range(1, lists):
        group = group + jnp.where(line >= z * NB_SRC, 1, 0)
    here = iota((count, LANES), 1) == line - group * NB_SRC

    def column(kind):
        row = ones(iota((count, packed.shape[0]), 1) == group * deep + kind)
        found = jnp.dot(row, packed, preferred_element_type=jnp.float32)
        return jnp.sum(jnp.where(here, found, 0.0), axis=1, keepdims=True).astype(jnp.int32)

    across = iota((count, height), 1)
    picks = []
    for block in (column(0), column(1)):
        first = jnp.bitwise_xor(block, place * blocks) * (BLK * WINDOWS)
        for offset in range(BLK * WINDOWS):
            picks.append((across == first + offset).astype(jnp.float32))
    rows_ref[...] = jnp.concatenate(picks, axis=0).astype(jnp.bfloat16)


def sequence(parts):
    order = list(reversed(range(parts)))
    return [order[0], order[-2], *order[1:-2], order[-1]]


def corr_kernel(per_step, parts, lists, wave, place, *refs):
    panel_refs, (table_ref, ends_ref), refs = dict(zip(sequence(parts), refs)), refs[parts : parts + 2], refs[parts + 2 :]
    step = pl.program_id(0)
    if wave:
        (total_in, edge_in, rows_ref), out_refs, (total, edge) = refs[:3], refs[3:-2], refs[-2:]
    else:
        note_refs, (total, edge, rows_ref) = refs[:lists], refs[lists:]

        @pl.when(step == 0)
        def prepare():
            choose_rows(lists, place[0], jnp.concatenate([ref[...] for ref in note_refs]), rows_ref)

    count = total.shape[0] // PAIRS
    panel = jnp.concatenate([panel_refs[d][...] for d in range(parts)])
    chosen = jnp.dot(rows_ref[...], panel, preferred_element_type=jnp.float32)

    def row(side, channel, window, start):
        first = ((side * BLK + channel) * WINDOWS + window) * count
        return chosen[first : first + count, start : start + LANES]

    reals = []
    imags = []
    lane = iota((1, LANES), 1)
    first_bin = jnp.logical_and(jnp.logical_and(place[0] == 0, step == 0), lane == 0)
    edge_part = 0.0
    for i in range(per_step):
        at = i * 2 * LANES
        real = []
        imag = []
        for p in range(BLK):
            for q in range(BLK):
                re = 0.0
                im = 0.0
                for w in range(WINDOWS):
                    ra, ia = row(0, p, w, at), row(0, p, w, at + LANES)
                    rb, ib = row(1, q, w, at), row(1, q, w, at + LANES)
                    re = re + (ra * rb + ia * ib)
                    im = im + (ia * rb - ra * ib)
                real.append(re * (1.0 / WINDOWS))
                imag.append(im * (1.0 / WINDOWS))
        real = jnp.concatenate(real, axis=0)
        imag = jnp.concatenate(imag, axis=0)
        ends = ends_ref[0:1]
        if i == 0 and wave == 0:
            ends = jnp.where(first_bin, 0.5 * ends, ends)
        edge_part = edge_part + (real * ends + imag * ends_ref[1:2])
        reals.append(real.astype(jnp.bfloat16))
        imags.append(imag.astype(jnp.bfloat16))

    def transform(pieces, columns):
        rows = jnp.concatenate(pieces, axis=1)
        return jnp.dot(rows, table_ref[:, columns], preferred_element_type=jnp.float32)

    even = transform(reals, slice(0, HALF))
    odd = transform(imags, slice(HALF, LAGS))

    @pl.when(step == 0)
    def start():
        total[:, :HALF] = total_in[:, :HALF] + even if wave else even
        total[:, HALF:] = total_in[:, HALF:] + odd if wave else odd
        edge[...] = edge_in[...] + edge_part if wave else edge_part

    @pl.when(step > 0)
    def add():
        total[:, :HALF] += even
        total[:, HALF:] += odd
        edge[...] += edge_part

    if wave < WAVES - 1:
        return

    @pl.when(step == pl.num_programs(0) - 1)
    def finish():
        even = total[:, :HALF]
        odd = total[:, HALF:]
        later = (even + odd).astype(jnp.bfloat16)
        mirror = ones(iota((HALF, HALF), 0) + iota((HALF, HALF), 1) == HALF)
        sooner = jnp.dot((even - odd).astype(jnp.bfloat16), mirror, preferred_element_type=jnp.float32)
        least = jnp.sum(edge[...], axis=1, keepdims=True)
        sooner = jnp.where(iota(sooner.shape, 1) == 0, least, sooner).astype(jnp.bfloat16)
        each = NB_SRC * PAIRS
        shape = (each * len(out_refs), PAIRS * count)
        column = iota(shape, 1)
        number = column * PAIRS
        for n in range(1, PAIRS):
            number = number - jnp.where(column >= n * count, count * PAIRS - 1, 0)
        order = ones(iota(shape, 0) == number)
        both = jnp.concatenate([sooner, later], axis=1)
        rows = jnp.dot(order, both, preferred_element_type=jnp.float32)
        for i, out_ref in enumerate(out_refs):
            out_ref[...] = rows[i * each : (i + 1) * each].astype(jnp.bfloat16)


def correlate(panels, table, place, parts, wanted, wave, before):
    chunks = table.shape[0] // LANES
    per_step = min(4, chunks // LATE)
    span = per_step * 2 * LANES
    rows = panels[0].shape[0]
    late = chunks // LATE // per_step
    early = chunks // per_step - late
    steps = late if wave else early
    lists = len(wanted)
    count = -(-lists * NB_SRC // 8) * 8
    each = NB_SRC * PAIRS
    turn = np.arange(LANES) * (np.pi / 16)
    ends = np.stack([np.cos(turn), np.sin(turn)]) * (2.0 / np.sqrt(F))
    sums = [
        jax.ShapeDtypeStruct((count * PAIRS, LAGS), jnp.float32),
        jax.ShapeDtypeStruct((count * PAIRS, LANES), jnp.float32),
    ]
    chosen = jax.ShapeDtypeStruct((2 * BLK * WINDOWS * count, rows * parts), jnp.bfloat16)
    whole = lambda array: pl.BlockSpec(array.shape, lambda i, place: (0, 0))
    if wave:
        extra = before
        extra_specs = [whole(array) for array in before]
        outs = [jax.ShapeDtypeStruct((each, LAGS), jnp.bfloat16)] * lists
        scratch = [pltpu.VMEM(array.shape, array.dtype) for array in sums]
    else:
        extra = [panels[d] for d in wanted]
        extra_specs = [pl.BlockSpec((rows, LANES), lambda i, place: (0, steps * span // LANES))] * lists
        outs = [*sums, chosen]
        scratch = []
    return pl.pallas_call(
        functools.partial(corr_kernel, per_step, parts, lists, wave),
        grid_spec=pltpu.PrefetchScalarGridSpec(
            num_scalar_prefetch=1,
            grid=(steps,),
            in_specs=[
                *[pl.BlockSpec((rows, span), lambda i, place: (0, i))] * parts,
                pl.BlockSpec((span // 2, LAGS), lambda i, place: (i + wave * early, 0)),
                pl.BlockSpec((2, LANES), lambda i, place: (0, 0)),
                *extra_specs,
            ],
            out_specs=[whole(array) for array in outs],
            scratch_shapes=scratch,
        ),
        out_shape=outs,
        compiler_params=pltpu.CompilerParams(vmem_limit_bytes=VMEM_LIMIT),
        cost_estimate=pl.CostEstimate(
            flops=count * PAIRS * steps * span * LAGS,
            bytes_accessed=steps * span * LAGS,
            transcendentals=0,
        ),
        name="correlate",
    )(place[None], *[panels[d] for d in sequence(parts)], table, jnp.asarray(ends, jnp.float32), *extra)


def settle_kernel(groups, mine_ref, owners_ref, *refs):
    part_refs, out_refs = refs[:-2], refs[-2:]
    rows = groups * ROOM * PAIRS
    slots = rows // PAIRS
    each = NB_SRC * PAIRS
    tall = 24
    spare = jnp.full((1, LANES - NB_SRC), rows, jnp.int32)
    owner = jnp.concatenate([owners_ref[...], spare], axis=1)
    wide = jnp.broadcast_to(owner, (tall, LANES)).astype(jnp.float32)
    line, lane = iota((tall, LANES), 0), iota((tall, LANES), 1)
    other = jnp.sum(jnp.where(line == lane, wide, 0.0), axis=1, keepdims=True)
    earlier = jnp.logical_and(other == wide, line < lane).astype(jnp.float32)
    rank = jnp.sum(earlier, axis=0, keepdims=True)
    turn = jnp.bitwise_xor(owner, mine_ref[0])
    block = lax.shift_right_logical(turn, 1) + jnp.bitwise_and(turn, 1) * (groups // 2)
    slot = jnp.where(owner < groups, block, rows).astype(jnp.float32) * ROOM + rank
    held = ones(iota((slots, LANES), 0).astype(jnp.float32) == slot)
    down = ones(lax.shift_right_logical(iota((rows, slots), 0), 2) == iota((rows, slots), 1))
    over = ones(lax.shift_right_logical(iota((LANES, each), 1), 2) == iota((LANES, each), 0))
    block = jnp.dot(down, held, preferred_element_type=jnp.float32).astype(jnp.bfloat16)
    block = jnp.dot(block, over, preferred_element_type=jnp.float32)
    same = jnp.bitwise_and(iota((rows, each), 0), PAIRS - 1) == jnp.bitwise_and(iota((rows, each), 1), PAIRS - 1)
    chosen = jnp.where(same, block, 0.0).astype(jnp.bfloat16)
    total = sum(ref[...].astype(jnp.float32) for ref in part_refs)
    placed = jnp.dot(chosen, total.astype(jnp.bfloat16), preferred_element_type=jnp.float32)
    for i, out_ref in enumerate(out_refs):
        out_ref[...] = placed[i * rows // 2 : (i + 1) * rows // 2].astype(jnp.bfloat16)


def settle(owners, partials, mine, groups):
    whole = lambda array: pl.BlockSpec(array.shape, lambda i, mine: (0, 0))
    outs = [jax.ShapeDtypeStruct((groups * ROOM * PAIRS // 2, LAGS), jnp.bfloat16)] * 2
    return list(pl.pallas_call(
        functools.partial(settle_kernel, groups),
        grid_spec=pltpu.PrefetchScalarGridSpec(
            num_scalar_prefetch=1,
            grid=(1,),
            in_specs=[whole(array) for array in [owners, *partials]],
            out_specs=[whole(array) for array in outs],
        ),
        out_shape=outs,
        compiler_params=pltpu.CompilerParams(vmem_limit_bytes=VMEM_LIMIT),
        name="settle",
    )(mine[None], owners, *partials))


def bundle_kernel(kept_ref, brought_ref, *out_refs):
    deep = ROOM * PAIRS
    for j, out_ref in enumerate(out_refs):
        out_ref[:deep] = kept_ref[j * deep : (j + 1) * deep]
        out_ref[deep:] = brought_ref[j * deep : (j + 1) * deep]


def bundle(kept, brought):
    count = kept.shape[0] // (ROOM * PAIRS)
    return list(pl.pallas_call(
        bundle_kernel,
        out_shape=[jax.ShapeDtypeStruct((2 * ROOM * PAIRS, LAGS), jnp.bfloat16)] * count,
        compiler_params=pltpu.CompilerParams(vmem_limit_bytes=VMEM_LIMIT),
        name="bundle",
    )(kept, brought))


def widen_kernel(mine_ref, *refs):
    part_refs, out_ref = refs[:-1], refs[-1]
    for j, part_ref in enumerate(part_refs):
        values = part_ref[...].astype(jnp.float32)
        for side in range(2):
            first = jnp.bitwise_xor(mine_ref[0], 2 * j + side) * MOST
            for r in range(MOST):
                at = (side * ROOM + r) * PAIRS
                out_ref[first + r] = values[at : at + PAIRS]


def widen(pieces, mine):
    shape = (2 * len(pieces) * MOST, PAIRS, LAGS)
    return pl.pallas_call(
        widen_kernel,
        grid_spec=pltpu.PrefetchScalarGridSpec(
            num_scalar_prefetch=1,
            grid=(1,),
            in_specs=[pl.BlockSpec(array.shape, lambda i, mine: (0, 0)) for array in pieces],
            out_specs=pl.BlockSpec(shape, lambda i, mine: (0, 0, 0)),
        ),
        out_shape=jax.ShapeDtypeStruct(shape, jnp.float32),
        compiler_params=pltpu.CompilerParams(vmem_limit_bytes=VMEM_LIMIT),
        name="widen",
    )(mine[None], *pieces)


def local(spectra, pair_blocks, owners):
    groups = lax.axis_size("grp")
    parts = lax.axis_size("chan")
    place = lax.axis_index("chan")
    chunks = F // LANES // parts

    def swap(array, d):
        return lax.ppermute(array, "chan", [(i, i ^ d) for i in range(parts)])

    def exchange(panels):
        moved = {d: swap(panels[d], d) for d in sequence(parts)[:-1]}
        return panels[:1] + [moved[d] for d in range(1, parts)]

    first, second = whiten(spectra, pair_blocks[0, 0].T, place, parts)
    first = exchange(first)
    table = tables(place, chunks)
    gates = [d for d in sequence(parts)[:2] if d]
    here, second = lax.optimization_barrier(([first[d] for d in gates], second))
    for d, panel in zip(gates, here):
        first[d] = panel
    second = exchange(second)

    order = list(reversed(range(parts)))
    halves = (order[:1], order[1:])
    sums = [correlate(first, table, place, parts, wanted, 0, None) for wanted in halves]
    ordered, sums = lax.optimization_barrier(([second[d] for d in sequence(parts)], sums))
    for d, panel in zip(sequence(parts), ordered):
        second[d] = panel
    partials = []
    for wanted, before in zip(halves, sums):
        for d, rows in zip(wanted, correlate(second, table, place, parts, wanted, 1, before)):
            partials.append(swap(rows, d) if d else rows)
    mine = lax.axis_index("grp")

    def trade(array, m):
        return lax.ppermute(array, "grp", [(i, i ^ m) for i in range(groups)])

    kept, cross = settle(owners[0, 0].T, partials, mine, groups)
    pieces = bundle(kept, trade(cross, 1))
    for j in reversed(range(1, groups // 2)):
        pieces[j] = trade(pieces[j], 2 * j)
    return widen(pieces, mine)[None, None]


def solution(mesh):
    return jax.shard_map(
        local,
        mesh=mesh,
        in_specs=(
            P(("grp", "chan"), None, None, None),
            P("grp", "chan", None, None),
            P("grp", "chan", None, None),
        ),
        out_specs=P("grp", "chan", None, None, None),
        check_vma=False,
    )
```

```python
import functools

import jax
import jax.numpy as jnp
import numpy as np
from jax import lax
from jax.experimental import pallas as pl
from jax.experimental.pallas import tpu as pltpu
from jax.sharding import PartitionSpec as P

F = 8192
LAGS = 1024
BLK = 2
NB_SRC = 18
MOST = 3
WINDOWS = 2
LANES = 128
PAIRS = BLK * BLK
VMEM_LIMIT = 24 * 1024 * 1024
HALF = LAGS // 2
ROOM = 4
WAVES = 2
LATE = 2


def whiten_kernel(parts, place_ref, spec_ref, pairs_ref, *out_refs):
    blocks = F // LANES
    each = blocks // parts
    late = each // LATE
    place = place_ref[0]

    def values(start):
        span = pl.ds(start, LANES)
        re = spec_ref[0, :, span].astype(jnp.float32)
        im = spec_ref[1, :, span].astype(jnp.float32)
        return re, im, re * re + im * im

    shape = (spec_ref.shape[1], LANES)
    line = lax.broadcasted_iota(jnp.int32, shape, 0)
    spare = jnp.zeros((1, LANES - NB_SRC), jnp.int32)
    wide = lambda row: jnp.broadcast_to(jnp.concatenate([row, spare], axis=1), shape)
    notes = jnp.where(line == 0, wide(pairs_ref[0:1]), wide(pairs_ref[1:2]))
    notes = notes.astype(jnp.float32).astype(jnp.bfloat16)
    for out_ref in out_refs[:parts]:
        out_ref[:, (each - late) * 2 * LANES :] = notes
    sums = [None] * 4
    for k in range(blocks):
        power = values(k * LANES)[2]
        sums[k % 4] = power if k < 4 else sums[k % 4] + power
    total = jnp.sum((sums[0] + sums[1]) + (sums[2] + sums[3]), axis=1, keepdims=True)
    level = 0.1 * (total * (1.0 / F) + 1e-05)
    for index, out_ref in enumerate(out_refs):
        wave, d = divmod(index, parts)
        first = jnp.bitwise_xor(place, d) * each + wave * (each - late)
        for k in range(late if wave else each - late):
            re, im, power = values(pl.multiple_of((first + k) * LANES, LANES))
            scale = lax.rsqrt(power + level)
            at = k * 2 * LANES
            out_ref[:, at : at + LANES] = (re * scale).astype(jnp.bfloat16)
            out_ref[:, at + LANES : at + 2 * LANES] = (im * scale).astype(jnp.bfloat16)


def whiten(spectra, pairs, place, parts):
    rows = spectra.shape[0] * WINDOWS
    planes = jnp.transpose(spectra.reshape(rows, 2, F), (1, 0, 2))
    width = 2 * F // parts
    late = width // LATE
    shapes = [(rows, width - late + LANES)] * parts + [(rows, late)] * parts
    whole = lambda array: pl.BlockSpec(array.shape, lambda i, place: (0,) * array.ndim)
    outs = pl.pallas_call(
        functools.partial(whiten_kernel, parts),
        grid_spec=pltpu.PrefetchScalarGridSpec(
            num_scalar_prefetch=1,
            grid=(1,),
            in_specs=[whole(array) for array in [planes, pairs]],
            out_specs=[pl.BlockSpec(shape, lambda i, place: (0, 0)) for shape in shapes],
        ),
        out_shape=[jax.ShapeDtypeStruct(shape, jnp.bfloat16) for shape in shapes],
        compiler_params=pltpu.CompilerParams(vmem_limit_bytes=VMEM_LIMIT),
        name="whiten",
    )(place[None], planes, pairs)
    return list(outs[:parts]), list(outs[parts:])


def table_kernel(first_ref, hi_cos_ref, hi_sin_ref, mid_cos_ref, mid_sin_ref, lo_cos_ref, lo_sin_ref, out_ref, cos, sin):
    s = pl.program_id(0)
    few = lo_cos_ref.shape[0]

    @pl.when(s == 0)
    def combine():
        lo_cos = lo_cos_ref[...]
        lo_sin = lo_sin_ref[...]
        for i in range(LANES // few):
            mid_cos = mid_cos_ref[i : i + 1]
            mid_sin = mid_sin_ref[i : i + 1]
            cos[i * few : (i + 1) * few] = mid_cos * lo_cos - mid_sin * lo_sin
            sin[i * few : (i + 1) * few] = mid_sin * lo_cos + mid_cos * lo_sin

    hi_cos = hi_cos_ref[pl.ds(s, 1), :]
    hi_sin = hi_sin_ref[pl.ds(s, 1), :]
    minus_cos = -hi_cos
    for i in range(0, LANES, 16):
        lo_cos = cos[i : i + 16]
        lo_sin = sin[i : i + 16]
        out_ref[i : i + 16, :HALF] = (hi_cos * lo_cos - hi_sin * lo_sin).astype(jnp.bfloat16)
        out_ref[i : i + 16, HALF:] = (minus_cos * lo_sin - hi_sin * lo_cos).astype(jnp.bfloat16)

    @pl.when(jnp.logical_and(first_ref[0] == 0, s == 0))
    def zero_bin():
        row = lax.broadcasted_iota(jnp.int32, (16, HALF), 0)
        weight = jnp.where(row == 0, 0.5, 1.0)
        out_ref[0:16, :HALF] = ((hi_cos * cos[0:16] - hi_sin * sin[0:16]) * weight).astype(jnp.bfloat16)


def tables(place, chunks):
    lag = jnp.arange(HALF, dtype=jnp.int32)
    few = 8
    middle = LANES // few
    bins = jnp.concatenate([
        (place * chunks + jnp.arange(chunks, dtype=jnp.int32)) * LANES,
        jnp.arange(middle, dtype=jnp.int32) * few,
        jnp.arange(few, dtype=jnp.int32),
    ])
    phase = bins[:, None] * lag[None, :] % (2 * F)
    angle = phase.astype(jnp.float32) * (jnp.pi / F)
    cos = jnp.cos(angle)
    sin = jnp.sin(angle)
    unit = 2.0 / jnp.sqrt(jnp.float32(F))
    cuts = [slice(0, chunks), slice(chunks, chunks + middle), slice(chunks + middle, None)]
    operands = [cos[cuts[0]] * unit, sin[cuts[0]] * unit, cos[cuts[1]], sin[cuts[1]], cos[cuts[2]], sin[cuts[2]]]
    return pl.pallas_call(
        table_kernel,
        grid_spec=pltpu.PrefetchScalarGridSpec(
            num_scalar_prefetch=1,
            grid=(chunks,),
            in_specs=[pl.BlockSpec(array.shape, lambda s, first: (0, 0)) for array in operands],
            out_specs=pl.BlockSpec((LANES, LAGS), lambda s, first: (s, 0)),
            scratch_shapes=[pltpu.VMEM((LANES, HALF), jnp.float32)] * 2,
        ),
        out_shape=jax.ShapeDtypeStruct((chunks * LANES, LAGS), jnp.bfloat16),
        cost_estimate=pl.CostEstimate(
            flops=chunks * LANES * LAGS * 4, bytes_accessed=chunks * LANES * LAGS * 2, transcendentals=0
        ),
        compiler_params=pltpu.CompilerParams(vmem_limit_bytes=VMEM_LIMIT),
        name="tables",
    )(place[None], *operands)


def iota(shape, axis):
    return lax.broadcasted_iota(jnp.int32, shape, axis)


def ones(hit):
    return hit.astype(jnp.float32).astype(jnp.bfloat16)


def choose_rows(lists, place, packed, rows_ref):
    height = rows_ref.shape[1]
    count = rows_ref.shape[0] // (2 * BLK * WINDOWS)
    deep = packed.shape[0] // lists
    blocks = deep // (BLK * WINDOWS)
    line = iota((count, 1), 0)
    group = jnp.zeros_like(line)
    for z in range(1, lists):
        group = group + jnp.where(line >= z * NB_SRC, 1, 0)
    here = iota((count, LANES), 1) == line - group * NB_SRC

    def column(kind):
        row = ones(iota((count, packed.shape[0]), 1) == group * deep + kind)
        found = jnp.dot(row, packed, preferred_element_type=jnp.float32)
        return jnp.sum(jnp.where(here, found, 0.0), axis=1, keepdims=True).astype(jnp.int32)

    across = iota((count, height), 1)
    picks = []
    for block in (column(0), column(1)):
        first = jnp.bitwise_xor(block, place * blocks) * (BLK * WINDOWS)
        for offset in range(BLK * WINDOWS):
            picks.append((across == first + offset).astype(jnp.float32))
    rows_ref[...] = jnp.concatenate(picks, axis=0).astype(jnp.bfloat16)


def sequence(parts):
    order = list(reversed(range(parts)))
    return [order[0], order[-2], *order[1:-2], order[-1]]


def corr_kernel(per_step, parts, lists, wave, place, *refs):
    panel_refs, (table_ref, ends_ref), refs = dict(zip(sequence(parts), refs)), refs[parts : parts + 2], refs[parts + 2 :]
    step = pl.program_id(0)
    if wave:
        (total_in, edge_in, rows_ref), out_refs, (total, edge) = refs[:3], refs[3:-2], refs[-2:]
    else:
        note_refs, (total, edge, rows_ref) = refs[:lists], refs[lists:]

        @pl.when(step == 0)
        def prepare():
            choose_rows(lists, place[0], jnp.concatenate([ref[...] for ref in note_refs]), rows_ref)

    count = total.shape[0] // PAIRS
    panel = jnp.concatenate([panel_refs[d][...] for d in range(parts)])
    chosen = jnp.dot(rows_ref[...], panel, preferred_element_type=jnp.float32)

    def row(side, channel, window, start):
        first = ((side * BLK + channel) * WINDOWS + window) * count
        return chosen[first : first + count, start : start + LANES]

    reals = []
    imags = []
    lane = iota((1, LANES), 1)
    first_bin = jnp.logical_and(jnp.logical_and(place[0] == 0, step == 0), lane == 0)
    edge_part = 0.0
    for i in range(per_step):
        at = i * 2 * LANES
        real = []
        imag = []
        for p in range(BLK):
            for q in range(BLK):
                re = 0.0
                im = 0.0
                for w in range(WINDOWS):
                    ra, ia = row(0, p, w, at), row(0, p, w, at + LANES)
                    rb, ib = row(1, q, w, at), row(1, q, w, at + LANES)
                    re = re + (ra * rb + ia * ib)
                    im = im + (ia * rb - ra * ib)
                real.append(re * (1.0 / WINDOWS))
                imag.append(im * (1.0 / WINDOWS))
        real = jnp.concatenate(real, axis=0)
        imag = jnp.concatenate(imag, axis=0)
        ends = ends_ref[0:1]
        if i == 0 and wave == 0:
            ends = jnp.where(first_bin, 0.5 * ends, ends)
        edge_part = edge_part + (real * ends + imag * ends_ref[1:2])
        reals.append(real.astype(jnp.bfloat16))
        imags.append(imag.astype(jnp.bfloat16))

    def transform(pieces, columns):
        rows = jnp.concatenate(pieces, axis=1)
        return jnp.dot(rows, table_ref[:, columns], preferred_element_type=jnp.float32)

    even = transform(reals, slice(0, HALF))
    odd = transform(imags, slice(HALF, LAGS))

    @pl.when(step == 0)
    def start():
        total[:, :HALF] = total_in[:, :HALF] + even if wave else even
        total[:, HALF:] = total_in[:, HALF:] + odd if wave else odd
        edge[...] = edge_in[...] + edge_part if wave else edge_part

    @pl.when(step > 0)
    def add():
        total[:, :HALF] += even
        total[:, HALF:] += odd
        edge[...] += edge_part

    if wave < WAVES - 1:
        return

    @pl.when(step == pl.num_programs(0) - 1)
    def finish():
        even = total[:, :HALF]
        odd = total[:, HALF:]
        later = (even + odd).astype(jnp.bfloat16)
        mirror = ones(iota((HALF, HALF), 0) + iota((HALF, HALF), 1) == HALF)
        sooner = jnp.dot((even - odd).astype(jnp.bfloat16), mirror, preferred_element_type=jnp.float32)
        least = jnp.sum(edge[...], axis=1, keepdims=True)
        sooner = jnp.where(iota(sooner.shape, 1) == 0, least, sooner).astype(jnp.bfloat16)
        each = NB_SRC * PAIRS
        shape = (each * len(out_refs), PAIRS * count)
        column = iota(shape, 1)
        number = column * PAIRS
        for n in range(1, PAIRS):
            number = number - jnp.where(column >= n * count, count * PAIRS - 1, 0)
        order = ones(iota(shape, 0) == number)
        both = jnp.concatenate([sooner, later], axis=1)
        rows = jnp.dot(order, both, preferred_element_type=jnp.float32)
        for i, out_ref in enumerate(out_refs):
            out_ref[...] = rows[i * each : (i + 1) * each].astype(jnp.bfloat16)


def correlate(panels, table, place, parts, wanted, wave, before):
    chunks = table.shape[0] // LANES
    per_step = min(4, chunks // LATE)
    span = per_step * 2 * LANES
    rows = panels[0].shape[0]
    late = chunks // LATE // per_step
    early = chunks // per_step - late
    steps = late if wave else early
    lists = len(wanted)
    count = -(-lists * NB_SRC // 8) * 8
    each = NB_SRC * PAIRS
    turn = np.arange(LANES) * (np.pi / 16)
    ends = np.stack([np.cos(turn), np.sin(turn)]) * (2.0 / np.sqrt(F))
    sums = [
        jax.ShapeDtypeStruct((count * PAIRS, LAGS), jnp.float32),
        jax.ShapeDtypeStruct((count * PAIRS, LANES), jnp.float32),
    ]
    chosen = jax.ShapeDtypeStruct((2 * BLK * WINDOWS * count, rows * parts), jnp.bfloat16)
    whole = lambda array: pl.BlockSpec(array.shape, lambda i, place: (0, 0))
    if wave:
        extra = before
        extra_specs = [whole(array) for array in before]
        outs = [jax.ShapeDtypeStruct((each, LAGS), jnp.bfloat16)] * lists
        scratch = [pltpu.VMEM(array.shape, array.dtype) for array in sums]
    else:
        extra = [panels[d] for d in wanted]
        extra_specs = [pl.BlockSpec((rows, LANES), lambda i, place: (0, steps * span // LANES))] * lists
        outs = [*sums, chosen]
        scratch = []
    return pl.pallas_call(
        functools.partial(corr_kernel, per_step, parts, lists, wave),
        grid_spec=pltpu.PrefetchScalarGridSpec(
            num_scalar_prefetch=1,
            grid=(steps,),
            in_specs=[
                *[pl.BlockSpec((rows, span), lambda i, place: (0, i))] * parts,
                pl.BlockSpec((span // 2, LAGS), lambda i, place: (i + wave * early, 0)),
                pl.BlockSpec((2, LANES), lambda i, place: (0, 0)),
                *extra_specs,
            ],
            out_specs=[whole(array) for array in outs],
            scratch_shapes=scratch,
        ),
        out_shape=outs,
        compiler_params=pltpu.CompilerParams(vmem_limit_bytes=VMEM_LIMIT),
        cost_estimate=pl.CostEstimate(
            flops=count * PAIRS * steps * span * LAGS,
            bytes_accessed=steps * span * LAGS,
            transcendentals=0,
        ),
        name="correlate",
    )(place[None], *[panels[d] for d in sequence(parts)], table, jnp.asarray(ends, jnp.float32), *extra)


def settle_kernel(groups, mine_ref, owners_ref, *refs):
    part_refs, out_refs = refs[:-2], refs[-2:]
    rows = groups * ROOM * PAIRS
    slots = rows // PAIRS
    each = NB_SRC * PAIRS
    tall = 24
    spare = jnp.full((1, LANES - NB_SRC), rows, jnp.int32)
    owner = jnp.concatenate([owners_ref[...], spare], axis=1)
    wide = jnp.broadcast_to(owner, (tall, LANES)).astype(jnp.float32)
    line, lane = iota((tall, LANES), 0), iota((tall, LANES), 1)
    other = jnp.sum(jnp.where(line == lane, wide, 0.0), axis=1, keepdims=True)
    earlier = jnp.logical_and(other == wide, line < lane).astype(jnp.float32)
    rank = jnp.sum(earlier, axis=0, keepdims=True)
    turn = jnp.bitwise_xor(owner, mine_ref[0])
    block = lax.shift_right_logical(turn, 1) + jnp.bitwise_and(turn, 1) * (groups // 2)
    slot = jnp.where(owner < groups, block, rows).astype(jnp.float32) * ROOM + rank
    held = ones(iota((slots, LANES), 0).astype(jnp.float32) == slot)
    down = ones(lax.shift_right_logical(iota((rows, slots), 0), 2) == iota((rows, slots), 1))
    over = ones(lax.shift_right_logical(iota((LANES, each), 1), 2) == iota((LANES, each), 0))
    block = jnp.dot(down, held, preferred_element_type=jnp.float32).astype(jnp.bfloat16)
    block = jnp.dot(block, over, preferred_element_type=jnp.float32)
    same = jnp.bitwise_and(iota((rows, each), 0), PAIRS - 1) == jnp.bitwise_and(iota((rows, each), 1), PAIRS - 1)
    chosen = jnp.where(same, block, 0.0).astype(jnp.bfloat16)
    total = sum(ref[...].astype(jnp.float32) for ref in part_refs)
    placed = jnp.dot(chosen, total.astype(jnp.bfloat16), preferred_element_type=jnp.float32)
    for i, out_ref in enumerate(out_refs):
        out_ref[...] = placed[i * rows // 2 : (i + 1) * rows // 2].astype(jnp.bfloat16)


def settle(owners, partials, mine, groups):
    whole = lambda array: pl.BlockSpec(array.shape, lambda i, mine: (0, 0))
    outs = [jax.ShapeDtypeStruct((groups * ROOM * PAIRS // 2, LAGS), jnp.bfloat16)] * 2
    return list(pl.pallas_call(
        functools.partial(settle_kernel, groups),
        grid_spec=pltpu.PrefetchScalarGridSpec(
            num_scalar_prefetch=1,
            grid=(1,),
            in_specs=[whole(array) for array in [owners, *partials]],
            out_specs=[whole(array) for array in outs],
        ),
        out_shape=outs,
        compiler_params=pltpu.CompilerParams(vmem_limit_bytes=VMEM_LIMIT),
        name="settle",
    )(mine[None], owners, *partials))


def bundle_kernel(kept_ref, brought_ref, *out_refs):
    deep = ROOM * PAIRS
    for j, out_ref in enumerate(out_refs):
        out_ref[:deep] = kept_ref[j * deep : (j + 1) * deep]
        out_ref[deep:] = brought_ref[j * deep : (j + 1) * deep]


def bundle(kept, brought):
    count = kept.shape[0] // (ROOM * PAIRS)
    return list(pl.pallas_call(
        bundle_kernel,
        out_shape=[jax.ShapeDtypeStruct((2 * ROOM * PAIRS, LAGS), jnp.bfloat16)] * count,
        compiler_params=pltpu.CompilerParams(vmem_limit_bytes=VMEM_LIMIT),
        name="bundle",
    )(kept, brought))


def widen_kernel(mine_ref, *refs):
    part_refs, out_ref = refs[:-1], refs[-1]
    for j, part_ref in enumerate(part_refs):
        values = part_ref[...].astype(jnp.float32)
        for side in range(2):
            first = jnp.bitwise_xor(mine_ref[0], 2 * j + side) * MOST
            for r in range(MOST):
                at = (side * ROOM + r) * PAIRS
                out_ref[first + r] = values[at : at + PAIRS]


def widen(pieces, mine):
    shape = (2 * len(pieces) * MOST, PAIRS, LAGS)
    return pl.pallas_call(
        widen_kernel,
        grid_spec=pltpu.PrefetchScalarGridSpec(
            num_scalar_prefetch=1,
            grid=(1,),
            in_specs=[pl.BlockSpec(array.shape, lambda i, mine: (0, 0)) for array in pieces],
            out_specs=pl.BlockSpec(shape, lambda i, mine: (0, 0, 0)),
        ),
        out_shape=jax.ShapeDtypeStruct(shape, jnp.float32),
        compiler_params=pltpu.CompilerParams(vmem_limit_bytes=VMEM_LIMIT),
        name="widen",
    )(mine[None], *pieces)


def local(spectra, pair_blocks, owners):
    groups = lax.axis_size("grp")
    parts = lax.axis_size("chan")
    place = lax.axis_index("chan")
    chunks = F // LANES // parts

    def swap(array, d):
        return lax.ppermute(array, "chan", [(i, i ^ d) for i in range(parts)])

    def exchange(panels):
        moved = {d: swap(panels[d], d) for d in sequence(parts)[:-1]}
        return panels[:1] + [moved[d] for d in range(1, parts)]

    first, second = whiten(spectra, pair_blocks[0, 0].T, place, parts)
    first = exchange(first)
    table = tables(place, chunks)
    gates = [d for d in sequence(parts)[:2] if d]
    here, second = lax.optimization_barrier(([first[d] for d in gates], second))
    for d, panel in zip(gates, here):
        first[d] = panel
    second = exchange(second)

    order = list(reversed(range(parts)))
    halves = (order[:1], order[1:])
    sums = [correlate(first, table, place, parts, wanted, 0, None) for wanted in halves]
    ordered, sums = lax.optimization_barrier(([second[d] for d in sequence(parts)], sums))
    for d, panel in zip(sequence(parts), ordered):
        second[d] = panel
    partials = []
    (foremost,) = correlate(second, table, place, parts, halves[0], 1, sums[0])
    foremost, before = lax.optimization_barrier((foremost, sums[1]))
    rest = correlate(second, table, place, parts, halves[1], 1, before)
    for d, rows in zip(order, [foremost, *rest]):
        partials.append(swap(rows, d) if d else rows)
    mine = lax.axis_index("grp")

    def trade(array, m):
        return lax.ppermute(array, "grp", [(i, i ^ m) for i in range(groups)])

    kept, cross = settle(owners[0, 0].T, partials, mine, groups)
    pieces = bundle(kept, trade(cross, 1))
    for j in reversed(range(1, groups // 2)):
        pieces[j] = trade(pieces[j], 2 * j)
    return widen(pieces, mine)[None, None]


def solution(mesh):
    return jax.shard_map(
        local,
        mesh=mesh,
        in_specs=(
            P(("grp", "chan"), None, None, None),
            P("grp", "chan", None, None),
            P("grp", "chan", None, None),
        ),
        out_specs=P("grp", "chan", None, None, None),
        check_vma=False,
    )
```

```python
import functools

import jax
import jax.numpy as jnp
import numpy as np
from jax import lax
from jax.experimental import pallas as pl
from jax.experimental.pallas import tpu as pltpu
from jax.sharding import PartitionSpec as P

F = 8192
LAGS = 1024
BLK = 2
NB_SRC = 18
MOST = 3
WINDOWS = 2
LANES = 128
PAIRS = BLK * BLK
VMEM_LIMIT = 24 * 1024 * 1024
HALF = LAGS // 2
ROOM = 4
WAVES = 2
LATE = 2


def whiten_kernel(parts, place_ref, spec_ref, pairs_ref, *out_refs):
    blocks = F // LANES
    each = blocks // parts
    late = each // LATE
    place = place_ref[0]

    def values(start):
        span = pl.ds(start, LANES)
        re = spec_ref[0, :, span].astype(jnp.float32)
        im = spec_ref[1, :, span].astype(jnp.float32)
        return re, im, re * re + im * im

    shape = (spec_ref.shape[1], LANES)
    line = lax.broadcasted_iota(jnp.int32, shape, 0)
    spare = jnp.zeros((1, LANES - NB_SRC), jnp.int32)
    wide = lambda row: jnp.broadcast_to(jnp.concatenate([row, spare], axis=1), shape)
    notes = jnp.where(line == 0, wide(pairs_ref[0:1]), wide(pairs_ref[1:2]))
    notes = notes.astype(jnp.float32).astype(jnp.bfloat16)
    for out_ref in out_refs[:parts]:
        out_ref[:, (each - late) * 2 * LANES :] = notes
    sums = [None] * 4
    for k in range(blocks):
        power = values(k * LANES)[2]
        sums[k % 4] = power if k < 4 else sums[k % 4] + power
    total = jnp.sum((sums[0] + sums[1]) + (sums[2] + sums[3]), axis=1, keepdims=True)
    level = 0.1 * (total * (1.0 / F) + 1e-05)
    for index, out_ref in enumerate(out_refs):
        wave, d = divmod(index, parts)
        first = jnp.bitwise_xor(place, d) * each + wave * (each - late)
        for k in range(late if wave else each - late):
            re, im, power = values(pl.multiple_of((first + k) * LANES, LANES))
            scale = lax.rsqrt(power + level)
            at = k * 2 * LANES
            out_ref[:, at : at + LANES] = (re * scale).astype(jnp.bfloat16)
            out_ref[:, at + LANES : at + 2 * LANES] = (im * scale).astype(jnp.bfloat16)


def whiten(spectra, pairs, place, parts):
    rows = spectra.shape[0] * WINDOWS
    planes = jnp.transpose(spectra.reshape(rows, 2, F), (1, 0, 2))
    width = 2 * F // parts
    late = width // LATE
    shapes = [(rows, width - late + LANES)] * parts + [(rows, late)] * parts
    whole = lambda array: pl.BlockSpec(array.shape, lambda i, place: (0,) * array.ndim)
    outs = pl.pallas_call(
        functools.partial(whiten_kernel, parts),
        grid_spec=pltpu.PrefetchScalarGridSpec(
            num_scalar_prefetch=1,
            grid=(1,),
            in_specs=[whole(array) for array in [planes, pairs]],
            out_specs=[pl.BlockSpec(shape, lambda i, place: (0, 0)) for shape in shapes],
        ),
        out_shape=[jax.ShapeDtypeStruct(shape, jnp.bfloat16) for shape in shapes],
        compiler_params=pltpu.CompilerParams(vmem_limit_bytes=VMEM_LIMIT),
        name="whiten",
    )(place[None], planes, pairs)
    return list(outs[:parts]), list(outs[parts:])


def table_kernel(first_ref, hi_cos_ref, hi_sin_ref, mid_cos_ref, mid_sin_ref, lo_cos_ref, lo_sin_ref, out_ref, cos, sin):
    s = pl.program_id(0)
    few = lo_cos_ref.shape[0]

    @pl.when(s == 0)
    def combine():
        lo_cos = lo_cos_ref[...]
        lo_sin = lo_sin_ref[...]
        for i in range(LANES // few):
            mid_cos = mid_cos_ref[i : i + 1]
            mid_sin = mid_sin_ref[i : i + 1]
            cos[i * few : (i + 1) * few] = mid_cos * lo_cos - mid_sin * lo_sin
            sin[i * few : (i + 1) * few] = mid_sin * lo_cos + mid_cos * lo_sin

    hi_cos = hi_cos_ref[pl.ds(s, 1), :]
    hi_sin = hi_sin_ref[pl.ds(s, 1), :]
    minus_cos = -hi_cos
    for i in range(0, LANES, 16):
        lo_cos = cos[i : i + 16]
        lo_sin = sin[i : i + 16]
        out_ref[i : i + 16, :HALF] = (hi_cos * lo_cos - hi_sin * lo_sin).astype(jnp.bfloat16)
        out_ref[i : i + 16, HALF:] = (minus_cos * lo_sin - hi_sin * lo_cos).astype(jnp.bfloat16)

    @pl.when(jnp.logical_and(first_ref[0] == 0, s == 0))
    def zero_bin():
        row = lax.broadcasted_iota(jnp.int32, (16, HALF), 0)
        weight = jnp.where(row == 0, 0.5, 1.0)
        out_ref[0:16, :HALF] = ((hi_cos * cos[0:16] - hi_sin * sin[0:16]) * weight).astype(jnp.bfloat16)


def tables(place, chunks):
    lag = jnp.arange(HALF, dtype=jnp.int32)
    few = 8
    middle = LANES // few
    bins = jnp.concatenate([
        (place * chunks + jnp.arange(chunks, dtype=jnp.int32)) * LANES,
        jnp.arange(middle, dtype=jnp.int32) * few,
        jnp.arange(few, dtype=jnp.int32),
    ])
    phase = bins[:, None] * lag[None, :] % (2 * F)
    angle = phase.astype(jnp.float32) * (jnp.pi / F)
    cos = jnp.cos(angle)
    sin = jnp.sin(angle)
    unit = 2.0 / jnp.sqrt(jnp.float32(F))
    cuts = [slice(0, chunks), slice(chunks, chunks + middle), slice(chunks + middle, None)]
    operands = [cos[cuts[0]] * unit, sin[cuts[0]] * unit, cos[cuts[1]], sin[cuts[1]], cos[cuts[2]], sin[cuts[2]]]
    return pl.pallas_call(
        table_kernel,
        grid_spec=pltpu.PrefetchScalarGridSpec(
            num_scalar_prefetch=1,
            grid=(chunks,),
            in_specs=[pl.BlockSpec(array.shape, lambda s, first: (0, 0)) for array in operands],
            out_specs=pl.BlockSpec((LANES, LAGS), lambda s, first: (s, 0)),
            scratch_shapes=[pltpu.VMEM((LANES, HALF), jnp.float32)] * 2,
        ),
        out_shape=jax.ShapeDtypeStruct((chunks * LANES, LAGS), jnp.bfloat16),
        cost_estimate=pl.CostEstimate(
            flops=chunks * LANES * LAGS * 4, bytes_accessed=chunks * LANES * LAGS * 2, transcendentals=0
        ),
        compiler_params=pltpu.CompilerParams(vmem_limit_bytes=VMEM_LIMIT),
        name="tables",
    )(place[None], *operands)


def iota(shape, axis):
    return lax.broadcasted_iota(jnp.int32, shape, axis)


def ones(hit):
    return hit.astype(jnp.float32).astype(jnp.bfloat16)


def choose_rows(lists, place, packed, rows_ref):
    height = rows_ref.shape[1]
    count = rows_ref.shape[0] // (2 * BLK * WINDOWS)
    deep = packed.shape[0] // lists
    blocks = deep // (BLK * WINDOWS)
    line = iota((count, 1), 0)
    group = jnp.zeros_like(line)
    for z in range(1, lists):
        group = group + jnp.where(line >= z * NB_SRC, 1, 0)
    here = iota((count, LANES), 1) == line - group * NB_SRC

    def column(kind):
        row = ones(iota((count, packed.shape[0]), 1) == group * deep + kind)
        found = jnp.dot(row, packed, preferred_element_type=jnp.float32)
        return jnp.sum(jnp.where(here, found, 0.0), axis=1, keepdims=True).astype(jnp.int32)

    across = iota((count, height), 1)
    picks = []
    for block in (column(0), column(1)):
        first = jnp.bitwise_xor(block, place * blocks) * (BLK * WINDOWS)
        for offset in range(BLK * WINDOWS):
            picks.append((across == first + offset).astype(jnp.float32))
    rows_ref[...] = jnp.concatenate(picks, axis=0).astype(jnp.bfloat16)


def sequence(parts):
    order = list(reversed(range(parts)))
    return [order[0], order[-2], *order[1:-2], order[-1]]


def corr_kernel(per_step, parts, lists, wave, place, *refs):
    panel_refs, (table_ref, ends_ref), refs = dict(zip(sequence(parts), refs)), refs[parts : parts + 2], refs[parts + 2 :]
    step = pl.program_id(0)
    if wave:
        (total_in, edge_in, rows_ref), out_refs, (total, edge) = refs[:3], refs[3:-2], refs[-2:]
    else:
        note_refs, (total, edge, rows_ref) = refs[:lists], refs[lists:]

        @pl.when(step == 0)
        def prepare():
            choose_rows(lists, place[0], jnp.concatenate([ref[...] for ref in note_refs]), rows_ref)

    count = total.shape[0] // PAIRS
    panel = jnp.concatenate([panel_refs[d][...] for d in range(parts)])
    chosen = jnp.dot(rows_ref[...], panel, preferred_element_type=jnp.float32)

    def row(side, channel, window, start):
        first = ((side * BLK + channel) * WINDOWS + window) * count
        return chosen[first : first + count, start : start + LANES]

    reals = []
    imags = []
    lane = iota((1, LANES), 1)
    first_bin = jnp.logical_and(jnp.logical_and(place[0] == 0, step == 0), lane == 0)
    edge_part = 0.0
    for i in range(per_step):
        at = i * 2 * LANES
        real = []
        imag = []
        for p in range(BLK):
            for q in range(BLK):
                re = 0.0
                im = 0.0
                for w in range(WINDOWS):
                    ra, ia = row(0, p, w, at), row(0, p, w, at + LANES)
                    rb, ib = row(1, q, w, at), row(1, q, w, at + LANES)
                    re = re + (ra * rb + ia * ib)
                    im = im + (ia * rb - ra * ib)
                real.append(re * (1.0 / WINDOWS))
                imag.append(im * (1.0 / WINDOWS))
        real = jnp.concatenate(real, axis=0)
        imag = jnp.concatenate(imag, axis=0)
        ends = ends_ref[0:1]
        if i == 0 and wave == 0:
            ends = jnp.where(first_bin, 0.5 * ends, ends)
        edge_part = edge_part + (real * ends + imag * ends_ref[1:2])
        reals.append(real.astype(jnp.bfloat16))
        imags.append(imag.astype(jnp.bfloat16))

    def transform(pieces, columns):
        rows = jnp.concatenate(pieces, axis=1)
        return jnp.dot(rows, table_ref[:, columns], preferred_element_type=jnp.float32)

    even = transform(reals, slice(0, HALF))
    odd = transform(imags, slice(HALF, LAGS))

    @pl.when(step == 0)
    def start():
        total[:, :HALF] = total_in[:, :HALF] + even if wave else even
        total[:, HALF:] = total_in[:, HALF:] + odd if wave else odd
        edge[...] = edge_in[...] + edge_part if wave else edge_part

    @pl.when(step > 0)
    def add():
        total[:, :HALF] += even
        total[:, HALF:] += odd
        edge[...] += edge_part

    if wave < WAVES - 1:
        return

    @pl.when(step == pl.num_programs(0) - 1)
    def finish():
        even = total[:, :HALF]
        odd = total[:, HALF:]
        later = (even + odd).astype(jnp.bfloat16)
        mirror = ones(iota((HALF, HALF), 0) + iota((HALF, HALF), 1) == HALF)
        sooner = jnp.dot((even - odd).astype(jnp.bfloat16), mirror, preferred_element_type=jnp.float32)
        least = jnp.sum(edge[...], axis=1, keepdims=True)
        sooner = jnp.where(iota(sooner.shape, 1) == 0, least, sooner).astype(jnp.bfloat16)
        each = NB_SRC * PAIRS
        shape = (each * len(out_refs), PAIRS * count)
        column = iota(shape, 1)
        number = column * PAIRS
        for n in range(1, PAIRS):
            number = number - jnp.where(column >= n * count, count * PAIRS - 1, 0)
        order = ones(iota(shape, 0) == number)
        both = jnp.concatenate([sooner, later], axis=1)
        rows = jnp.dot(order, both, preferred_element_type=jnp.float32)
        for i, out_ref in enumerate(out_refs):
            out_ref[...] = rows[i * each : (i + 1) * each].astype(jnp.bfloat16)


def correlate(panels, table, place, parts, wanted, wave, before):
    chunks = table.shape[0] // LANES
    per_step = min(8, chunks // LATE)
    span = per_step * 2 * LANES
    rows = panels[0].shape[0]
    late = chunks // LATE // per_step
    early = chunks // per_step - late
    steps = late if wave else early
    lists = len(wanted)
    count = -(-lists * NB_SRC // 8) * 8
    each = NB_SRC * PAIRS
    turn = np.arange(LANES) * (np.pi / 16)
    ends = np.stack([np.cos(turn), np.sin(turn)]) * (2.0 / np.sqrt(F))
    sums = [
        jax.ShapeDtypeStruct((count * PAIRS, LAGS), jnp.float32),
        jax.ShapeDtypeStruct((count * PAIRS, LANES), jnp.float32),
    ]
    chosen = jax.ShapeDtypeStruct((2 * BLK * WINDOWS * count, rows * parts), jnp.bfloat16)
    whole = lambda array: pl.BlockSpec(array.shape, lambda i, place: (0, 0))
    if wave:
        extra = before
        extra_specs = [whole(array) for array in before]
        outs = [jax.ShapeDtypeStruct((each, LAGS), jnp.bfloat16)] * lists
        scratch = [pltpu.VMEM(array.shape, array.dtype) for array in sums]
    else:
        extra = [panels[d] for d in wanted]
        extra_specs = [pl.BlockSpec((rows, LANES), lambda i, place: (0, steps * span // LANES))] * lists
        outs = [*sums, chosen]
        scratch = []
    return pl.pallas_call(
        functools.partial(corr_kernel, per_step, parts, lists, wave),
        grid_spec=pltpu.PrefetchScalarGridSpec(
            num_scalar_prefetch=1,
            grid=(steps,),
            in_specs=[
                *[pl.BlockSpec((rows, span), lambda i, place: (0, i))] * parts,
                pl.BlockSpec((span // 2, LAGS), lambda i, place: (i + wave * early, 0)),
                pl.BlockSpec((2, LANES), lambda i, place: (0, 0)),
                *extra_specs,
            ],
            out_specs=[whole(array) for array in outs],
            scratch_shapes=scratch,
        ),
        out_shape=outs,
        compiler_params=pltpu.CompilerParams(vmem_limit_bytes=VMEM_LIMIT),
        cost_estimate=pl.CostEstimate(
            flops=count * PAIRS * steps * span * LAGS,
            bytes_accessed=steps * span * LAGS,
            transcendentals=0,
        ),
        name="correlate",
    )(place[None], *[panels[d] for d in sequence(parts)], table, jnp.asarray(ends, jnp.float32), *extra)


def settle_kernel(groups, mine_ref, owners_ref, *refs):
    part_refs, out_refs = refs[:-2], refs[-2:]
    rows = groups * ROOM * PAIRS
    slots = rows // PAIRS
    each = NB_SRC * PAIRS
    tall = 24
    spare = jnp.full((1, LANES - NB_SRC), rows, jnp.int32)
    owner = jnp.concatenate([owners_ref[...], spare], axis=1)
    wide = jnp.broadcast_to(owner, (tall, LANES)).astype(jnp.float32)
    line, lane = iota((tall, LANES), 0), iota((tall, LANES), 1)
    other = jnp.sum(jnp.where(line == lane, wide, 0.0), axis=1, keepdims=True)
    earlier = jnp.logical_and(other == wide, line < lane).astype(jnp.float32)
    rank = jnp.sum(earlier, axis=0, keepdims=True)
    turn = jnp.bitwise_xor(owner, mine_ref[0])
    block = lax.shift_right_logical(turn, 1) + jnp.bitwise_and(turn, 1) * (groups // 2)
    slot = jnp.where(owner < groups, block, rows).astype(jnp.float32) * ROOM + rank
    held = ones(iota((slots, LANES), 0).astype(jnp.float32) == slot)
    down = ones(lax.shift_right_logical(iota((rows, slots), 0), 2) == iota((rows, slots), 1))
    over = ones(lax.shift_right_logical(iota((LANES, each), 1), 2) == iota((LANES, each), 0))
    block = jnp.dot(down, held, preferred_element_type=jnp.float32).astype(jnp.bfloat16)
    block = jnp.dot(block, over, preferred_element_type=jnp.float32)
    same = jnp.bitwise_and(iota((rows, each), 0), PAIRS - 1) == jnp.bitwise_and(iota((rows, each), 1), PAIRS - 1)
    chosen = jnp.where(same, block, 0.0).astype(jnp.bfloat16)
    total = sum(ref[...].astype(jnp.float32) for ref in part_refs)
    placed = jnp.dot(chosen, total.astype(jnp.bfloat16), preferred_element_type=jnp.float32)
    for i, out_ref in enumerate(out_refs):
        out_ref[...] = placed[i * rows // 2 : (i + 1) * rows // 2].astype(jnp.bfloat16)


def settle(owners, partials, mine, groups):
    whole = lambda array: pl.BlockSpec(array.shape, lambda i, mine: (0, 0))
    outs = [jax.ShapeDtypeStruct((groups * ROOM * PAIRS // 2, LAGS), jnp.bfloat16)] * 2
    return list(pl.pallas_call(
        functools.partial(settle_kernel, groups),
        grid_spec=pltpu.PrefetchScalarGridSpec(
            num_scalar_prefetch=1,
            grid=(1,),
            in_specs=[whole(array) for array in [owners, *partials]],
            out_specs=[whole(array) for array in outs],
        ),
        out_shape=outs,
        compiler_params=pltpu.CompilerParams(vmem_limit_bytes=VMEM_LIMIT),
        name="settle",
    )(mine[None], owners, *partials))


def bundle_kernel(kept_ref, brought_ref, *out_refs):
    deep = ROOM * PAIRS
    for j, out_ref in enumerate(out_refs):
        out_ref[:deep] = kept_ref[j * deep : (j + 1) * deep]
        out_ref[deep:] = brought_ref[j * deep : (j + 1) * deep]


def bundle(kept, brought):
    count = kept.shape[0] // (ROOM * PAIRS)
    return list(pl.pallas_call(
        bundle_kernel,
        out_shape=[jax.ShapeDtypeStruct((2 * ROOM * PAIRS, LAGS), jnp.bfloat16)] * count,
        compiler_params=pltpu.CompilerParams(vmem_limit_bytes=VMEM_LIMIT),
        name="bundle",
    )(kept, brought))


def widen_kernel(mine_ref, *refs):
    part_refs, out_ref = refs[:-1], refs[-1]
    for j, part_ref in enumerate(part_refs):
        values = part_ref[...].astype(jnp.float32)
        for side in range(2):
            first = jnp.bitwise_xor(mine_ref[0], 2 * j + side) * MOST
            for r in range(MOST):
                at = (side * ROOM + r) * PAIRS
                out_ref[first + r] = values[at : at + PAIRS]


def widen(pieces, mine):
    shape = (2 * len(pieces) * MOST, PAIRS, LAGS)
    return pl.pallas_call(
        widen_kernel,
        grid_spec=pltpu.PrefetchScalarGridSpec(
            num_scalar_prefetch=1,
            grid=(1,),
            in_specs=[pl.BlockSpec(array.shape, lambda i, mine: (0, 0)) for array in pieces],
            out_specs=pl.BlockSpec(shape, lambda i, mine: (0, 0, 0)),
        ),
        out_shape=jax.ShapeDtypeStruct(shape, jnp.float32),
        compiler_params=pltpu.CompilerParams(vmem_limit_bytes=VMEM_LIMIT),
        name="widen",
    )(mine[None], *pieces)


def local(spectra, pair_blocks, owners):
    groups = lax.axis_size("grp")
    parts = lax.axis_size("chan")
    place = lax.axis_index("chan")
    chunks = F // LANES // parts

    def swap(array, d):
        return lax.ppermute(array, "chan", [(i, i ^ d) for i in range(parts)])

    def exchange(panels):
        moved = {d: swap(panels[d], d) for d in sequence(parts)[:-1]}
        return panels[:1] + [moved[d] for d in range(1, parts)]

    first, second = whiten(spectra, pair_blocks[0, 0].T, place, parts)
    first = exchange(first)
    table = tables(place, chunks)
    gates = [d for d in sequence(parts)[:2] if d]
    here, second = lax.optimization_barrier(([first[d] for d in gates], second))
    for d, panel in zip(gates, here):
        first[d] = panel
    second = exchange(second)

    order = list(reversed(range(parts)))
    halves = (order[:1], order[1:])
    sums = [correlate(first, table, place, parts, wanted, 0, None) for wanted in halves]
    ordered, sums = lax.optimization_barrier(([second[d] for d in sequence(parts)], sums))
    for d, panel in zip(sequence(parts), ordered):
        second[d] = panel
    partials = []
    for wanted, before in zip(halves, sums):
        for d, rows in zip(wanted, correlate(second, table, place, parts, wanted, 1, before)):
            partials.append(swap(rows, d) if d else rows)
    mine = lax.axis_index("grp")

    def trade(array, m):
        return lax.ppermute(array, "grp", [(i, i ^ m) for i in range(groups)])

    kept, cross = settle(owners[0, 0].T, partials, mine, groups)
    pieces = bundle(kept, trade(cross, 1))
    for j in reversed(range(1, groups // 2)):
        pieces[j] = trade(pieces[j], 2 * j)
    return widen(pieces, mine)[None, None]


def solution(mesh):
    return jax.shard_map(
        local,
        mesh=mesh,
        in_specs=(
            P(("grp", "chan"), None, None, None),
            P("grp", "chan", None, None),
            P("grp", "chan", None, None),
        ),
        out_specs=P("grp", "chan", None, None, None),
        check_vma=False,
    )
```

```python
import functools

import jax
import jax.numpy as jnp
import numpy as np
from jax import lax
from jax.experimental import pallas as pl
from jax.experimental.pallas import tpu as pltpu
from jax.sharding import PartitionSpec as P

F = 8192
LAGS = 1024
BLK = 2
NB_SRC = 18
MOST = 3
WINDOWS = 2
LANES = 128
PAIRS = BLK * BLK
VMEM_LIMIT = 24 * 1024 * 1024
HALF = LAGS // 2
ROOM = 4
WAVES = 2
LATE = 2


def whiten_kernel(parts, place_ref, spec_ref, pairs_ref, *out_refs):
    blocks = F // LANES
    each = blocks // parts
    late = each // LATE
    place = place_ref[0]

    def values(start):
        span = pl.ds(start, LANES)
        re = spec_ref[0, :, span].astype(jnp.float32)
        im = spec_ref[1, :, span].astype(jnp.float32)
        return re, im, re * re + im * im

    shape = (spec_ref.shape[1], LANES)
    line = lax.broadcasted_iota(jnp.int32, shape, 0)
    spare = jnp.zeros((1, LANES - NB_SRC), jnp.int32)
    wide = lambda row: jnp.broadcast_to(jnp.concatenate([row, spare], axis=1), shape)
    notes = jnp.where(line == 0, wide(pairs_ref[0:1]), wide(pairs_ref[1:2]))
    notes = notes.astype(jnp.float32).astype(jnp.bfloat16)
    for out_ref in out_refs[:parts]:
        out_ref[:, (each - late) * 2 * LANES :] = notes
    sums = [None] * 4
    for k in range(blocks):
        power = values(k * LANES)[2]
        sums[k % 4] = power if k < 4 else sums[k % 4] + power
    total = jnp.sum((sums[0] + sums[1]) + (sums[2] + sums[3]), axis=1, keepdims=True)
    level = 0.1 * (total * (1.0 / F) + 1e-05)
    for index, out_ref in enumerate(out_refs):
        wave, d = divmod(index, parts)
        first = jnp.bitwise_xor(place, d) * each + wave * (each - late)
        for k in range(late if wave else each - late):
            re, im, power = values(pl.multiple_of((first + k) * LANES, LANES))
            scale = lax.rsqrt(power + level)
            at = k * 2 * LANES
            out_ref[:, at : at + LANES] = (re * scale).astype(jnp.bfloat16)
            out_ref[:, at + LANES : at + 2 * LANES] = (im * scale).astype(jnp.bfloat16)


def whiten(spectra, pairs, place, parts):
    rows = spectra.shape[0] * WINDOWS
    planes = jnp.transpose(spectra.reshape(rows, 2, F), (1, 0, 2))
    width = 2 * F // parts
    late = width // LATE
    shapes = [(rows, width - late + LANES)] * parts + [(rows, late)] * parts
    whole = lambda array: pl.BlockSpec(array.shape, lambda i, place: (0,) * array.ndim)
    outs = pl.pallas_call(
        functools.partial(whiten_kernel, parts),
        grid_spec=pltpu.PrefetchScalarGridSpec(
            num_scalar_prefetch=1,
            grid=(1,),
            in_specs=[whole(array) for array in [planes, pairs]],
            out_specs=[pl.BlockSpec(shape, lambda i, place: (0, 0)) for shape in shapes],
        ),
        out_shape=[jax.ShapeDtypeStruct(shape, jnp.bfloat16) for shape in shapes],
        compiler_params=pltpu.CompilerParams(vmem_limit_bytes=VMEM_LIMIT),
        name="whiten",
    )(place[None], planes, pairs)
    return list(outs[:parts]), list(outs[parts:])


def table_kernel(first_ref, hi_cos_ref, hi_sin_ref, mid_cos_ref, mid_sin_ref, lo_cos_ref, lo_sin_ref, out_ref, cos, sin):
    s = pl.program_id(0)
    few = lo_cos_ref.shape[0]

    @pl.when(s == 0)
    def combine():
        lo_cos = lo_cos_ref[...]
        lo_sin = lo_sin_ref[...]
        for i in range(LANES // few):
            mid_cos = mid_cos_ref[i : i + 1]
            mid_sin = mid_sin_ref[i : i + 1]
            cos[i * few : (i + 1) * few] = mid_cos * lo_cos - mid_sin * lo_sin
            sin[i * few : (i + 1) * few] = mid_sin * lo_cos + mid_cos * lo_sin

    hi_cos = hi_cos_ref[pl.ds(s, 1), :]
    hi_sin = hi_sin_ref[pl.ds(s, 1), :]
    minus_cos = -hi_cos
    for i in range(0, LANES, 16):
        lo_cos = cos[i : i + 16]
        lo_sin = sin[i : i + 16]
        out_ref[i : i + 16, :HALF] = (hi_cos * lo_cos - hi_sin * lo_sin).astype(jnp.bfloat16)
        out_ref[i : i + 16, HALF:] = (minus_cos * lo_sin - hi_sin * lo_cos).astype(jnp.bfloat16)

    @pl.when(jnp.logical_and(first_ref[0] == 0, s == 0))
    def zero_bin():
        row = lax.broadcasted_iota(jnp.int32, (16, HALF), 0)
        weight = jnp.where(row == 0, 0.5, 1.0)
        out_ref[0:16, :HALF] = ((hi_cos * cos[0:16] - hi_sin * sin[0:16]) * weight).astype(jnp.bfloat16)


def tables(place, chunks):
    lag = jnp.arange(HALF, dtype=jnp.int32)
    few = 8
    middle = LANES // few
    bins = jnp.concatenate([
        (place * chunks + jnp.arange(chunks, dtype=jnp.int32)) * LANES,
        jnp.arange(middle, dtype=jnp.int32) * few,
        jnp.arange(few, dtype=jnp.int32),
    ])
    phase = bins[:, None] * lag[None, :] % (2 * F)
    angle = phase.astype(jnp.float32) * (jnp.pi / F)
    cos = jnp.cos(angle)
    sin = jnp.sin(angle)
    unit = 2.0 / jnp.sqrt(jnp.float32(F))
    cuts = [slice(0, chunks), slice(chunks, chunks + middle), slice(chunks + middle, None)]
    operands = [cos[cuts[0]] * unit, sin[cuts[0]] * unit, cos[cuts[1]], sin[cuts[1]], cos[cuts[2]], sin[cuts[2]]]
    return pl.pallas_call(
        table_kernel,
        grid_spec=pltpu.PrefetchScalarGridSpec(
            num_scalar_prefetch=1,
            grid=(chunks,),
            in_specs=[pl.BlockSpec(array.shape, lambda s, first: (0, 0)) for array in operands],
            out_specs=pl.BlockSpec((LANES, LAGS), lambda s, first: (s, 0)),
            scratch_shapes=[pltpu.VMEM((LANES, HALF), jnp.float32)] * 2,
        ),
        out_shape=jax.ShapeDtypeStruct((chunks * LANES, LAGS), jnp.bfloat16),
        cost_estimate=pl.CostEstimate(
            flops=chunks * LANES * LAGS * 4, bytes_accessed=chunks * LANES * LAGS * 2, transcendentals=0
        ),
        compiler_params=pltpu.CompilerParams(vmem_limit_bytes=VMEM_LIMIT),
        name="tables",
    )(place[None], *operands)


def iota(shape, axis):
    return lax.broadcasted_iota(jnp.int32, shape, axis)


def ones(hit):
    return hit.astype(jnp.float32).astype(jnp.bfloat16)


def choose_rows(lists, place, packed, rows_ref):
    height = rows_ref.shape[1]
    count = rows_ref.shape[0] // (2 * BLK * WINDOWS)
    deep = packed.shape[0] // lists
    blocks = deep // (BLK * WINDOWS)
    line = iota((count, 1), 0)
    group = jnp.zeros_like(line)
    for z in range(1, lists):
        group = group + jnp.where(line >= z * NB_SRC, 1, 0)
    here = iota((count, LANES), 1) == line - group * NB_SRC

    def column(kind):
        row = ones(iota((count, packed.shape[0]), 1) == group * deep + kind)
        found = jnp.dot(row, packed, preferred_element_type=jnp.float32)
        return jnp.sum(jnp.where(here, found, 0.0), axis=1, keepdims=True).astype(jnp.int32)

    across = iota((count, height), 1)
    picks = []
    for block in (column(0), column(1)):
        first = jnp.bitwise_xor(block, place * blocks) * (BLK * WINDOWS)
        for offset in range(BLK * WINDOWS):
            picks.append((across == first + offset).astype(jnp.float32))
    rows_ref[...] = jnp.concatenate(picks, axis=0).astype(jnp.bfloat16)


def sequence(parts):
    order = list(reversed(range(parts)))
    return [order[0], order[-2], *order[1:-2], order[-1]]


def corr_kernel(per_step, parts, lists, wave, place, *refs):
    panel_refs, (table_ref, ends_ref), refs = dict(zip(sequence(parts), refs)), refs[parts : parts + 2], refs[parts + 2 :]
    step = pl.program_id(0)
    if wave:
        (total_in, edge_in, rows_ref), out_refs, (total, edge) = refs[:3], refs[3:-2], refs[-2:]
    else:
        note_refs, (total, edge, rows_ref) = refs[:lists], refs[lists:]

        @pl.when(step == 0)
        def prepare():
            choose_rows(lists, place[0], jnp.concatenate([ref[...] for ref in note_refs]), rows_ref)

    count = total.shape[0] // PAIRS
    panel = jnp.concatenate([panel_refs[d][...] for d in range(parts)])
    chosen = jnp.dot(rows_ref[...], panel, preferred_element_type=jnp.float32)

    def row(side, channel, window, start):
        first = ((side * BLK + channel) * WINDOWS + window) * count
        return chosen[first : first + count, start : start + LANES]

    reals = []
    imags = []
    lane = iota((1, LANES), 1)
    first_bin = jnp.logical_and(jnp.logical_and(place[0] == 0, step == 0), lane == 0)
    edge_part = 0.0
    for i in range(per_step):
        at = i * 2 * LANES
        real = []
        imag = []
        for p in range(BLK):
            for q in range(BLK):
                re = 0.0
                im = 0.0
                for w in range(WINDOWS):
                    ra, ia = row(0, p, w, at), row(0, p, w, at + LANES)
                    rb, ib = row(1, q, w, at), row(1, q, w, at + LANES)
                    re = re + (ra * rb + ia * ib)
                    im = im + (ia * rb - ra * ib)
                real.append(re * (1.0 / WINDOWS))
                imag.append(im * (1.0 / WINDOWS))
        real = jnp.concatenate(real, axis=0)
        imag = jnp.concatenate(imag, axis=0)
        ends = ends_ref[0:1]
        if i == 0 and wave == 0:
            ends = jnp.where(first_bin, 0.5 * ends, ends)
        edge_part = edge_part + (real * ends + imag * ends_ref[1:2])
        reals.append(real.astype(jnp.bfloat16))
        imags.append(imag.astype(jnp.bfloat16))

    def transform(pieces, columns):
        rows = jnp.concatenate(pieces, axis=1)
        return jnp.dot(rows, table_ref[:, columns], preferred_element_type=jnp.float32)

    even = transform(reals, slice(0, HALF))
    odd = transform(imags, slice(HALF, LAGS))

    @pl.when(step == 0)
    def start():
        total[:, :HALF] = total_in[:, :HALF] + even if wave else even
        total[:, HALF:] = total_in[:, HALF:] + odd if wave else odd
        edge[...] = edge_in[...] + edge_part if wave else edge_part

    @pl.when(step > 0)
    def add():
        total[:, :HALF] += even
        total[:, HALF:] += odd
        edge[...] += edge_part

    if wave < WAVES - 1:
        return

    @pl.when(step == pl.num_programs(0) - 1)
    def finish():
        even = total[:, :HALF]
        odd = total[:, HALF:]
        later = (even + odd).astype(jnp.bfloat16)
        mirror = ones(iota((HALF, HALF), 0) + iota((HALF, HALF), 1) == HALF)
        sooner = jnp.dot((even - odd).astype(jnp.bfloat16), mirror, preferred_element_type=jnp.float32)
        least = jnp.sum(edge[...], axis=1, keepdims=True)
        sooner = jnp.where(iota(sooner.shape, 1) == 0, least, sooner).astype(jnp.bfloat16)
        each = NB_SRC * PAIRS
        shape = (each * len(out_refs), PAIRS * count)
        column = iota(shape, 1)
        number = column * PAIRS
        for n in range(1, PAIRS):
            number = number - jnp.where(column >= n * count, count * PAIRS - 1, 0)
        order = ones(iota(shape, 0) == number)
        both = jnp.concatenate([sooner, later], axis=1)
        rows = jnp.dot(order, both, preferred_element_type=jnp.float32)
        for i, out_ref in enumerate(out_refs):
            out_ref[...] = rows[i * each : (i + 1) * each].astype(jnp.bfloat16)


def correlate(panels, table, place, parts, wanted, wave, before):
    chunks = table.shape[0] // LANES
    per_step = min(8, chunks // LATE)
    span = per_step * 2 * LANES
    rows = panels[0].shape[0]
    late = chunks // LATE // per_step
    early = chunks // per_step - late
    steps = late if wave else early
    lists = len(wanted)
    count = -(-lists * NB_SRC // 8) * 8
    each = NB_SRC * PAIRS
    turn = np.arange(LANES) * (np.pi / 16)
    ends = np.stack([np.cos(turn), np.sin(turn)]) * (2.0 / np.sqrt(F))
    sums = [
        jax.ShapeDtypeStruct((count * PAIRS, LAGS), jnp.float32),
        jax.ShapeDtypeStruct((count * PAIRS, LANES), jnp.float32),
    ]
    chosen = jax.ShapeDtypeStruct((2 * BLK * WINDOWS * count, rows * parts), jnp.bfloat16)
    whole = lambda array: pl.BlockSpec(array.shape, lambda i, place: (0, 0))
    if wave:
        extra = before
        extra_specs = [whole(array) for array in before]
        outs = [jax.ShapeDtypeStruct((each, LAGS), jnp.bfloat16)] * lists
        scratch = [pltpu.VMEM(array.shape, array.dtype) for array in sums]
    else:
        extra = [panels[d] for d in wanted]
        extra_specs = [pl.BlockSpec((rows, LANES), lambda i, place: (0, steps * span // LANES))] * lists
        outs = [*sums, chosen]
        scratch = []
    return pl.pallas_call(
        functools.partial(corr_kernel, per_step, parts, lists, wave),
        grid_spec=pltpu.PrefetchScalarGridSpec(
            num_scalar_prefetch=1,
            grid=(steps,),
            in_specs=[
                *[pl.BlockSpec((rows, span), lambda i, place: (0, i))] * parts,
                pl.BlockSpec((span // 2, LAGS), lambda i, place: (i + wave * early, 0)),
                pl.BlockSpec((2, LANES), lambda i, place: (0, 0)),
                *extra_specs,
            ],
            out_specs=[whole(array) for array in outs],
            scratch_shapes=scratch,
        ),
        out_shape=outs,
        compiler_params=pltpu.CompilerParams(vmem_limit_bytes=VMEM_LIMIT),
        cost_estimate=pl.CostEstimate(
            flops=count * PAIRS * steps * span * LAGS,
            bytes_accessed=steps * span * LAGS,
            transcendentals=0,
        ),
        name="correlate",
    )(place[None], *[panels[d] for d in sequence(parts)], table, jnp.asarray(ends, jnp.float32), *extra)


def settle_kernel(groups, mine_ref, owners_ref, *refs):
    part_refs, out_refs = refs[:-2], refs[-2:]
    rows = groups * ROOM * PAIRS
    slots = rows // PAIRS
    each = NB_SRC * PAIRS
    tall = 24
    spare = jnp.full((1, LANES - NB_SRC), rows, jnp.int32)
    owner = jnp.concatenate([owners_ref[...], spare], axis=1)
    wide = jnp.broadcast_to(owner, (tall, LANES)).astype(jnp.float32)
    line, lane = iota((tall, LANES), 0), iota((tall, LANES), 1)
    other = jnp.sum(jnp.where(line == lane, wide, 0.0), axis=1, keepdims=True)
    earlier = jnp.logical_and(other == wide, line < lane).astype(jnp.float32)
    rank = jnp.sum(earlier, axis=0, keepdims=True)
    turn = jnp.bitwise_xor(owner, mine_ref[0])
    block = lax.shift_right_logical(turn, 1) + jnp.bitwise_and(turn, 1) * (groups // 2)
    slot = jnp.where(owner < groups, block, rows).astype(jnp.float32) * ROOM + rank
    held = ones(iota((slots, LANES), 0).astype(jnp.float32) == slot)
    down = ones(lax.shift_right_logical(iota((rows, slots), 0), 2) == iota((rows, slots), 1))
    over = ones(lax.shift_right_logical(iota((LANES, each), 1), 2) == iota((LANES, each), 0))
    block = jnp.dot(down, held, preferred_element_type=jnp.float32).astype(jnp.bfloat16)
    block = jnp.dot(block, over, preferred_element_type=jnp.float32)
    same = jnp.bitwise_and(iota((rows, each), 0), PAIRS - 1) == jnp.bitwise_and(iota((rows, each), 1), PAIRS - 1)
    chosen = jnp.where(same, block, 0.0).astype(jnp.bfloat16)
    total = sum(ref[...].astype(jnp.float32) for ref in part_refs)
    placed = jnp.dot(chosen, total.astype(jnp.bfloat16), preferred_element_type=jnp.float32)
    for i, out_ref in enumerate(out_refs):
        out_ref[...] = placed[i * rows // 2 : (i + 1) * rows // 2].astype(jnp.bfloat16)


def settle(owners, partials, mine, groups):
    whole = lambda array: pl.BlockSpec(array.shape, lambda i, mine: (0, 0))
    outs = [jax.ShapeDtypeStruct((groups * ROOM * PAIRS // 2, LAGS), jnp.bfloat16)] * 2
    return list(pl.pallas_call(
        functools.partial(settle_kernel, groups),
        grid_spec=pltpu.PrefetchScalarGridSpec(
            num_scalar_prefetch=1,
            grid=(1,),
            in_specs=[whole(array) for array in [owners, *partials]],
            out_specs=[whole(array) for array in outs],
        ),
        out_shape=outs,
        compiler_params=pltpu.CompilerParams(vmem_limit_bytes=VMEM_LIMIT),
        name="settle",
    )(mine[None], owners, *partials))


def bundle_kernel(kept_ref, brought_ref, *out_refs):
    deep = ROOM * PAIRS
    for j, out_ref in enumerate(out_refs):
        out_ref[:deep] = kept_ref[j * deep : (j + 1) * deep]
        out_ref[deep:] = brought_ref[j * deep : (j + 1) * deep]


def bundle(kept, brought):
    count = kept.shape[0] // (ROOM * PAIRS)
    return list(pl.pallas_call(
        bundle_kernel,
        out_shape=[jax.ShapeDtypeStruct((2 * ROOM * PAIRS, LAGS), jnp.bfloat16)] * count,
        compiler_params=pltpu.CompilerParams(vmem_limit_bytes=VMEM_LIMIT),
        name="bundle",
    )(kept, brought))


def widen_kernel(mine_ref, *refs):
    part_refs, out_ref = refs[:-1], refs[-1]
    for j, part_ref in enumerate(part_refs):
        values = part_ref[...].astype(jnp.float32)
        for side in range(2):
            first = jnp.bitwise_xor(mine_ref[0], 2 * j + side) * MOST
            for r in range(MOST):
                at = (side * ROOM + r) * PAIRS
                out_ref[first + r] = values[at : at + PAIRS]


def widen(pieces, mine):
    shape = (2 * len(pieces) * MOST, PAIRS, LAGS)
    return pl.pallas_call(
        widen_kernel,
        grid_spec=pltpu.PrefetchScalarGridSpec(
            num_scalar_prefetch=1,
            grid=(1,),
            in_specs=[pl.BlockSpec(array.shape, lambda i, mine: (0, 0)) for array in pieces],
            out_specs=pl.BlockSpec(shape, lambda i, mine: (0, 0, 0)),
        ),
        out_shape=jax.ShapeDtypeStruct(shape, jnp.float32),
        compiler_params=pltpu.CompilerParams(vmem_limit_bytes=VMEM_LIMIT),
        name="widen",
    )(mine[None], *pieces)


def local(spectra, pair_blocks, owners):
    groups = lax.axis_size("grp")
    parts = lax.axis_size("chan")
    place = lax.axis_index("chan")
    chunks = F // LANES // parts

    def swap(array, d):
        return lax.ppermute(array, "chan", [(i, i ^ d) for i in range(parts)])

    def exchange(panels):
        moved = {d: swap(panels[d], d) for d in sequence(parts)[:-1]}
        return panels[:1] + [moved[d] for d in range(1, parts)]

    first, second = whiten(spectra, pair_blocks[0, 0].T, place, parts)
    first = exchange(first)
    table = tables(place, chunks)
    gates = sequence(parts)[:1]
    here, second = lax.optimization_barrier(([first[d] for d in gates], second))
    for d, panel in zip(gates, here):
        first[d] = panel
    second = exchange(second)

    order = list(reversed(range(parts)))
    halves = (order[:1], order[1:])
    sums = [correlate(first, table, place, parts, wanted, 0, None) for wanted in halves]
    ordered, sums = lax.optimization_barrier(([second[d] for d in sequence(parts)], sums))
    for d, panel in zip(sequence(parts), ordered):
        second[d] = panel
    partials = []
    for wanted, before in zip(halves, sums):
        for d, rows in zip(wanted, correlate(second, table, place, parts, wanted, 1, before)):
            partials.append(swap(rows, d) if d else rows)
    mine = lax.axis_index("grp")

    def trade(array, m):
        return lax.ppermute(array, "grp", [(i, i ^ m) for i in range(groups)])

    kept, cross = settle(owners[0, 0].T, partials, mine, groups)
    pieces = bundle(kept, trade(cross, 1))
    for j in reversed(range(1, groups // 2)):
        pieces[j] = trade(pieces[j], 2 * j)
    return widen(pieces, mine)[None, None]


def solution(mesh):
    return jax.shard_map(
        local,
        mesh=mesh,
        in_specs=(
            P(("grp", "chan"), None, None, None),
            P("grp", "chan", None, None),
            P("grp", "chan", None, None),
        ),
        out_specs=P("grp", "chan", None, None, None),
        check_vma=False,
    )
```
